128 devices in a mesh: emit: 2 (over x_hi), slab: 64 (over z, y, x_lo, core).
Axes of the slice: x: 4 (x_hi: 2, x_lo: 2; x = x_hi * 2 + x_lo), y: 4, z: 4, core: 2. Of those that a mesh axis runs over, the one named last changes fastest.
Arguments:
- sound_speed: float32 [256, 256, 256], P('slab'), may hold values from 0.7 to 1.4
- density: float32 [256, 256, 256], P('slab'), may hold values from 0.8 to 1.8
- absorption: float32 [256, 256, 256], P('slab'), may hold values from 0.05 to 1
- pressure_start: float32 [2, 256, 256, 256], P('emit', 'slab'), may hold values from -6 to 6
- velocity_start: float32 [2, 3, 256, 256, 256], P('emit', None, 'slab'), may hold values from -3 to 3
- adjoint_pressure: float32 [2, 256, 256, 256], P('emit', 'slab'), may hold values from -6 to 6
- adjoint_velocity: float32 [2, 3, 256, 256, 256], P('emit', None, 'slab'), may hold values from -6 to 6
- emitter_voxel: int32 [2, 256], P('emit'), may hold values from 0 to 16777215
- emitter_delay: int32 [2, 256], P('emit'), may hold values from 0 to 62
- drive_waveform_samples: float32 [64], replicated, may hold values from -8 to 8
- recorded_pressures: float32 [2, 2, 1024], P('emit'), may hold values from -6 to 6
- sensor_flat_position: int32 [1024], replicated, may hold values from 0 to 16777215
Outputs:
- grad_speed: float32 [256, 256, 256], P('slab')
- grad_density: float32 [256, 256, 256], P('slab')
The draws below stay inside these ranges and needn't reach their ends.
Inputs may be any that keep to these rules, and one draw needn't show every extreme that they name: `emitter_voxel`: flat index x * 256 * 256 + y * 256 + z of a voxel. `sensor_flat_position`: flat index x * 256 * 256 + y * 256 + z of a voxel.
All inputs are finite; a program needn't handle non-finite values.
Results may differ from the reference program's by a relative error of at most 0.0001.
Values sent between devices are 32-bit elements; how exact they have to be, the bound alone decides.
No kernel may reach another device: no remote copies, remote signals or barrier semaphores. Data moves between devices by JAX's collectives and lax.ppermute only.
A program may use at most 128 MiB of HBM per device.

```python
import math
import jax
import jax.numpy as jnp
from jax import lax

NX = 256
NY = 256
NZ = 256
STEPS = 2
EMITTERS = 256
RECEIVERS = 1024
SAMPLES = 64
SOURCE_BATCHES = 2


two_pi = 2.0 * math.pi


def oscillation_trace_table(key, bounding_span, radiated_intensity):
    subkeys = jax.random.split(key, 5)
    single_shape = bounding_span + (1, 1, 1)
    second = jax.random.randint(subkeys[0], single_shape, 2, 6)
    phase_a = jax.random.uniform(subkeys[1], single_shape, jnp.float32, 0.0, two_pi)
    phase_b = jax.random.uniform(subkeys[2], single_shape, jnp.float32, 0.0, two_pi)
    tilt_y = jax.random.uniform(subkeys[3], single_shape, jnp.float32, 0.0, two_pi)
    tilt_z = jax.random.uniform(subkeys[4], single_shape, jnp.float32, 0.0, two_pi)
    x_cells = jnp.arange(NX, dtype=jnp.int32).reshape(NX, 1, 1)
    y_cells = jnp.arange(NY, dtype=jnp.float32).reshape(1, NY, 1)
    z_cells = jnp.arange(NZ, dtype=jnp.float32).reshape(1, 1, NZ)
    top_mode = (NX // 2 - 1) * x_cells % NX
    next_mode = (NX // 2 - second) * x_cells % NX
    first_phase_shift = top_mode.astype(jnp.float32) * (two_pi / NX) + phase_a
    second_phase_shift = next_mode.astype(jnp.float32) * (two_pi / NX) + phase_b
    taper_profile = 0.75 + 0.25 * jnp.cos(y_cells * (two_pi / NY) + tilt_y) * jnp.cos(z_cells * (two_pi / NZ) + tilt_z)
    return radiated_intensity * taper_profile * (0.65 * jnp.cos(first_phase_shift) + 0.35 * jnp.cos(second_phase_shift))


def draw_pressure_start(key, part):
    key = jax.random.fold_in(key, 11)
    tone_prng_seed, delay_prng_seed = jax.random.split(key)
    sinusoid_signal = oscillation_trace_table(tone_prng_seed, (SOURCE_BATCHES,), 3.0)
    onset_perturbation = jnp.clip(jax.random.normal(delay_prng_seed, sinusoid_signal.shape, jnp.float32), -3.0, 3.0)
    return sinusoid_signal + onset_perturbation


def draw_velocity_start(key, part):
    key = jax.random.fold_in(key, 23)
    tone_prng_seed, delay_prng_seed = jax.random.split(key)
    sinusoid_signal = oscillation_trace_table(tone_prng_seed, (SOURCE_BATCHES, 3), 1.5)
    onset_perturbation = jnp.clip(0.5 * jax.random.normal(delay_prng_seed, sinusoid_signal.shape, jnp.float32), -1.5, 1.5)
    return sinusoid_signal + onset_perturbation


def draw_adjoint_pressure(key, part):
    key = jax.random.fold_in(key, 37)
    tone_prng_seed, delay_prng_seed = jax.random.split(key)
    sinusoid_signal = oscillation_trace_table(tone_prng_seed, (SOURCE_BATCHES,), 3.0)
    onset_perturbation = jnp.clip(jax.random.normal(delay_prng_seed, sinusoid_signal.shape, jnp.float32), -3.0, 3.0)
    return sinusoid_signal + onset_perturbation


def draw_adjoint_velocity(key, part):
    key = jax.random.fold_in(key, 41)
    tone_prng_seed, delay_prng_seed = jax.random.split(key)
    sinusoid_signal = oscillation_trace_table(tone_prng_seed, (SOURCE_BATCHES, 3), 3.0)
    onset_perturbation = jnp.clip(jax.random.normal(delay_prng_seed, sinusoid_signal.shape, jnp.float32), -3.0, 3.0)
    return sinusoid_signal + onset_perturbation


def touch_ends(array, key, least, top_value):
    extent = array.shape
    index_at = [jax.random.randint(jax.random.fold_in(key, axis), (), 0, extent[axis]) for axis in range(len(extent))]
    array = array.at[tuple(index_at)].set(least)
    longest = extent.index(max(extent))
    index_at[longest] = (index_at[longest] + 1) % extent[longest]
    return array.at[tuple(index_at)].set(top_value)


def block_levels(own_key, extent, cuts, least, high):
    loudness = 1.0
    for position, blocks in cuts:
        draws = jax.random.uniform(jax.random.fold_in(jax.random.fold_in(own_key, 6), position), (blocks,), jnp.float32, least / len(cuts), high / len(cuts))
        loudness = loudness * jnp.repeat(jnp.exp(draws), extent[position] // blocks).reshape((-1,) + (1,) * (len(extent) - 1 - position))
    return loudness


def scatter_about(stream_key, shape, spread, reach, cuts=(), kind=jnp.bfloat16):
    gain = block_levels(stream_key, shape, cuts, -0.22, 0.18) if cuts else 1.0
    result = jax.random.normal(stream_key, shape, jnp.float32) * spread * gain
    return jnp.minimum(jnp.maximum(result, -reach), reach).astype(kind)


def setup_inputs(seed: int = 0) -> dict:
    splits = jax.random.split(jax.random.key(seed), 13)
    return {
        "sound_speed": jnp.clip(0.7 + 0.7 * jax.random.uniform(splits[0], (NX, NY, NZ), jnp.float32) ** block_levels(splits[0], (NX, NY, NZ), ((0, 64),), -0.2, 0.2), 0.7, 1.4),
        "density": jnp.clip(jnp.exp(math.log(1.8) - 0.8109302 * jax.random.uniform(splits[1], (NX, NY, NZ), jnp.float32) ** block_levels(splits[1], (NX, NY, NZ), ((0, 64),), -0.2, 0.2)), 0.8, 1.8),
        "absorption": jnp.clip(jnp.exp(math.log(1.0) - 2.9957323 * jax.random.uniform(splits[2], (NX, NY, NZ), jnp.float32) ** block_levels(splits[2], (NX, NY, NZ), ((0, 64),), -0.2, 0.2)), 0.05, 1.0),
        "pressure_start": draw_pressure_start(jax.random.fold_in(splits[12], 71), 0),
        "velocity_start": draw_velocity_start(jax.random.fold_in(splits[12], 71), 0),
        "adjoint_pressure": draw_adjoint_pressure(jax.random.fold_in(splits[12], 71), 0),
        "adjoint_velocity": draw_adjoint_velocity(jax.random.fold_in(splits[12], 71), 0),
        "emitter_voxel": touch_ends(jax.random.randint(splits[7], (SOURCE_BATCHES, EMITTERS), 0, NX * NY * NZ), jax.random.fold_in(splits[7], 1), 0, (NX * NY * NZ) - 1).astype(jnp.int32),
        "emitter_delay": touch_ends(jax.random.randint(splits[8], (SOURCE_BATCHES, EMITTERS), 0, SAMPLES - STEPS + 1), jax.random.fold_in(splits[8], 1), 0, SAMPLES - STEPS).astype(jnp.int32),
        "drive_waveform_samples": scatter_about(splits[9], (SAMPLES,), 2.0, 8.0, (), jnp.float32),
        "recorded_pressures": scatter_about(splits[10], (SOURCE_BATCHES, STEPS, RECEIVERS), 1.0, 6.0, ((0, 2),), jnp.float32),
        "sensor_flat_position": touch_ends(jax.random.randint(splits[11], (RECEIVERS,), 0, NX * NY * NZ), jax.random.fold_in(splits[11], 1), 0, (NX * NY * NZ) - 1).astype(jnp.int32),
    }


time_step = 0.2


def deriv_matrix(length):
    halfway = length // 2
    modes = jnp.arange(1, halfway, dtype=jnp.int32)
    points = jnp.arange(length, dtype=jnp.int32)
    shifted = (modes[None, :] * (2 * points[:, None] + 1)) % (2 * length)
    unshifted = (modes[None, :] * (2 * points[:, None])) % (2 * length)
    factor = math.pi / length
    wavenumber = modes.astype(jnp.float32) * (2.0 * factor)
    shift_angle = shifted.astype(jnp.float32) * factor
    plain_angle = unshifted.astype(jnp.float32) * factor
    cosine_part = jnp.cos(shift_angle) * wavenumber[None, :]
    sine_part = jnp.sin(shift_angle) * wavenumber[None, :]
    matrix = jnp.dot(cosine_part, jnp.sin(plain_angle).T, precision=lax.Precision.HIGHEST)
    matrix = matrix - jnp.dot(sine_part, jnp.cos(plain_angle).T, precision=lax.Precision.HIGHEST)
    return matrix * (2.0 / length)


def along_first(matrix, volume):
    return jnp.einsum("ij,jbc->ibc", matrix, volume, precision=lax.Precision.HIGHEST)


def along_second(matrix, volume):
    return jnp.einsum("ij,ajc->aic", matrix, volume, precision=lax.Precision.HIGHEST)


def along_third(matrix, volume):
    return jnp.einsum("abj,ij->abi", volume, matrix, precision=lax.Precision.HIGHEST)


def single_cohort(compressibility_modulus, inverse_density, retained_snapshots, pressure_tension, particle_motion, costate_compression, costate_motion, radiator_position, transmit_latency, drive_waveform_samples, recorded_pressures, sensor_flat_position, operator_blocks):
    matrix_x, matrix_y, matrix_z = operator_blocks
    lattice_layout = pressure_tension.shape
    vel_x, vel_y, vel_z = particle_motion[0], particle_motion[1], particle_motion[2]
    saved = []
    residuals = []
    for loop_tally in range(STEPS):
        previous = pressure_tension
        vel_x = vel_x - time_step * inverse_density * along_first(matrix_x, pressure_tension)
        vel_y = vel_y - time_step * inverse_density * along_second(matrix_y, pressure_tension)
        vel_z = vel_z - time_step * inverse_density * along_third(matrix_z, pressure_tension)
        divergence = along_first(matrix_x.T, vel_x) + along_second(matrix_y.T, vel_y) + along_third(matrix_z.T, vel_z)
        pressure_tension = retained_snapshots * pressure_tension + time_step * compressibility_modulus * divergence
        radiated_intensity = drive_waveform_samples[transmit_latency + loop_tally]
        pressure_tension = pressure_tension.reshape(-1).at[radiator_position].add(radiated_intensity).reshape(lattice_layout)
        residuals.append(pressure_tension.reshape(-1)[sensor_flat_position] - recorded_pressures[loop_tally])
        saved.append((previous, divergence))
    grad_bulk = jnp.zeros(lattice_layout, jnp.float32)
    grad_buoy = jnp.zeros(lattice_layout, jnp.float32)
    adj_p = costate_compression
    adj_x, adj_y, adj_z = costate_motion[0], costate_motion[1], costate_motion[2]
    for loop_tally in reversed(range(STEPS)):
        previous, divergence = saved[loop_tally]
        adj_p = adj_p.reshape(-1).at[sensor_flat_position].add(residuals[loop_tally]).reshape(lattice_layout)
        grad_bulk = grad_bulk + time_step * divergence * adj_p
        weight = time_step * compressibility_modulus * adj_p
        adj_x = adj_x + along_first(matrix_x, weight)
        adj_y = adj_y + along_second(matrix_y, weight)
        adj_z = adj_z + along_third(matrix_z, weight)
        products = along_first(matrix_x, previous) * adj_x + along_second(matrix_y, previous) * adj_y + along_third(matrix_z, previous) * adj_z
        grad_buoy = grad_buoy - time_step * products
        back = along_first(matrix_x.T, inverse_density * adj_x) + along_second(matrix_y.T, inverse_density * adj_y) + along_third(matrix_z.T, inverse_density * adj_z)
        adj_p = retained_snapshots * adj_p - time_step * back
    return grad_bulk, grad_buoy


def reference(sound_speed, density, absorption, pressure_start, velocity_start, adjoint_pressure, adjoint_velocity, emitter_voxel, emitter_delay, drive_waveform_samples, recorded_pressures, sensor_flat_position):
    operator_blocks = (deriv_matrix(NX), deriv_matrix(NY), deriv_matrix(NZ))
    compressibility_modulus = density * sound_speed * sound_speed
    inverse_density = 1.0 / density
    retained_snapshots = 1.0 - time_step * absorption
    speed_total = jnp.zeros(sound_speed.shape, jnp.float32)
    density_total = jnp.zeros(sound_speed.shape, jnp.float32)
    for group_index in range(SOURCE_BATCHES):
        grad_bulk, grad_buoy = single_cohort(compressibility_modulus, inverse_density, retained_snapshots, pressure_start[group_index], velocity_start[group_index], adjoint_pressure[group_index], adjoint_velocity[group_index], emitter_voxel[group_index], emitter_delay[group_index], drive_waveform_samples, recorded_pressures[group_index], sensor_flat_position, operator_blocks)
        speed_total = speed_total + grad_bulk * 2.0 * density * sound_speed
        density_total = density_total + (grad_bulk * sound_speed * sound_speed - grad_buoy * inverse_density * inverse_density)
    return speed_total, density_total
```

```python
import numpy as np
import jax
import jax.numpy as jnp
from jax import lax
from jax.experimental import pallas as pl
from jax.experimental.pallas import tpu as pltpu
from jax.sharding import PartitionSpec as P

STEPS = 2
DT = 0.2
F32 = jnp.float32
BF16 = jnp.bfloat16
ALL = ("emit", "slab")
VMEM_LIMIT = 48 * 2**20


def deriv_matrix(n):
    k = np.arange(1, n // 2, dtype=np.int64)
    pts = np.arange(n, dtype=np.int64)
    shifted = (k[None, :] * (2 * pts[:, None] + 1)) % (2 * n) * (np.pi / n)
    plain = (k[None, :] * (2 * pts[:, None])) % (2 * n) * (np.pi / n)
    w = k * (2.0 * np.pi / n)
    m = (np.cos(shifted) * w) @ np.sin(plain).T - (np.sin(shifted) * w) @ np.cos(plain).T
    return m * (2.0 / n)


def pair_const(m):
    m = m.astype(np.float32)
    return [jnp.asarray(m), jnp.asarray(np.ascontiguousarray(m.T))]


def split2(v):
    hi = v.astype(BF16)
    return hi, (v - hi.astype(F32)).astype(BF16)


def split3(v):
    hi = v.astype(BF16)
    rest = v - hi.astype(F32)
    mid = rest.astype(BF16)
    return hi, mid, (rest - mid.astype(F32)).astype(BF16)


def dot(a, b):
    return jnp.dot(a, b, preferred_element_type=F32)


def left(m, v):
    mh, ml = split2(m[...])
    h, l = split2(v)
    return dot(mh, h) + (dot(mh, l) + dot(ml, h))


def right(v, m):
    mh, ml = split2(m[...])
    h, l = split2(v)
    return dot(h, mh) + (dot(l, mh) + dot(h, ml))


def params(n_grid):
    return pltpu.CompilerParams(
        dimension_semantics=("arbitrary",) * n_grid, vmem_limit_bytes=VMEM_LIMIT
    )


def plane_onehot(pos_row, plane, ny, nz):
    local = pos_row - plane * (ny * nz)
    y = lax.broadcasted_iota(jnp.int32, (ny, pos_row.shape[1]), 0)
    return jnp.where((local >= y * nz) & (local < y * nz + nz), 1.0, 0.0).astype(BF16)


def column_onehot(pos_col, nz):
    z = lax.broadcasted_iota(jnp.int32, (pos_col.shape[0], nz), 1)
    return (pos_col & (nz - 1) if nz & (nz - 1) == 0 else lax.rem(pos_col, nz)) == z


def drive_at(delay_col, drive_row, step):
    k = lax.broadcasted_iota(jnp.int32, (delay_col.shape[0], drive_row.shape[1]), 1)
    return jnp.sum(jnp.where(delay_col + step == k, drive_row, 0.0), axis=1, keepdims=True)


def three(onehot, value_col):
    return jnp.concatenate([jnp.where(onehot, v.astype(F32), 0.0).astype(BF16) for v in split3(value_col)], axis=1)


def sum3(v, n):
    return v[:, :n] + v[:, n : 2 * n] + v[:, 2 * n :]


def start_kernel(
    ids, c, rho, alpha, p0, ux, uy, uz, vx, epos_row, epos_col, delay, drive, gm, tm,
    buf, u1y, u1z, yz0, gy0, gz0, v0, mat, rhs,
):
    i = pl.program_id(0)
    ny, nz = p0.shape[1], p0.shape[2]
    half = ny // 2

    @pl.when(i == 0)
    def _():
        rhs[...] = three(column_onehot(epos_col[...], nz), drive_at(delay[...], drive[...], 0))

    @pl.when(i < 4)
    def _():
        dens, speed, p = rho[0], c[0], p0[0]
        b = 1.0 / dens
        bulk = dens * speed * speed
        gy = left(gm, p)
        gz = right(p, tm)
        wy = uy[0] - DT * b * gy
        wz = uz[0] - DT * b * gz
        yz = left(tm, wy) + right(wz, gm)
        shot = sum3(dot(plane_onehot(epos_row[...], ids[1] * 4 + i, ny, nz), rhs[...]), nz)
        v = (1.0 - DT * alpha[0]) * p + (DT * bulk) * yz + shot
        u1y[0], u1z[0], yz0[0], gy0[0], gz0[0], v0[0] = wy, wz, yz, gy, gz, v
        for yl in range(2):
            rows = slice(yl * half, (yl + 1) * half)
            buf[:, 0, yl, :] = p[rows]
            buf[:, 0, 2 + yl, :] = ux[0, rows, :]
            buf[:, 0, 4 + yl, :] = v[rows]
            buf[:, 0, 6 + yl, :] = vx[0, rows, :]
        for xm in range(2):

            @pl.when(i == 2 * ids[0] + xm)
            def _():
                for yl in range(2):
                    rows = slice(yl * half, (yl + 1) * half)
                    mat[:, 4 * xm + yl, :] = b[rows]
                    mat[:, 4 * xm + 2 + yl, :] = bulk[rows]

    @pl.when(i == 4)
    def _():
        buf[:, 0] = mat[...]


def whole(shape):
    return pl.BlockSpec(shape, lambda i: (0,) * len(shape))


def smem():
    return pl.BlockSpec(memory_space=pltpu.SMEM)


def group_plane(shape, pick):
    block = (None,) * (len(shape) - 3) + (1,) + shape[-2:]
    return lambda a: pl.BlockSpec(block, lambda i: (0, a)[: len(shape) - 3] + (pick(i), 0, 0))


def start_call(ids, c, rho, alpha, p0, u, v, epos, delay, drive, mats, ndev):
    nx, ny, nz = c.shape
    pick = lambda i: jnp.minimum(i, 3)
    plane = pl.BlockSpec((1, ny, nz), lambda i: (pick(i), 0, 0))
    vec = group_plane(u.shape, pick)
    n_e = epos.shape[0]
    nat = jax.ShapeDtypeStruct(c.shape, F32)
    return pl.pallas_call(
        start_kernel,
        grid=(5,),
        in_specs=[smem()] + [plane] * 3
        + [group_plane(p0.shape, pick)(0), vec(0), vec(1), vec(2), vec(0)]
        + [whole((1, n_e)), whole((n_e, 1)), whole((n_e, 1)), whole((1, drive.shape[0]))]
        + [whole((ny, ny))] * 2,
        out_specs=[pl.BlockSpec((ndev, 1, 8, nz), lambda i: (0, i, 0, 0))] + [plane] * 6,
        out_shape=[jax.ShapeDtypeStruct((ndev, 5, 8, nz), F32)] + [nat] * 6,
        scratch_shapes=[pltpu.VMEM((ndev, 8, nz), F32), pltpu.VMEM((n_e, 3 * nz), BF16)],
        compiler_params=params(1),
        cost_estimate=pl.CostEstimate(flops=2 * 10**9, bytes_accessed=19 * 2**20, transcendentals=0),
        name="start",
    )(
        ids, c, rho, alpha, p0, u, u, u, v, epos.reshape(1, -1), epos.reshape(-1, 1),
        delay.reshape(-1, 1), drive.reshape(1, -1), *mats,
    )


def maps_kernel(
    ids, spos_row, spos_col, rec, epos_row, epos_col, delay, drive, cnt, d0, d1, e1, srhs, erhs
):
    i = pl.program_id(0)
    ny, nz = cnt.shape[1], cnt.shape[2]

    @pl.when(i == 0)
    def _():
        oh = column_onehot(spos_col[...], nz)
        srhs[:, :nz] = jnp.where(oh, 1.0, 0.0).astype(BF16)
        srhs[:, nz : 4 * nz] = three(oh, rec[:, 0:1])
        srhs[:, 4 * nz :] = three(oh, rec[:, 1:2])
        erhs[...] = three(column_onehot(epos_col[...], nz), drive_at(delay[...], drive[...], 1))

    plane = ids[1] * 4 + i
    s = plane_onehot(spos_row[...], plane, ny, nz)
    cnt[0] = dot(s, srhs[:, :nz])
    d0[0] = sum3(dot(s, srhs[:, nz : 4 * nz]), nz)
    d1[0] = sum3(dot(s, srhs[:, 4 * nz :]), nz)
    e1[0] = sum3(dot(plane_onehot(epos_row[...], plane, ny, nz), erhs[...]), nz)


def maps_call(ids, spos, rec, epos, delay, drive, shape):
    nx, ny, nz = shape
    plane = pl.BlockSpec((1, ny, nz), lambda i: (i, 0, 0))
    n_e, n_s = epos.shape[0], spos.shape[0]
    nat = jax.ShapeDtypeStruct(shape, F32)
    return pl.pallas_call(
        maps_kernel,
        grid=(nx,),
        in_specs=[smem(), whole((1, n_s)), whole((n_s, 1)), whole((n_s, STEPS)),
                  whole((1, n_e)), whole((n_e, 1)), whole((n_e, 1)), whole((1, drive.shape[0]))],
        out_specs=[plane] * 4,
        out_shape=[nat] * 4,
        scratch_shapes=[pltpu.VMEM((n_s, 7 * nz), BF16), pltpu.VMEM((n_e, 3 * nz), BF16)],
        compiler_params=params(1),
        cost_estimate=pl.CostEstimate(flops=4 * 10**9, bytes_accessed=5 * 2**20, transcendentals=0),
        name="maps",
    )(
        ids, spos.reshape(1, -1), spos.reshape(-1, 1), rec.T, epos.reshape(1, -1),
        epos.reshape(-1, 1), delay.reshape(-1, 1), drive.reshape(1, -1),
    )


def line_get(ref, f, yl):
    return jnp.concatenate([ref[0, :, xl, 2 * f + yl, :] for xl in range(4)], axis=0)


def mat_get(ref, f, yl):
    return jnp.concatenate(
        [ref[xl // 2, :, 0, 4 * (xl % 2) + 2 * f + yl, :] for xl in range(4)], axis=0
    )


def pair_get(ref, f, yl):
    return jnp.concatenate(
        [ref[0, :, xl // 2, 4 * (xl % 2) + 2 * f + yl, :] for xl in range(4)], axis=0
    )


def pair_put(ref, g, f, yl, v):
    n = v.shape[0] // 4
    for xl in range(4):
        ref[g, :, xl // 2, 4 * (xl % 2) + 2 * f + yl, :] = v[xl * n : (xl + 1) * n]


def forward_kernel(fields, mat, gm, tm, out, gx0, gx1):
    for yl in range(2):
        b = DT * mat_get(mat, 0, yl)
        bulk = DT * mat_get(mat, 1, yl)
        g0 = left(gm, line_get(fields, 0, yl))
        u1 = line_get(fields, 1, yl) - b * g0
        x0 = left(tm, u1)
        p1 = line_get(fields, 2, yl) + bulk * x0
        g1 = left(gm, p1)
        x1 = left(tm, u1 - b * g1)
        gx0[0, yl] = g0
        gx1[0, yl] = g1
        pair_put(out, 0, 0, yl, x0)
        pair_put(out, 0, 1, yl, x1)


def forward_call(buf, mats):
    _, ns, _, _, nz = buf.shape
    nx = 4 * ns
    line = pl.BlockSpec((1, 2, nx, nz), lambda g: (g, 0, 0, 0))
    return pl.pallas_call(
        forward_kernel,
        grid=(2,),
        in_specs=[pl.BlockSpec((1, ns, 4, 8, nz), lambda g: (g, 0, 0, 0, 0)),
                  pl.BlockSpec((2, ns, 1, 8, nz), lambda g: (0, 0, 4, 0, 0))]
        + [whole((nx, nx))] * 2,
        out_specs=[pl.BlockSpec((1, ns, 2, 8, nz), lambda g: (g, 0, 0, 0, 0)), line, line],
        out_shape=[jax.ShapeDtypeStruct((2, ns, 2, 8, nz), F32)]
        + [jax.ShapeDtypeStruct((2, 2, nx, nz), F32)] * 2,
        compiler_params=params(1),
        cost_estimate=pl.CostEstimate(flops=16 * 10**8, bytes_accessed=9 * 2**20, transcendentals=0),
        name="lines_forward",
    )(buf, buf, *mats)


def plane_get(ref, i, f, dst):
    half = dst.shape[0] // 2
    for xm in range(2):

        @pl.when(lax.rem(i, 2) == xm)
        def _():
            for yl in range(2):
                dst[yl * half : (yl + 1) * half, :] = ref[:, 0, 4 * xm + 2 * f + yl, :]


def middle_kernel(
    xs, c, rho, alpha, v0, u1y, u1z, yz0, gy0, gz0, pa, uya, uza, cnt, m0, m1, e1, gm, tm,
    buf, d0, w0, t1, t2, x0s, x1s,
):
    i = pl.program_id(0)
    half = c.shape[1] // 2
    plane_get(xs, i, 0, x0s)
    plane_get(xs, i, 1, x1s)
    x0, x1 = x0s[...], x1s[...]
    dens, speed = rho[0], c[0]
    b = 1.0 / dens
    dk = DT * (dens * speed * speed)
    keep = 1.0 - DT * alpha[0]
    p1 = v0[0] + dk * x0
    d0[0] = x0 + yz0[0]
    gy = left(gm, p1)
    gz = right(p1, tm)
    db = DT * b
    div1 = x1 + left(tm, u1y[0] - db * gy) + right(u1z[0] - db * gz, gm)
    p2 = keep * p1 + dk * div1 + e1[0]
    adj = pa[0] + (cnt[0] * p2 - m1[0])
    q = dk * adj
    ay = uya[0] + left(gm, q)
    az = uza[0] + right(q, tm)
    back = left(tm, b * ay) + right(b * az, gm)
    w = keep * adj - DT * back + (cnt[0] * p1 - m0[0])
    w0[0] = w
    t1[0] = div1 * adj
    t2[0] = (gy + gy0[0]) * ay + (gz + gz0[0]) * az
    for xm in range(2):

        @pl.when(lax.rem(i, 2) == xm)
        def _():
            for yl in range(2):
                rows = slice(yl * half, (yl + 1) * half)
                buf[:, 0, 4 * xm + yl, :] = q[rows]
                buf[:, 0, 4 * xm + 2 + yl, :] = w[rows]


def middle_call(xs, fields, pa, v, maps, mats):
    ndev, _, _, nz = xs.shape
    nx, ny, _ = fields[0].shape
    plane = pl.BlockSpec((1, ny, nz), lambda i: (i, 0, 0))
    pick = lambda i: i
    vec = group_plane(v.shape, pick)
    pair = pl.BlockSpec((ndev, 1, 8, nz), lambda i: (0, i // 2, 0, 0))
    nat = jax.ShapeDtypeStruct((nx, ny, nz), F32)
    return pl.pallas_call(
        middle_kernel,
        grid=(nx,),
        in_specs=[pair] + [plane] * len(fields) + [group_plane(pa.shape, pick)(0), vec(1), vec(2)]
        + [plane] * len(maps) + [whole((ny, ny))] * 2,
        out_specs=[pair] + [plane] * 4,
        out_shape=[jax.ShapeDtypeStruct(xs.shape, F32)] + [nat] * 4,
        scratch_shapes=[pltpu.VMEM((ny, nz), F32)] * 2,
        compiler_params=params(1),
        cost_estimate=pl.CostEstimate(flops=32 * 10**8, bytes_accessed=24 * 2**20, transcendentals=0),
        name="slab_middle",
    )(xs, *fields, pa, v, v, *maps, *mats)


def adjoint_kernel(qw, fields, mat, gx0, gx1, gm, tm, out, acc):
    g = pl.program_id(0)
    for yl in range(2):
        b = mat_get(mat, 0, yl)
        bulk = DT * mat_get(mat, 1, yl)
        ax = line_get(fields, 3, yl) + left(gm, pair_get(qw, 0, yl))
        back = left(tm, b * ax)
        q0 = bulk * (pair_get(qw, 1, yl) - DT * back)
        bx = gx1[0, yl] * ax + gx0[0, yl] * (ax + left(gm, q0))
        pair_put(out, g, 0, yl, back)

        @pl.when(g == 0)
        def _():
            acc[yl] = bx

        @pl.when(g == 1)
        def _():
            total = acc[yl] + bx
            pair_put(out, 0, 1, yl, total)
            pair_put(out, 1, 1, yl, total)


def adjoint_call(qw, buf, gx0, gx1, mats):
    _, ns, _, _, nz = buf.shape
    nx = 4 * ns
    line = pl.BlockSpec((1, 2, nx, nz), lambda g: (g, 0, 0, 0))
    return pl.pallas_call(
        adjoint_kernel,
        grid=(2,),
        in_specs=[pl.BlockSpec((1, ns, 2, 8, nz), lambda g: (g, 0, 0, 0, 0)),
                  pl.BlockSpec((1, ns, 4, 8, nz), lambda g: (g, 0, 0, 0, 0)),
                  pl.BlockSpec((2, ns, 1, 8, nz), lambda g: (0, 0, 4, 0, 0)), line, line]
        + [whole((nx, nx))] * 2,
        out_specs=whole((2, ns, 2, 8, nz)),
        out_shape=jax.ShapeDtypeStruct((2, ns, 2, 8, nz), F32),
        scratch_shapes=[pltpu.VMEM((2, nx, nz), F32)],
        compiler_params=params(1),
        cost_estimate=pl.CostEstimate(flops=12 * 10**8, bytes_accessed=11 * 2**20, transcendentals=0),
        name="lines_adjoint",
    )(qw, buf, buf, gx0, gx1, *mats)


def last_kernel(xs, c, rho, d0, w0, t1, t2, gy0, gz0, gm, tm, out, bx, xb):
    i = pl.program_id(0)
    plane_get(xs, i, 0, xb)
    plane_get(xs, i, 1, bx.at[0])
    p = w0[0] - DT * xb[...]
    q = (DT * (rho[0] * c[0] * c[0])) * p
    out[0, 0] = t1[0] + d0[0] * p
    out[1, 0] = t2[0] + gy0[0] * left(gm, q) + gz0[0] * right(q, tm)


def last_call(xs, fields, mats):
    ndev, _, _, nz = xs.shape
    nx, ny, _ = fields[0].shape
    plane = pl.BlockSpec((1, ny, nz), lambda i: (i, 0, 0))
    return pl.pallas_call(
        last_kernel,
        grid=(nx,),
        in_specs=[pl.BlockSpec((ndev, 1, 8, nz), lambda i: (0, i // 2, 0, 0))]
        + [plane] * len(fields) + [whole((ny, ny))] * 2,
        out_specs=[pl.BlockSpec((2, 1, ny, nz), lambda i: (0, i, 0, 0)), plane],
        out_shape=[jax.ShapeDtypeStruct((2, nx, ny, nz), F32), jax.ShapeDtypeStruct((nx, ny, nz), F32)],
        scratch_shapes=[pltpu.VMEM((ny, nz), F32)],
        compiler_params=params(1),
        cost_estimate=pl.CostEstimate(flops=8 * 10**8, bytes_accessed=13 * 2**20, transcendentals=0),
        name="slab_last",
    )(xs, *fields, *mats)


def change_layout(v):
    return lax.all_to_all(v, ALL, split_axis=0, concat_axis=0, tiled=True)


def local(
    sound_speed, density, absorption, pressure_start, velocity_start, adjoint_pressure,
    adjoint_velocity, emitter_voxel, emitter_delay, drive_waveform_samples, recorded_pressures,
    sensor_flat_position,
):
    n_emit, n_slab = lax.axis_size("emit"), lax.axis_size("slab")
    ndev = n_emit * n_slab
    planes, ny, nz = sound_speed.shape
    nx = planes * n_slab
    ids = jnp.stack([lax.axis_index("emit"), lax.axis_index("slab")]).astype(jnp.int32)
    mats = pair_const(deriv_matrix(ny))
    order = (4 * np.arange(n_slab)[None, :] + np.arange(4)[:, None]).reshape(-1)
    line_mats = pair_const(deriv_matrix(nx)[np.ix_(order, order)])
    epos, delay, drive = emitter_voxel[0], emitter_delay[0], drive_waveform_samples
    buf, u1y, u1z, yz0, gy0, gz0, v0 = start_call(
        ids, sound_speed, density, absorption, pressure_start, velocity_start, adjoint_velocity,
        epos, delay, drive, mats, ndev,
    )
    cnt, m0, m1, e1 = maps_call(
        ids, sensor_flat_position, recorded_pressures[0], epos, delay, drive, sound_speed.shape
    )
    lines = change_layout(buf).reshape(n_emit, n_slab, 5, 8, nz)
    xs, gx0, gx1 = forward_call(lines, line_mats)
    xs = change_layout(xs.reshape(ndev, 2, 8, nz))
    qw, d0, w0, t1, t2 = middle_call(
        xs,
        [sound_speed, density, absorption, v0, u1y, u1z, yz0, gy0, gz0],
        adjoint_pressure, adjoint_velocity, [cnt, m0, m1, e1], mats,
    )
    qw = change_layout(qw).reshape(n_emit, n_slab, 2, 8, nz)
    xs = adjoint_call(qw, lines, gx0, gx1, line_mats)
    xs = change_layout(xs.reshape(ndev, 2, 8, nz))
    t, bx = last_call(xs, [sound_speed, density, d0, w0, t1, t2, gy0, gz0], mats)
    other = lax.ppermute(t, "emit", [(0, 1), (1, 0)])
    s1 = t[0] + other[0]
    s2 = t[1] + other[1] + bx
    b = 1.0 / density
    speed_total = (2.0 * DT) * s1 * density * sound_speed
    density_total = DT * (s1 * sound_speed * sound_speed + s2 * b * b)
    return speed_total, density_total


def solution(mesh):
    in_specs = (
        P("slab", None, None), P("slab", None, None), P("slab", None, None),
        P("emit", "slab", None, None), P("emit", None, "slab", None, None),
        P("emit", "slab", None, None), P("emit", None, "slab", None, None),
        P("emit", None), P("emit", None), P(), P("emit", None, None), P(),
    )
    out_specs = (P("slab", None, None), P("slab", None, None))
    return jax.shard_map(local, mesh=mesh, in_specs=in_specs, out_specs=out_specs, check_vma=False)
```

```python
import numpy as np
import jax
import jax.numpy as jnp
from jax import lax
from jax.experimental import pallas as pl
from jax.experimental.pallas import tpu as pltpu
from jax.sharding import PartitionSpec as P

STEPS = 2
DT = 0.2
F32 = jnp.float32
BF16 = jnp.bfloat16
ALL = ("emit", "slab")
MIB = 2**20


def deriv_matrix(n):
    k = np.arange(1, n // 2, dtype=np.int64)
    pts = np.arange(n, dtype=np.int64)
    shifted = (k[None, :] * (2 * pts[:, None] + 1)) % (2 * n) * (np.pi / n)
    plain = (k[None, :] * (2 * pts[:, None])) % (2 * n) * (np.pi / n)
    w = k * (2.0 * np.pi / n)
    m = (np.cos(shifted) * w) @ np.sin(plain).T - (np.sin(shifted) * w) @ np.cos(plain).T
    return m * (2.0 / n)


def pair_const(m):
    m = m.astype(np.float32)
    return [jnp.asarray(m), jnp.asarray(np.ascontiguousarray(m.T))]


def split2(v):
    hi = v.astype(BF16)
    return hi, (v - hi.astype(F32)).astype(BF16)


def split3(v):
    hi = v.astype(BF16)
    rest = v - hi.astype(F32)
    mid = rest.astype(BF16)
    return hi, mid, (rest - mid.astype(F32)).astype(BF16)


def dot(a, b):
    return jnp.dot(a, b, preferred_element_type=F32)


def left(m, v):
    mh, ml = split2(m[...])
    h, l = split2(v)
    return dot(mh, h) + (dot(mh, l) + dot(ml, h))


def right(v, m):
    mh, ml = split2(m[...])
    h, l = split2(v)
    return dot(h, mh) + (dot(l, mh) + dot(h, ml))


def params(mib):
    return pltpu.CompilerParams(
        dimension_semantics=("arbitrary",), vmem_limit_bytes=mib * MIB
    )


def cost(mflop, mib):
    return pl.CostEstimate(flops=mflop * 10**6, bytes_accessed=mib * MIB, transcendentals=0)


def swap(v):
    return jnp.swapaxes(v, 0, 1)


def whole(shape):
    return pl.BlockSpec(shape, lambda i, ids: (0,) * len(shape))


def group_plane(shape, pick, a=0):
    block = (None,) * (len(shape) - 3) + (1,) + shape[-2:]
    return pl.BlockSpec(block, lambda i, ids: (0, a)[: len(shape) - 3] + (pick(i, ids), 0, 0))


def plane_onehot(pos, plane, ny, nz):
    local = pos - plane * (ny * nz)
    y = lax.broadcasted_iota(jnp.int32, (ny, pos.shape[1]), 0) * nz
    return jnp.where((local >= y) & (local < y + nz), 1.0, 0.0).astype(BF16)


def column_onehot(pos, nz):
    z = lax.broadcasted_iota(jnp.int32, (nz, pos.shape[1]), 0)
    return lax.rem(pos, nz) == z


def drive_at(delay, drive, step):
    amp = jnp.zeros(delay.shape, F32)
    for k in range(drive.shape[0]):
        amp = jnp.where(delay + step == k, drive[k], amp)
    return amp


def three(onehot, value):
    return jnp.concatenate(
        [jnp.where(onehot, v.astype(F32), 0.0).astype(BF16) for v in split3(value)], axis=0
    )


def spread(rows, cols):
    return lax.dot_general(rows, cols, (((1,), (1,)), ((), ())), preferred_element_type=F32)


def sum3(v):
    n = v.shape[1] // 3
    return v[:, :n] + v[:, n : 2 * n] + v[:, 2 * n :]


def start_kernel(
    ids, drive, c, rho, alpha, p0, ux, uy, uz, vx, epos, delay, gm, tm,
    buf, u1y, u1z, yz0, gy0, gz0, v0, mat, cols, pack,
):
    i = pl.program_id(0)
    ny, nz = p0.shape[1], p0.shape[2]
    half = ny // 2

    @pl.when(i == 0)
    def _():
        cols[...] = three(column_onehot(epos[...], nz), drive_at(delay[...], drive, 0))

    @pl.when(i < 4)
    def _():
        dens, speed, p = rho[0], c[0], p0[0]
        b = 1.0 / dens
        bulk = dens * speed * speed
        gy = left(gm, p)
        gz = right(p, tm)
        wy = uy[0] - DT * b * gy
        wz = uz[0] - DT * b * gz
        yz = left(tm, wy) + right(wz, gm)
        shot = sum3(spread(plane_onehot(epos[...], ids[1] * 4 + i, ny, nz), cols[...]))
        v = (1.0 - DT * alpha[0]) * p + (DT * bulk) * yz + shot
        u1y[0], u1z[0], yz0[0], gy0[0], gz0[0], v0[0] = wy, wz, yz, gy, gz, v
        for f, field in enumerate((p, ux[0], v, vx[0])):
            pack[2 * f : 2 * f + 2] = field.reshape(2, half, nz)
        buf[:, 0] = swap(pack[...])
        for xm in range(2):

            @pl.when(i == 2 * ids[0] + xm)
            def _():
                mat[4 * xm : 4 * xm + 2] = b.reshape(2, half, nz)
                mat[4 * xm + 2 : 4 * xm + 4] = bulk.reshape(2, half, nz)

    @pl.when(i == 4)
    def _():
        buf[:, 0] = swap(mat[...])


def start_call(ids, c, rho, alpha, p0, u, v, epos, delay, drive, mats, ndev):
    nx, ny, nz = c.shape
    pick = lambda i, ids: jnp.minimum(i, nx - 1)
    plane = group_plane(c.shape, pick)
    n_e = epos.shape[1]
    nat = jax.ShapeDtypeStruct(c.shape, F32)
    return pl.pallas_call(
        start_kernel,
        grid_spec=pltpu.PrefetchScalarGridSpec(
            num_scalar_prefetch=1,
            grid=(nx + 1,),
            in_specs=[pl.BlockSpec(memory_space=pltpu.SMEM)] + [plane] * 3
            + [group_plane(p0.shape, pick)]
            + [group_plane(u.shape, pick, a) for a in (0, 1, 2, 0)]
            + [whole((1, n_e))] * 2 + [whole((ny, ny))] * 2,
            out_specs=[pl.BlockSpec((ndev, 1, 8, nz), lambda i, ids: (0, i, 0, 0))] + [plane] * 6,
            scratch_shapes=[pltpu.VMEM((8, ndev, nz), F32), pltpu.VMEM((3 * nz, n_e), BF16),
                            pltpu.VMEM((8, ndev, nz), F32)],
        ),
        out_shape=[jax.ShapeDtypeStruct((ndev, 5, 8, nz), F32)] + [nat] * 6,
        compiler_params=params(60),
        cost_estimate=cost(2000, 19),
        name="start",
    )(ids, drive, c, rho, alpha, p0, u, u, u, v, epos, delay, *mats)


def maps_kernel(ids, drive, spos, rec, epos, delay, cnt, d0, d1, e1, scols, ecols):
    i = pl.program_id(0)
    ny, nz = cnt.shape[1], cnt.shape[2]

    @pl.when(i == 0)
    def _():
        oh = column_onehot(spos[...], nz)
        scols[:nz] = jnp.where(oh, 1.0, 0.0).astype(BF16)
        scols[nz : 4 * nz] = three(oh, rec[0:1])
        scols[4 * nz :] = three(oh, rec[1:2])
        ecols[...] = three(column_onehot(epos[...], nz), drive_at(delay[...], drive, 1))

    plane = ids[1] * 4 + i
    s = plane_onehot(spos[...], plane, ny, nz)
    cnt[0] = spread(s, scols[:nz])
    d0[0] = sum3(spread(s, scols[nz : 4 * nz]))
    d1[0] = sum3(spread(s, scols[4 * nz :]))
    e1[0] = sum3(spread(plane_onehot(epos[...], plane, ny, nz), ecols[...]))


def maps_call(ids, spos, rec, epos, delay, drive, shape):
    nx, ny, nz = shape
    n_e, n_s = epos.shape[1], spos.shape[1]
    return pl.pallas_call(
        maps_kernel,
        grid_spec=pltpu.PrefetchScalarGridSpec(
            num_scalar_prefetch=1,
            grid=(nx,),
            in_specs=[pl.BlockSpec(memory_space=pltpu.SMEM), whole((1, n_s)),
                      pl.BlockSpec((None, STEPS, n_s), lambda i, ids: (0, 0, 0)),
                      whole((1, n_e)), whole((1, n_e))],
            out_specs=[group_plane(shape, lambda i, ids: i)] * 4,
            scratch_shapes=[pltpu.VMEM((7 * nz, n_s), BF16), pltpu.VMEM((3 * nz, n_e), BF16)],
        ),
        out_shape=[jax.ShapeDtypeStruct(shape, F32)] * 4,
        compiler_params=params(32),
        cost_estimate=cost(4000, 5),
        name="maps",
    )(ids, drive, spos, rec, epos, delay)


def unpack(block, dst, first):
    t = swap(block)
    n = t.shape[1]
    for xm in range(2):
        dst[:, (first + xm) * n : (first + xm + 1) * n, :] = t[4 * xm : 4 * xm + 4]


def forward_kernel(ids, fields, mat, gm, tm, out, gx0, gx1, ax, bk, f_s, o_s):
    n = fields.shape[1]

    @pl.when(pl.program_id(0) == 0)
    def _():
        for e in range(2):
            unpack(mat[e, :, 0], bk, 2 * e)

    for xl in range(4):
        f_s[:, xl * n : (xl + 1) * n, :] = swap(fields[0, :, xl])
    for yl in range(2):
        b = DT * bk[yl]
        bulk = DT * bk[2 + yl]
        g0 = left(gm, f_s[yl])
        u1 = f_s[2 + yl] - b * g0
        x0 = left(tm, u1)
        p1 = f_s[4 + yl] + bulk * x0
        g1 = left(gm, p1)
        gx0[0, yl] = g0
        gx1[0, yl] = g1
        ax[0, yl] = f_s[6 + yl]
        o_s[yl] = x0
        o_s[2 + yl] = left(tm, u1 - b * g1)
    for h in range(2):
        both = [o_s[:, (2 * h + xm) * n : (2 * h + xm + 1) * n, :] for xm in range(2)]
        out[0, :, h] = swap(jnp.concatenate(both, axis=0))


def forward_call(ids, buf, mats):
    _, ns, _, _, nz = buf.shape
    nx = 4 * ns
    line = pl.BlockSpec((1, 2, nx, nz), lambda g, ids: (g, 0, 0, 0))
    full = jax.ShapeDtypeStruct((2, 2, nx, nz), F32)
    return pl.pallas_call(
        forward_kernel,
        grid_spec=pltpu.PrefetchScalarGridSpec(
            num_scalar_prefetch=1,
            grid=(2,),
            in_specs=[pl.BlockSpec((1, ns, 4, 8, nz), lambda g, ids: (g, 0, 0, 0, 0)),
                      pl.BlockSpec((2, ns, 1, 8, nz), lambda g, ids: (0, 0, 4, 0, 0))]
            + [whole((nx, nx))] * 2,
            out_specs=[pl.BlockSpec((1, ns, 2, 8, nz), lambda g, ids: (g, 0, 0, 0, 0)),
                       line, line, line, whole((4, nx, nz))],
            scratch_shapes=[pltpu.VMEM((8, nx, nz), F32), pltpu.VMEM((4, nx, nz), F32)],
        ),
        out_shape=[jax.ShapeDtypeStruct((2, ns, 2, 8, nz), F32), full, full, full,
                   jax.ShapeDtypeStruct((4, nx, nz), F32)],
        compiler_params=params(36),
        cost_estimate=cost(1600, 11),
        name="lines_forward",
    )(ids, buf, buf, *mats)


def middle_kernel(
    ids, xs, c, rho, alpha, v0, u1y, u1z, yz0, gy0, gz0, pa, uya, uza, cnt, m0, m1, e1, gm, tm,
    buf, send, keep, x_s, o_s,
):
    i = pl.program_id(0)
    xm = lax.rem(i, 2)
    ny, nz = c.shape[1], c.shape[2]
    half = ny // 2

    @pl.when(xm == 0)
    def _():
        x_s[...] = swap(xs[:, 0]).reshape(4, ny, nz)

    x0, x1 = x_s[2 * xm], x_s[2 * xm + 1]
    dens, speed = rho[0], c[0]
    b = 1.0 / dens
    dk = DT * (dens * speed * speed)
    stay = 1.0 - DT * alpha[0]
    p1 = v0[0] + dk * x0
    gy = left(gm, p1)
    gz = right(p1, tm)
    db = DT * b
    div1 = x1 + left(tm, u1y[0] - db * gy) + right(u1z[0] - db * gz, gm)
    p2 = stay * p1 + dk * div1 + e1[0]
    adj = pa[0] + (cnt[0] * p2 - m1[0])
    q = dk * adj
    ay = uya[0] + left(gm, q)
    az = uza[0] + right(q, tm)
    back = left(tm, b * ay) + right(b * az, gm)
    o_s[2 * xm] = q
    o_s[2 * xm + 1] = stay * adj - DT * back + (cnt[0] * p1 - m0[0])
    d0 = x0 + yz0[0]
    t1 = div1 * adj
    t2 = (gy + gy0[0]) * ay + (gz + gz0[0]) * az

    @pl.when(i < 2)
    def _():
        send[0, 0], send[0, 1], send[0, 2] = d0, t1, t2

    @pl.when(i >= 2)
    def _():
        keep[0, 0], keep[0, 1], keep[0, 2] = d0, t1, t2

    @pl.when(xm == 1)
    def _():
        buf[:, 0] = swap(o_s[...].reshape(8, half, nz))


def middle_call(ids, xs, fields, pa, v, maps, mats):
    ndev, _, _, nz = xs.shape
    nx, ny, _ = fields[0].shape
    pick = lambda i, ids: lax.rem(i + 2 * (1 - ids[0]), nx)
    plane = group_plane(fields[0].shape, pick)
    pair = pl.BlockSpec((ndev, 1, 8, nz), lambda i, ids: (0, pick(i, ids) // 2, 0, 0))
    three_fields = lambda f: pl.BlockSpec((1, 3, ny, nz), lambda i, ids: (f(i), 0, 0, 0))
    part = jax.ShapeDtypeStruct((2, 3, ny, nz), F32)
    return pl.pallas_call(
        middle_kernel,
        grid_spec=pltpu.PrefetchScalarGridSpec(
            num_scalar_prefetch=1,
            grid=(nx,),
            in_specs=[pair] + [plane] * len(fields) + [group_plane(pa.shape, pick)]
            + [group_plane(v.shape, pick, a) for a in (1, 2)]
            + [plane] * len(maps) + [whole((ny, ny))] * 2,
            out_specs=[pair, three_fields(lambda i: jnp.minimum(i, 1)),
                       three_fields(lambda i: jnp.maximum(i - 2, 0))],
            scratch_shapes=[pltpu.VMEM((4, ny, nz), F32)] * 2,
        ),
        out_shape=[jax.ShapeDtypeStruct(xs.shape, F32), part, part],
        compiler_params=params(36),
        cost_estimate=cost(3200, 24),
        name="slab_middle",
    )(ids, xs, *fields, pa, v, v, *maps, *mats)


def adjoint_kernel(ids, qw, ux, bk, gx0, gx1, gm, tm, out, f_s, p_s, bx_s):
    g = pl.program_id(0)
    n = qw.shape[1]
    nz = qw.shape[4]
    for h in range(2):
        unpack(qw[0, :, h], f_s, 2 * h)
    for yl in range(2):
        ax = ux[0, yl] + left(gm, f_s[yl])
        p0 = f_s[2 + yl] - DT * left(tm, bk[yl] * ax)
        p_s[2 * g + yl] = p0
        bx = gx1[0, yl] * ax + gx0[0, yl] * (ax + left(gm, (DT * bk[2 + yl]) * p0))

        @pl.when(g == 0)
        def _():
            bx_s[yl] = bx

        @pl.when(g == 1)
        def _():
            bx_s[yl] += bx

    @pl.when(g == 1)
    def _():
        lanes = [slice(z, z + nz // 2) for z in (0, nz // 2)]
        for e in range(2):
            rows = [slice((2 * e + xm) * n, (2 * e + xm + 1) * n) for xm in range(2)]
            for zh, z in enumerate(lanes):
                v = [p_s[2 * gr : 2 * gr + 2, x, z] for gr in range(2) for x in rows]
                out[e, :, 8 * zh : 8 * zh + 8, :] = swap(jnp.concatenate(v, axis=0))
            v = [bx_s[:, x, z] for z in lanes for x in rows]
            out[e, :, 16:24, :] = swap(jnp.concatenate(v, axis=0))


def adjoint_call(ids, qw, ux, bk, gx0, gx1, mats):
    _, ns, _, _, nz = qw.shape
    nx = 4 * ns
    line = pl.BlockSpec((1, 2, nx, nz), lambda g, ids: (g, 0, 0, 0))
    return pl.pallas_call(
        adjoint_kernel,
        grid_spec=pltpu.PrefetchScalarGridSpec(
            num_scalar_prefetch=1,
            grid=(2,),
            in_specs=[pl.BlockSpec((1, ns, 2, 8, nz), lambda g, ids: (g, 0, 0, 0, 0)),
                      line, whole((4, nx, nz)), line, line]
            + [whole((nx, nx))] * 2,
            out_specs=whole((2, ns, 24, nz // 2)),
            scratch_shapes=[pltpu.VMEM((4, nx, nz), F32), pltpu.VMEM((4, nx, nz), F32),
                            pltpu.VMEM((2, nx, nz), F32)],
        ),
        out_shape=jax.ShapeDtypeStruct((2, ns, 24, nz // 2), F32),
        compiler_params=params(36),
        cost_estimate=cost(1200, 9),
        name="lines_adjoint",
    )(ids, qw, ux, bk, gx0, gx1, *mats)


def last_kernel(ids, xs, c, rho, pa, pb, ta, tb, gm, tm, out, p_s, bx_s):
    i = pl.program_id(0)
    ny, nz = c.shape[1], c.shape[2]
    half = ny // 2

    @pl.when(i == 0)
    def _():
        for zh in range(2):
            z = slice(zh * (nz // 2), (zh + 1) * (nz // 2))
            p_s[:, :, z] = swap(xs[:, 8 * zh : 8 * zh + 8, :]).reshape(4, ny, nz // 2)
        t = swap(xs[:, 16:24, :]).reshape(4, ny, nz // 2)
        for zh in range(2):
            bx_s[:, :, zh * (nz // 2) : (zh + 1) * (nz // 2)] = t[2 * zh : 2 * zh + 2]

    dens, speed = rho[0], c[0]
    dk = DT * (dens * speed * speed)
    s1 = ta[0, 1] + tb[0, 1]
    s2 = ta[0, 2] + tb[0, 2] + bx_s[i]
    for group, start, t in ((ids[0], pa, ta), (1 - ids[0], pb, tb)):
        p = p_s[2 * group + i]
        q = dk * p
        s1 += t[0, 0] * p
        s2 += left(gm, start[0]) * left(gm, q) + right(start[0], tm) * right(q, tm)
    b = 1.0 / dens
    out[0, 0] = (2.0 * DT) * s1 * dens * speed
    out[1, 0] = DT * (s1 * speed * speed + s2 * b * b)


def last_call(ids, xs, c, rho, p0, p0_other, keep, other, mats):
    nx, ny, nz = c.shape
    pick = lambda i, ids: 2 * ids[0] + i
    plane = group_plane(c.shape, pick)
    three_fields = pl.BlockSpec((1, 3, ny, nz), lambda i, ids: (i, 0, 0, 0))
    return pl.pallas_call(
        last_kernel,
        grid_spec=pltpu.PrefetchScalarGridSpec(
            num_scalar_prefetch=1,
            grid=(2,),
            in_specs=[whole(xs.shape), plane, plane, group_plane(p0.shape, pick),
                      pl.BlockSpec((1, ny, nz), lambda i, ids: (i, 0, 0)), three_fields, three_fields]
            + [whole((ny, ny))] * 2,
            out_specs=pl.BlockSpec((2, 1, ny, nz), lambda i, ids: (0, i, 0, 0)),
            scratch_shapes=[pltpu.VMEM((4, ny, nz), F32), pltpu.VMEM((2, ny, nz), F32)],
        ),
        out_shape=jax.ShapeDtypeStruct((2, 2, ny, nz), F32),
        compiler_params=params(36),
        cost_estimate=cost(1100, 9),
        name="slab_last",
    )(ids, xs, c, rho, p0, p0_other, keep, other, *mats)


def change_layout(v):
    return lax.all_to_all(v, ALL, split_axis=0, concat_axis=0, tiled=True)


def swap_groups(v):
    return lax.ppermute(v, "emit", [(0, 1), (1, 0)])


def local(
    sound_speed, density, absorption, pressure_start, velocity_start, adjoint_pressure,
    adjoint_velocity, emitter_voxel, emitter_delay, drive_waveform_samples, recorded_pressures,
    sensor_flat_position,
):
    n_emit, n_slab = lax.axis_size("emit"), lax.axis_size("slab")
    ndev = n_emit * n_slab
    planes, ny, nz = sound_speed.shape
    nx = planes * n_slab
    emit = lax.axis_index("emit")
    ids = jnp.stack([emit, lax.axis_index("slab")]).astype(jnp.int32)
    mats = pair_const(deriv_matrix(ny))
    order = (4 * np.arange(n_slab)[None, :] + np.arange(4)[:, None]).reshape(-1)
    line_mats = pair_const(deriv_matrix(nx)[np.ix_(order, order)])

    p0_other = swap_groups(lax.dynamic_slice_in_dim(pressure_start[0], 2 * (1 - emit), 2, axis=0))
    buf, u1y, u1z, yz0, gy0, gz0, v0 = start_call(
        ids, sound_speed, density, absorption, pressure_start, velocity_start, adjoint_velocity,
        emitter_voxel, emitter_delay, drive_waveform_samples, mats, ndev,
    )
    maps = maps_call(
        ids, sensor_flat_position.reshape(1, -1), recorded_pressures, emitter_voxel,
        emitter_delay, drive_waveform_samples, sound_speed.shape,
    )
    lines = change_layout(buf).reshape(n_emit, n_slab, 5, 8, nz)
    xs, gx0, gx1, ux, bk = forward_call(ids, lines, line_mats)
    xs = change_layout(xs.reshape(ndev, 2, 8, nz))
    qw, send, keep = middle_call(
        ids, xs, [sound_speed, density, absorption, v0, u1y, u1z, yz0, gy0, gz0],
        adjoint_pressure, adjoint_velocity, maps, mats,
    )
    other = swap_groups(send)
    qw = change_layout(qw).reshape(n_emit, n_slab, 2, 8, nz)
    xs = adjoint_call(ids, qw, ux, bk, gx0, gx1, line_mats)
    xs = change_layout(xs.reshape(ndev, 24, nz // 2))
    own = last_call(
        ids, xs, sound_speed, density, pressure_start, p0_other, keep, other, mats
    )
    other = swap_groups(own)
    first = emit == 0
    out = jnp.concatenate(
        [jnp.where(first, own, other), jnp.where(first, other, own)], axis=1
    )
    return out[0], out[1]


def solution(mesh):
    in_specs = (
        P("slab", None, None), P("slab", None, None), P("slab", None, None),
        P("emit", "slab", None, None), P("emit", None, "slab", None, None),
        P("emit", "slab", None, None), P("emit", None, "slab", None, None),
        P("emit", None), P("emit", None), P(), P("emit", None, None), P(),
    )
    out_specs = (P("slab", None, None), P("slab", None, None))
    return jax.shard_map(local, mesh=mesh, in_specs=in_specs, out_specs=out_specs, check_vma=False)
```

```python
import numpy as np
import jax
import jax.numpy as jnp
from jax import lax
from jax.experimental import pallas as pl
from jax.experimental.pallas import tpu as pltpu
from jax.sharding import PartitionSpec as P

STEPS = 2
DT = 0.2
F32 = jnp.float32
BF16 = jnp.bfloat16
ALL = ("emit", "slab")
MIB = 2**20
LIMIT = {"start": 60, "prepare": 60, "forward": 60, "middle": 60, "adjoint": 60, "last": 60}


def deriv_matrix(n):
    k = np.arange(1, n // 2, dtype=np.int64)
    pts = np.arange(n, dtype=np.int64)
    shifted = (k[None, :] * (2 * pts[:, None] + 1)) % (2 * n) * (np.pi / n)
    plain = (k[None, :] * (2 * pts[:, None])) % (2 * n) * (np.pi / n)
    w = k * (2.0 * np.pi / n)
    m = (np.cos(shifted) * w) @ np.sin(plain).T - (np.sin(shifted) * w) @ np.cos(plain).T
    return m * (2.0 / n)


def pair_const(m):
    m = m.astype(np.float32)
    return [jnp.asarray(m), jnp.asarray(np.ascontiguousarray(m.T))]


def split2(v):
    hi = v.astype(BF16)
    return hi, (v - hi.astype(F32)).astype(BF16)


def split3(v):
    hi = v.astype(BF16)
    rest = v - hi.astype(F32)
    mid = rest.astype(BF16)
    return hi, mid, (rest - mid.astype(F32)).astype(BF16)


def dot(a, b):
    return jnp.dot(a, b, preferred_element_type=F32)


def left(m, v):
    mh, ml = split2(m[...])
    h, l = split2(v)
    return dot(mh, h) + (dot(mh, l) + dot(ml, h))


def right(v, m):
    mh, ml = split2(m[...])
    h, l = split2(v)
    return dot(h, mh) + (dot(l, mh) + dot(h, ml))


def params(mib, n_grid=1):
    return pltpu.CompilerParams(
        dimension_semantics=("arbitrary",) * n_grid, vmem_limit_bytes=mib * MIB
    )


def cost(mflop, mib):
    return pl.CostEstimate(flops=mflop * 10**6, bytes_accessed=mib * MIB, transcendentals=0)


def swap(v):
    return jnp.swapaxes(v, 0, 1)


def whole(shape):
    return pl.BlockSpec(shape, lambda i, ids: (0,) * len(shape))


def group_plane(shape, pick, a=0):
    block = (None,) * (len(shape) - 3) + (1,) + shape[-2:]
    return pl.BlockSpec(block, lambda i, ids: (0, a)[: len(shape) - 3] + (pick(i, ids), 0, 0))


def plane_onehot(pos, plane, ny, nz):
    local = pos - plane * (ny * nz)
    y = lax.broadcasted_iota(jnp.int32, (ny, pos.shape[1]), 0) * nz
    return jnp.where((local >= y) & (local < y + nz), 1.0, 0.0).astype(BF16)


def column_onehot(pos, nz):
    z = lax.broadcasted_iota(jnp.int32, (nz, pos.shape[1]), 0)
    return lax.rem(pos, nz) == z


def drive_at(delay, drive, step):
    amp = jnp.zeros(delay.shape, F32)
    for k in range(drive.shape[0]):
        amp = jnp.where(delay + step == k, drive[k], amp)
    return amp


def three(onehot, value):
    return jnp.concatenate(
        [jnp.where(onehot, v.astype(F32), 0.0).astype(BF16) for v in split3(value)], axis=0
    )


def spread(rows, cols):
    return lax.dot_general(rows, cols, (((1,), (1,)), ((), ())), preferred_element_type=F32)


def sum3(v):
    n = v.shape[1] // 3
    return v[:, :n] + v[:, n : 2 * n] + v[:, 2 * n :]


def first_step(c, rho, alpha, p0, uy, uz, epos, cols, plane, gm, tm):
    ny, nz = p0.shape[1], p0.shape[2]
    dens, speed, p = rho[0], c[0], p0[0]
    b = 1.0 / dens
    bulk = dens * speed * speed
    gy = left(gm, p)
    gz = right(p, tm)
    wy = uy[0] - DT * b * gy
    wz = uz[0] - DT * b * gz
    yz = left(tm, wy) + right(wz, gm)
    shot = sum3(spread(plane_onehot(epos[...], plane, ny, nz), cols[...]))
    v = (1.0 - DT * alpha[0]) * p + (DT * bulk) * yz + shot
    return gy, gz, wy, wz, yz, v, b, bulk


def start_kernel(
    ids, drive, c, rho, alpha, p0, ux, uy, uz, vx, epos, delay, gm, tm, buf, mat, cols, pack
):
    i = pl.program_id(0)
    ny, nz = p0.shape[1], p0.shape[2]
    half = ny // 2

    @pl.when(i == 0)
    def _():
        cols[...] = three(column_onehot(epos[...], nz), drive_at(delay[...], drive, 0))

    @pl.when(i < 4)
    def _():
        _, _, _, _, _, v, b, bulk = first_step(
            c, rho, alpha, p0, uy, uz, epos, cols, ids[1] * 4 + i, gm, tm
        )
        for f, field in enumerate((p0[0], ux[0], v, vx[0])):
            pack[2 * f : 2 * f + 2] = field.reshape(2, half, nz)
        buf[:, 0] = swap(pack[...])
        for xm in range(2):

            @pl.when(i == 2 * ids[0] + xm)
            def _():
                mat[4 * xm : 4 * xm + 2] = b.reshape(2, half, nz)
                mat[4 * xm + 2 : 4 * xm + 4] = bulk.reshape(2, half, nz)

    @pl.when(i == 4)
    def _():
        buf[:, 0] = swap(mat[...])


def start_call(ids, c, rho, alpha, p0, u, v, epos, delay, drive, mats, ndev):
    nx, ny, nz = c.shape
    pick = lambda i, ids: jnp.minimum(i, nx - 1)
    plane = group_plane(c.shape, pick)
    n_e = epos.shape[1]
    return pl.pallas_call(
        start_kernel,
        grid_spec=pltpu.PrefetchScalarGridSpec(
            num_scalar_prefetch=1,
            grid=(nx + 1,),
            in_specs=[pl.BlockSpec(memory_space=pltpu.SMEM)] + [plane] * 3
            + [group_plane(p0.shape, pick)]
            + [group_plane(u.shape, pick, a) for a in (0, 1, 2, 0)]
            + [whole((1, n_e))] * 2 + [whole((ny, ny))] * 2,
            out_specs=pl.BlockSpec((ndev, 1, 8, nz), lambda i, ids: (0, i, 0, 0)),
            scratch_shapes=[pltpu.VMEM((8, ndev, nz), F32), pltpu.VMEM((3 * nz, n_e), BF16),
                            pltpu.VMEM((8, ndev, nz), F32)],
        ),
        out_shape=jax.ShapeDtypeStruct((ndev, 5, 8, nz), F32),
        compiler_params=params(LIMIT["start"]),
        cost_estimate=cost(2000, 13),
        name="start",
    )(ids, drive, c, rho, alpha, p0, u, u, u, v, epos, delay, *mats)


def prepare_kernel(
    ids, drive, c, rho, alpha, p0, uy, uz, pa, spos, rec, epos, delay, gm, tm,
    v0, u1y, u1z, yz0, gy0, gz0, cnt, m0, pm, scols, ecols,
):
    i = pl.program_id(0)
    ny, nz = cnt.shape[1], cnt.shape[2]

    @pl.when(i == 0)
    def _():
        oh = column_onehot(spos[...], nz)
        scols[:nz] = jnp.where(oh, 1.0, 0.0).astype(BF16)
        scols[nz : 4 * nz] = three(oh, rec[0:1])
        scols[4 * nz :] = three(oh, rec[1:2])
        for step in range(STEPS):
            ecols[step] = three(column_onehot(epos[...], nz), drive_at(delay[...], drive, step))

    plane = ids[1] * 4 + i
    gy0[0], gz0[0], u1y[0], u1z[0], yz0[0], v0[0], _, _ = first_step(
        c, rho, alpha, p0, uy, uz, epos, ecols.at[0], plane, gm, tm
    )
    s = plane_onehot(spos[...], plane, ny, nz)
    count = spread(s, scols[:nz])
    cnt[0] = count
    m0[0] = sum3(spread(s, scols[nz : 4 * nz]))
    shot = sum3(spread(plane_onehot(epos[...], plane, ny, nz), ecols[1]))
    pm[0] = pa[0] + (count * shot - sum3(spread(s, scols[4 * nz :])))


def prepare_call(ids, c, rho, alpha, p0, u, pa, spos, rec, epos, delay, drive, mats):
    nx, ny, nz = c.shape
    n_e, n_s = epos.shape[1], spos.shape[1]
    pick = lambda i, ids: i
    plane = group_plane(c.shape, pick)
    return pl.pallas_call(
        prepare_kernel,
        grid_spec=pltpu.PrefetchScalarGridSpec(
            num_scalar_prefetch=1,
            grid=(nx,),
            in_specs=[pl.BlockSpec(memory_space=pltpu.SMEM)] + [plane] * 3
            + [group_plane(p0.shape, pick)] + [group_plane(u.shape, pick, a) for a in (1, 2)]
            + [group_plane(pa.shape, pick), whole((1, n_s)),
               pl.BlockSpec((None, STEPS, n_s), lambda i, ids: (0, 0, 0)),
               whole((1, n_e)), whole((1, n_e))] + [whole((ny, ny))] * 2,
            out_specs=[plane] * 9,
            scratch_shapes=[pltpu.VMEM((7 * nz, n_s), BF16), pltpu.VMEM((STEPS, 3 * nz, n_e), BF16)],
        ),
        out_shape=[jax.ShapeDtypeStruct(c.shape, F32)] * 9,
        compiler_params=params(LIMIT["prepare"]),
        cost_estimate=cost(6000, 17),
        name="prepare",
    )(ids, drive, c, rho, alpha, p0, u, u, pa, spos, rec, epos, delay, *mats)


def unpack(block, dst, first):
    t = swap(block)
    n, hz = t.shape[1], t.shape[2]
    for xm in range(2):
        for f in range(2):
            for yl in range(2):
                dst[f, (first + xm) * n : (first + xm + 1) * n, yl * hz : (yl + 1) * hz] = t[4 * xm + 2 * f + yl]


def line_rows(v, xl, n):
    hz = v.shape[1] // 2
    rows = v[xl * n : (xl + 1) * n]
    return jnp.stack([rows[:, :hz], rows[:, hz:]])


def forward_kernel(ids, fields, mat, gm, tm, out, gx0, gx1, ax, bk, f_s, o_s):
    n, hz = fields.shape[1], fields.shape[4]

    @pl.when(pl.program_id(1) == 0)
    def _():
        for e in range(2):
            unpack(mat[e, :, 0], bk.at[0], 2 * e)

    for xl in range(4):
        t = swap(fields[0, :, xl])
        for f in range(4):
            dst = f_s if f < 3 else ax.at[0]
            for yl in range(2):
                dst[f if f < 3 else 0, xl * n : (xl + 1) * n, yl * hz : (yl + 1) * hz] = t[2 * f + yl]
    b = DT * bk[0, 0]
    g0 = left(gm, f_s[0])
    u1 = f_s[1] - b * g0
    x0 = left(tm, u1)
    g1 = left(gm, f_s[2] + (DT * bk[0, 1]) * x0)
    gx0[0, 0] = g0
    gx1[0, 0] = g1
    o_s[0] = x0
    o_s[1] = left(tm, u1 - b * g1)
    for h in range(2):
        rows = [line_rows(o_s[f], 2 * h + xm, n) for xm in range(2) for f in range(2)]
        out[0, :, h] = swap(jnp.concatenate(rows, axis=0))


def line_specs(nx, hz):
    return (pl.BlockSpec((1, 1, nx, 2 * hz), lambda zh, g, ids: (g, zh, 0, 0)),
            pl.BlockSpec((1, 2, nx, 2 * hz), lambda zh, g, ids: (zh, 0, 0, 0)),
            pl.BlockSpec((nx, nx), lambda zh, g, ids: (0, 0)))


def forward_call(ids, buf, mats):
    _, ns, _, _, nz = buf.shape
    nx, hz = 4 * ns, nz // 2
    line, pair, mat = line_specs(nx, hz)
    full = jax.ShapeDtypeStruct((2, 2, nx, nz), F32)
    return pl.pallas_call(
        forward_kernel,
        grid_spec=pltpu.PrefetchScalarGridSpec(
            num_scalar_prefetch=1,
            grid=(2, 2),
            in_specs=[pl.BlockSpec((1, ns, 4, 8, hz), lambda zh, g, ids: (g, 0, 0, 0, zh)),
                      pl.BlockSpec((2, ns, 1, 8, hz), lambda zh, g, ids: (0, 0, 4, 0, zh)), mat, mat],
            out_specs=[pl.BlockSpec((1, ns, 2, 8, hz), lambda zh, g, ids: (g, 0, 0, 0, zh)),
                       line, line, line, pair],
            scratch_shapes=[pltpu.VMEM((3, nx, nz), F32), pltpu.VMEM((2, nx, nz), F32)],
        ),
        out_shape=[jax.ShapeDtypeStruct((2, ns, 2, 8, nz), F32), full, full, full, full],
        compiler_params=params(LIMIT["forward"], 2),
        cost_estimate=cost(1600, 11),
        name="lines_forward",
    )(ids, buf, buf, *mats)


def middle_kernel(
    ids, xs, c, rho, alpha, uya, uza, v0, u1y, u1z, yz0, gy0, gz0, cnt, m0, pm, gm, tm,
    buf, d0, t1, t2, x_s, o_s,
):
    xm = lax.rem(pl.program_id(0), 2)
    ny, nz = c.shape[1], c.shape[2]
    half = ny // 2

    @pl.when(xm == 0)
    def _():
        x_s[...] = swap(xs[:, 0]).reshape(4, ny, nz)

    x0 = x_s[2 * xm]
    dens, speed = rho[0], c[0]
    b = 1.0 / dens
    dk = DT * (dens * speed * speed)
    stay = 1.0 - DT * alpha[0]
    p1 = v0[0] + dk * x0
    d0[0] = x0 + yz0[0]
    gy = left(gm, p1)
    gz = right(p1, tm)
    db = DT * b
    div1 = x_s[2 * xm + 1] + left(tm, u1y[0] - db * gy) + right(u1z[0] - db * gz, gm)
    adj = pm[0] + cnt[0] * (stay * p1 + dk * div1)
    q = dk * adj
    ay = uya[0] + left(gm, q)
    az = uza[0] + right(q, tm)
    back = left(tm, b * ay) + right(b * az, gm)
    o_s[2 * xm] = q
    o_s[2 * xm + 1] = stay * adj - DT * back + (cnt[0] * p1 - m0[0])
    t1[0] = div1 * adj
    t2[0] = (gy + gy0[0]) * ay + (gz + gz0[0]) * az

    @pl.when(xm == 1)
    def _():
        buf[:, 0] = swap(o_s[...].reshape(8, half, nz))


def middle_call(ids, xs, c, rho, alpha, v, fields, mats):
    ndev, _, _, nz = xs.shape
    nx, ny, _ = c.shape
    pick = lambda i, ids: i
    plane = group_plane(c.shape, pick)
    pair = pl.BlockSpec((ndev, 1, 8, nz), lambda i, ids: (0, i // 2, 0, 0))
    return pl.pallas_call(
        middle_kernel,
        grid_spec=pltpu.PrefetchScalarGridSpec(
            num_scalar_prefetch=1,
            grid=(nx,),
            in_specs=[pair] + [plane] * 3 + [group_plane(v.shape, pick, a) for a in (1, 2)]
            + [plane] * len(fields) + [whole((ny, ny))] * 2,
            out_specs=[pair] + [plane] * 3,
            scratch_shapes=[pltpu.VMEM((4, ny, nz), F32)] * 2,
        ),
        out_shape=[jax.ShapeDtypeStruct(xs.shape, F32)] + [jax.ShapeDtypeStruct(c.shape, F32)] * 3,
        compiler_params=params(LIMIT["middle"]),
        cost_estimate=cost(3200, 21),
        name="slab_middle",
    )(ids, xs, c, rho, alpha, v, v, *fields, *mats)


def adjoint_kernel(ids, qw, ux, bk, gx0, gx1, gm, tm, out, f_s, bx_s):
    zh, g = pl.program_id(0), pl.program_id(1)
    n, hz = qw.shape[1], qw.shape[4]
    for h in range(2):
        unpack(qw[0, :, h], f_s, 2 * h)
    ax = ux[0, 0] + left(gm, f_s[0])
    p0 = f_s[1] - DT * left(tm, bk[0, 0] * ax)
    bx = gx1[0, 0] * ax + gx0[0, 0] * (ax + left(gm, (DT * bk[0, 1]) * p0))
    rows = swap(jnp.concatenate([line_rows(p0, xl, n) for xl in range(4)], axis=0))
    for z in range(2):

        @pl.when(zh == z)
        def _():
            out[pl.ds(g, 1), :, 8 * z : 8 * z + 8, :] = rows[None]

    @pl.when(g == 0)
    def _():
        bx_s[zh] = bx

    @pl.when(g == 1)
    def _():
        bx_s[zh] += bx

    @pl.when((g == 1) & (zh == 1))
    def _():
        for e in range(2):
            v = [line_rows(bx_s[z], 2 * e + xm, n) for z in range(2) for xm in range(2)]
            out[e, :, 16:24, :] = swap(jnp.concatenate(v, axis=0))


def adjoint_call(ids, qw, ux, bk, gx0, gx1, mats):
    _, ns, _, _, nz = qw.shape
    nx, hz = 4 * ns, nz // 2
    line, pair, mat = line_specs(nx, hz)
    return pl.pallas_call(
        adjoint_kernel,
        grid_spec=pltpu.PrefetchScalarGridSpec(
            num_scalar_prefetch=1,
            grid=(2, 2),
            in_specs=[pl.BlockSpec((1, ns, 2, 8, hz), lambda zh, g, ids: (g, 0, 0, 0, zh)),
                      line, pair, line, line, mat, mat],
            out_specs=pl.BlockSpec((2, ns, 24, hz), lambda zh, g, ids: (0, 0, 0, 0)),
            scratch_shapes=[pltpu.VMEM((2, nx, nz), F32), pltpu.VMEM((2, nx, nz), F32)],
        ),
        out_shape=jax.ShapeDtypeStruct((2, ns, 24, hz), F32),
        compiler_params=params(LIMIT["adjoint"], 2),
        cost_estimate=cost(1200, 9),
        name="lines_adjoint",
    )(ids, qw, ux, bk, gx0, gx1, *mats)


def last_bulk_kernel(ids, xs, d0, t1, out, p0):
    p = swap(xs[...]).reshape(p0.shape)
    p0[...] = p
    out[...] = t1[...] + d0[...] * p


def last_bulk_call(ids, xs, d0, t1):
    nx, ny, nz = d0.shape
    part = pl.BlockSpec((nx, ny, nz // 2), lambda zh, ids: (0, 0, zh))
    return pl.pallas_call(
        last_bulk_kernel,
        grid_spec=pltpu.PrefetchScalarGridSpec(
            num_scalar_prefetch=1,
            grid=(2,),
            in_specs=[pl.BlockSpec((xs.shape[0], 8, nz // 2), lambda zh, ids: (0, zh, 0)), part, part],
            out_specs=[part, part],
        ),
        out_shape=[jax.ShapeDtypeStruct(d0.shape, F32)] * 2,
        compiler_params=params(LIMIT["last"]),
        cost_estimate=cost(1, 5),
        name="slab_last_bulk",
    )(ids, xs, d0, t1)


def last_buoy_kernel(ids, xs, p0, c, rho, t2, gy0, gz0, gm, tm, out, bx_s):
    i = pl.program_id(0)
    ny, nz = c.shape[1], c.shape[2]

    @pl.when(i == 0)
    def _():
        t = swap(xs[...]).reshape(4, ny, nz // 2)
        for zh in range(2):
            bx_s[:, :, zh * (nz // 2) : (zh + 1) * (nz // 2)] = t[2 * zh : 2 * zh + 2]

    q = (DT * (rho[0] * c[0] * c[0])) * p0[0]
    out[0] = t2[0] + gy0[0] * left(gm, q) + gz0[0] * right(q, tm)

    @pl.when(i // 2 == ids[0])
    def _():
        out[0] += bx_s[lax.rem(i, 2)]


def last_buoy_call(ids, xs, p0, c, rho, t2, gy0, gz0, mats):
    nx, ny, nz = c.shape
    plane = group_plane(c.shape, lambda i, ids: i)
    return pl.pallas_call(
        last_buoy_kernel,
        grid_spec=pltpu.PrefetchScalarGridSpec(
            num_scalar_prefetch=1,
            grid=(nx,),
            in_specs=[pl.BlockSpec((xs.shape[0], 8, nz // 2), lambda i, ids: (0, 2, 0))]
            + [plane] * 6 + [whole((ny, ny))] * 2,
            out_specs=plane,
            scratch_shapes=[pltpu.VMEM((2, ny, nz), F32)],
        ),
        out_shape=jax.ShapeDtypeStruct(c.shape, F32),
        compiler_params=params(LIMIT["last"]),
        cost_estimate=cost(800, 8),
        name="slab_last_buoy",
    )(ids, xs, p0, c, rho, t2, gy0, gz0, *mats)


def change_layout(v):
    return lax.all_to_all(v, ALL, split_axis=0, concat_axis=0, tiled=True)


def swap_groups(v):
    return lax.ppermute(v, "emit", [(0, 1), (1, 0)])


def local(
    sound_speed, density, absorption, pressure_start, velocity_start, adjoint_pressure,
    adjoint_velocity, emitter_voxel, emitter_delay, drive_waveform_samples, recorded_pressures,
    sensor_flat_position,
):
    n_emit, n_slab = lax.axis_size("emit"), lax.axis_size("slab")
    ndev = n_emit * n_slab
    planes, ny, nz = sound_speed.shape
    nx = planes * n_slab
    emit = lax.axis_index("emit")
    ids = jnp.stack([emit, lax.axis_index("slab")]).astype(jnp.int32)
    mats = pair_const(deriv_matrix(ny))
    order = (4 * np.arange(n_slab)[None, :] + np.arange(4)[:, None]).reshape(-1)
    line_mats = pair_const(deriv_matrix(nx)[np.ix_(order, order)])

    buf = start_call(
        ids, sound_speed, density, absorption, pressure_start, velocity_start, adjoint_velocity,
        emitter_voxel, emitter_delay, drive_waveform_samples, mats, ndev,
    )
    v0, u1y, u1z, yz0, gy0, gz0, cnt, m0, pm = prepare_call(
        ids, sound_speed, density, absorption, pressure_start, velocity_start, adjoint_pressure,
        sensor_flat_position.reshape(1, -1), recorded_pressures, emitter_voxel, emitter_delay,
        drive_waveform_samples, mats,
    )
    lines = change_layout(buf).reshape(n_emit, n_slab, 5, 8, nz)
    xs, gx0, gx1, ux, bk = forward_call(ids, lines, line_mats)
    xs = change_layout(xs.reshape(ndev, 2, 8, nz))
    qw, d0, t1, t2 = middle_call(
        ids, xs, sound_speed, density, absorption, adjoint_velocity,
        [v0, u1y, u1z, yz0, gy0, gz0, cnt, m0, pm], mats,
    )
    qw = change_layout(qw).reshape(n_emit, n_slab, 2, 8, nz)
    xs = adjoint_call(ids, qw, ux, bk, gx0, gx1, line_mats)
    xs = change_layout(xs.reshape(ndev, 24, nz // 2))
    bulk_part, p0 = last_bulk_call(ids, xs, d0, t1)
    other = swap_groups(bulk_part)
    buoy_part = last_buoy_call(ids, xs, p0, sound_speed, density, t2, gy0, gz0, mats)
    s1 = bulk_part + other
    s2 = buoy_part + swap_groups(buoy_part)
    b = 1.0 / density
    speed_total = (2.0 * DT) * s1 * density * sound_speed
    density_total = DT * (s1 * sound_speed * sound_speed + s2 * b * b)
    return speed_total, density_total


def solution(mesh):
    in_specs = (
        P("slab", None, None), P("slab", None, None), P("slab", None, None),
        P("emit", "slab", None, None), P("emit", None, "slab", None, None),
        P("emit", "slab", None, None), P("emit", None, "slab", None, None),
        P("emit", None), P("emit", None), P(), P("emit", None, None), P(),
    )
    out_specs = (P("slab", None, None), P("slab", None, None))
    return jax.shard_map(local, mesh=mesh, in_specs=in_specs, out_specs=out_specs, check_vma=False)
```

```python
import numpy as np
import jax
import jax.numpy as jnp
from jax import lax
from jax.experimental import pallas as pl
from jax.experimental.pallas import tpu as pltpu
from jax.sharding import PartitionSpec as P

STEPS = 2
DT = 0.2
F32 = jnp.float32
BF16 = jnp.bfloat16
ALL = ("emit", "slab")
MIB = 2**20
LIMIT = {"start": 60, "prepare": 60, "forward": 16, "middle": 14, "adjoint": 14, "last": 12}


def deriv_matrix(n):
    k = np.arange(1, n // 2, dtype=np.int64)
    pts = np.arange(n, dtype=np.int64)
    shifted = (k[None, :] * (2 * pts[:, None] + 1)) % (2 * n) * (np.pi / n)
    plain = (k[None, :] * (2 * pts[:, None])) % (2 * n) * (np.pi / n)
    w = k * (2.0 * np.pi / n)
    m = (np.cos(shifted) * w) @ np.sin(plain).T - (np.sin(shifted) * w) @ np.cos(plain).T
    return m * (2.0 / n)


def pair_const(m):
    m = m.astype(np.float32)
    return [jnp.asarray(m), jnp.asarray(np.ascontiguousarray(m.T))]


def split2(v):
    hi = v.astype(BF16)
    return hi, (v - hi.astype(F32)).astype(BF16)


def split3(v):
    hi = v.astype(BF16)
    rest = v - hi.astype(F32)
    mid = rest.astype(BF16)
    return hi, mid, (rest - mid.astype(F32)).astype(BF16)


def dot(a, b):
    return jnp.dot(a, b, preferred_element_type=F32)


def split_mats(gm, tm, ms):
    for k, m in enumerate((gm, tm)):
        ms[2 * k], ms[2 * k + 1] = split2(m[...])


G, T = 0, 2


def left(ms, k, v):
    h, l = split2(v)
    return dot(ms[k], h) + (dot(ms[k], l) + dot(ms[k + 1], h))


def right(v, ms, k):
    h, l = split2(v)
    return dot(h, ms[k]) + (dot(l, ms[k]) + dot(h, ms[k + 1]))


def mats_scratch(mats):
    return pltpu.VMEM((4,) + mats[0].shape, BF16)


def params(mib, n_grid=1):
    return pltpu.CompilerParams(
        dimension_semantics=("arbitrary",) * n_grid, vmem_limit_bytes=mib * MIB
    )


def cost(mflop, mib):
    return pl.CostEstimate(flops=mflop * 10**6, bytes_accessed=mib * MIB, transcendentals=0)


def swap(v):
    return jnp.swapaxes(v, 0, 1)


def whole(shape):
    return pl.BlockSpec(shape, lambda i, ids: (0,) * len(shape))


def group_plane(shape, pick, a=0):
    block = (None,) * (len(shape) - 3) + (1,) + shape[-2:]
    return pl.BlockSpec(block, lambda i, ids: (0, a)[: len(shape) - 3] + (pick(i, ids), 0, 0))


def plane_onehot(pos, plane, ny, nz):
    local = pos - plane * (ny * nz)
    y = lax.broadcasted_iota(jnp.int32, (ny, pos.shape[1]), 0) * nz
    return jnp.where((local >= y) & (local < y + nz), 1.0, 0.0).astype(BF16)


def column_onehot(pos, nz):
    z = lax.broadcasted_iota(jnp.int32, (nz, pos.shape[1]), 0)
    return lax.rem(pos, nz) == z


def drive_at(delay, drive, step):
    amp = jnp.zeros(delay.shape, F32)
    for k in range(drive.shape[0]):
        amp = jnp.where(delay + step == k, drive[k], amp)
    return amp


def three(onehot, value):
    return jnp.concatenate(
        [jnp.where(onehot, v.astype(F32), 0.0).astype(BF16) for v in split3(value)], axis=0
    )


def spread(rows, cols):
    return lax.dot_general(rows, cols, (((1,), (1,)), ((), ())), preferred_element_type=F32)


def sum3(v):
    n = v.shape[1] // 3
    return v[:, :n] + v[:, n : 2 * n] + v[:, 2 * n :]


def first_step(c, rho, alpha, p0, uy, uz, epos, cols, plane, ms):
    ny, nz = p0.shape[1], p0.shape[2]
    dens, speed, p = rho[0], c[0], p0[0]
    b = 1.0 / dens
    bulk = dens * speed * speed
    gy = left(ms, G, p)
    gz = right(p, ms, T)
    wy = uy[0] - DT * b * gy
    wz = uz[0] - DT * b * gz
    yz = left(ms, T, wy) + right(wz, ms, G)
    shot = sum3(spread(plane_onehot(epos[...], plane, ny, nz), cols[...]))
    v = (1.0 - DT * alpha[0]) * p + (DT * bulk) * yz + shot
    return gy, gz, wy, wz, yz, v, b, bulk


def start_kernel(
    ids, drive, c, rho, alpha, p0, ux, uy, uz, vx, epos, delay, gm, tm, buf, mat, cols, pack, ms
):
    i = pl.program_id(0)
    ny, nz = p0.shape[1], p0.shape[2]
    half = ny // 2

    @pl.when(i == 0)
    def _():
        split_mats(gm, tm, ms)
        cols[...] = three(column_onehot(epos[...], nz), drive_at(delay[...], drive, 0))

    @pl.when(i < 4)
    def _():
        _, _, _, _, _, v, b, bulk = first_step(
            c, rho, alpha, p0, uy, uz, epos, cols, ids[1] * 4 + i, ms
        )
        for f, field in enumerate((p0[0], ux[0], v, vx[0])):
            pack[2 * f : 2 * f + 2] = field.reshape(2, half, nz)
        buf[:, 0] = swap(pack[...])
        for xm in range(2):

            @pl.when(i == 2 * ids[0] + xm)
            def _():
                mat[4 * xm : 4 * xm + 2] = b.reshape(2, half, nz)
                mat[4 * xm + 2 : 4 * xm + 4] = bulk.reshape(2, half, nz)

    @pl.when(i == 4)
    def _():
        buf[:, 0] = swap(mat[...])


def start_call(ids, c, rho, alpha, p0, u, v, epos, delay, drive, mats, ndev):
    nx, ny, nz = c.shape
    pick = lambda i, ids: jnp.minimum(i, nx - 1)
    plane = group_plane(c.shape, pick)
    n_e = epos.shape[1]
    return pl.pallas_call(
        start_kernel,
        grid_spec=pltpu.PrefetchScalarGridSpec(
            num_scalar_prefetch=1,
            grid=(nx + 1,),
            in_specs=[pl.BlockSpec(memory_space=pltpu.SMEM)] + [plane] * 3
            + [group_plane(p0.shape, pick)]
            + [group_plane(u.shape, pick, a) for a in (0, 1, 2, 0)]
            + [whole((1, n_e))] * 2 + [whole((ny, ny))] * 2,
            out_specs=pl.BlockSpec((ndev, 1, 8, nz), lambda i, ids: (0, i, 0, 0)),
            scratch_shapes=[pltpu.VMEM((8, ndev, nz), F32), pltpu.VMEM((3 * nz, n_e), BF16),
                            pltpu.VMEM((8, ndev, nz), F32), mats_scratch(mats)],
        ),
        out_shape=jax.ShapeDtypeStruct((ndev, 5, 8, nz), F32),
        compiler_params=params(LIMIT["start"]),
        cost_estimate=cost(2000, 13),
        name="start",
    )(ids, drive, c, rho, alpha, p0, u, u, u, v, epos, delay, *mats)


def prepare_kernel(
    ids, drive, c, rho, alpha, p0, uy, uz, pa, ay, az, spos, rec, epos, delay, gm, tm,
    dk, stay, b, pm, cdk, wb, yz1, yz0, gsy, gsz, gy0, gz0, scols, ecols, ms,
):
    i = pl.program_id(0)
    ny, nz = c.shape[1], c.shape[2]

    @pl.when(i == 0)
    def _():
        split_mats(gm, tm, ms)
        oh = column_onehot(spos[...], nz)
        scols[:nz] = jnp.where(oh, 1.0, 0.0).astype(BF16)
        scols[nz : 4 * nz] = three(oh, rec[0:1])
        scols[4 * nz :] = three(oh, rec[1:2])
        for step in range(STEPS):
            ecols[step] = three(column_onehot(epos[...], nz), drive_at(delay[...], drive, step))

    plane = ids[1] * 4 + i
    gy, gz, u1y, u1z, yz0[0], v0, buoy, bulk = first_step(
        c, rho, alpha, p0, uy, uz, epos, ecols.at[0], plane, ms
    )
    keep = 1.0 - DT * alpha[0]
    s = plane_onehot(spos[...], plane, ny, nz)
    count = spread(s, scols[:nz])
    m0 = sum3(spread(s, scols[nz : 4 * nz]))
    m1 = sum3(spread(s, scols[4 * nz :]))
    shot = sum3(spread(plane_onehot(epos[...], plane, ny, nz), ecols[1]))
    gyv = left(ms, G, v0)
    gzv = right(v0, ms, T)
    db = DT * buoy
    yz = left(ms, T, u1y - db * gyv) + right(u1z - db * gzv, ms, G)
    back = left(ms, T, buoy * ay[0]) + right(buoy * az[0], ms, G)
    dk[0] = DT * bulk
    stay[0] = keep
    b[0] = buoy
    cdk[0] = count * (DT * bulk)
    pm[0] = pa[0] + (count * (keep * v0 + (DT * bulk) * yz + shot) - m1)
    wb[0] = (count * v0 - m0) - DT * back
    yz1[0] = yz
    gsy[0] = gy + gyv
    gsz[0] = gz + gzv
    gy0[0] = gy
    gz0[0] = gz


def prepare_call(ids, c, rho, alpha, p0, u, pa, v, spos, rec, epos, delay, drive, mats):
    nx, ny, nz = c.shape
    n_e, n_s = epos.shape[1], spos.shape[1]
    pick = lambda i, ids: i
    plane = group_plane(c.shape, pick)
    return pl.pallas_call(
        prepare_kernel,
        grid_spec=pltpu.PrefetchScalarGridSpec(
            num_scalar_prefetch=1,
            grid=(nx,),
            in_specs=[pl.BlockSpec(memory_space=pltpu.SMEM)] + [plane] * 3
            + [group_plane(p0.shape, pick)] + [group_plane(u.shape, pick, a) for a in (1, 2)]
            + [group_plane(pa.shape, pick)] + [group_plane(v.shape, pick, a) for a in (1, 2)]
            + [whole((1, n_s)), pl.BlockSpec((None, STEPS, n_s), lambda i, ids: (0, 0, 0)),
               whole((1, n_e)), whole((1, n_e))] + [whole((ny, ny))] * 2,
            out_specs=[plane] * 12,
            scratch_shapes=[pltpu.VMEM((7 * nz, n_s), BF16), pltpu.VMEM((STEPS, 3 * nz, n_e), BF16),
                            mats_scratch(mats)],
        ),
        out_shape=[jax.ShapeDtypeStruct(c.shape, F32)] * 12,
        compiler_params=params(LIMIT["prepare"]),
        cost_estimate=cost(8000, 22),
        name="prepare",
    )(ids, drive, c, rho, alpha, p0, u, u, pa, v, v, spos, rec, epos, delay, *mats)


def on_chip(kernel, args, shapes, scratch, limit, estimate, name, away=0):
    vmem = pl.BlockSpec(memory_space=pltpu.VMEM)
    return pl.pallas_call(
        kernel,
        in_specs=[pl.BlockSpec(memory_space=pl.ANY)] * away + [vmem] * (len(args) - away),
        out_specs=[vmem] * len(shapes),
        out_shape=[jax.ShapeDtypeStruct(v, F32) for v in shapes],
        scratch_shapes=[pltpu.VMEM(v, F32) for v in scratch] + [mats_scratch(args[-2:])],
        compiler_params=pltpu.CompilerParams(vmem_limit_bytes=limit * MIB),
        cost_estimate=estimate,
        name=name,
    )(*args)


def unpack(block, dst, first):
    t = swap(block)
    n = t.shape[1]
    for xm in range(2):
        dst[:, (first + xm) * n : (first + xm + 1) * n, :] = t[4 * xm : 4 * xm + 4]


def forward_kernel(ready, lines, gm, tm, out, gx0, gx1, ax, bk, f_s, o_s, ms):
    n = lines.shape[1]
    split_mats(gm, tm, ms)
    for e in range(2):
        unpack(lines[e, :, 4], bk, 2 * e)

    @pl.loop(0, 2)
    def _(g):
        for xl in range(4):
            rows = slice(xl * n, (xl + 1) * n)
            t = swap(lines[g, :, xl])
            f_s[g, :, rows, :] = t[:6]
            ax[pl.ds(2 * g, 2), rows, :] = t[6:]

    @pl.loop(0, 4)
    def _(j):
        g, yl = j // 2, lax.rem(j, 2)
        b = DT * bk[yl]
        g0 = left(ms, G, f_s[g, yl])
        u1 = f_s[g, 2 + yl] - b * g0
        x0 = left(ms, T, u1)
        g1 = left(ms, G, f_s[g, 4 + yl] + (DT * bk[2 + yl]) * x0)
        gx0[j] = g0
        gx1[j] = g1
        o_s[g, yl] = x0
        o_s[g, 2 + yl] = left(ms, T, u1 - b * g1)

    @pl.loop(0, 2)
    def _(g):
        for h in range(2):
            both = [o_s[g, :, (2 * h + xm) * n : (2 * h + xm + 1) * n, :] for xm in range(2)]
            out[g, :, h] = swap(jnp.concatenate(both, axis=0))


def forward_call(ready, lines, mats):
    _, ns, _, _, nz = lines.shape
    nx = 4 * ns
    full = (4, nx, nz)
    return on_chip(
        forward_kernel, (ready, lines, *mats), [(2, ns, 2, 8, nz), full, full, full, full],
        [(2, 6, nx, nz), (2, 4, nx, nz)], LIMIT["forward"], cost(1600, 11), "lines_forward", 1,
    )


def middle_kernel(
    xs, dk, stay, b, pm, cdk, wb, yz1, yz0, gsy, gsz, v, gm, tm, buf, d0, t1, t2, x_s, o_s, ms
):
    nx, ny, nz = dk.shape
    split_mats(gm, tm, ms)
    for h in range(2):
        x_s[4 * h : 4 * h + 4] = swap(xs[:, h]).reshape(4, ny, nz)

    @pl.loop(0, nx)
    def _(i):
        x0 = x_s[2 * i]
        add = dk[i] * x0
        ey = left(ms, G, add)
        ez = right(add, ms, T)
        db = DT * b[i]
        rest = x_s[2 * i + 1] - (left(ms, T, db * ey) + right(db * ez, ms, G))
        adj = pm[i] + cdk[i] * (stay[i] * x0 + rest)
        q = dk[i] * adj
        fy = left(ms, G, q)
        fz = right(q, ms, T)
        back = left(ms, T, b[i] * fy) + right(b[i] * fz, ms, G)
        o_s[2 * i] = q
        o_s[2 * i + 1] = stay[i] * adj + (cdk[i] * x0 + wb[i]) - DT * back
        d0[i] = x0 + yz0[i]
        t1[i] = (yz1[i] + rest) * adj
        t2[i] = (gsy[i] + ey) * (v[0, 1, i] + fy) + (gsz[i] + ez) * (v[0, 2, i] + fz)

    for h in range(2):
        buf[:, h] = swap(o_s[4 * h : 4 * h + 4].reshape(8, ny // 2, nz))


def middle_call(xs, fields, v, mats):
    nat = fields[0].shape
    saved = (8,) + nat[1:]
    return on_chip(
        middle_kernel, (xs, *fields, v, *mats), [xs.shape, nat, nat, nat], [saved, saved],
        LIMIT["middle"], cost(3200, 18), "slab_middle",
    )


def adjoint_kernel(qw, ux, bk, gx0, gx1, gm, tm, out, f_s, p_s, bx_s, ms):
    split_mats(gm, tm, ms)
    n, nz = qw.shape[1], qw.shape[4]
    lanes = [slice(0, nz // 2), slice(nz // 2, nz)]

    @pl.loop(0, 2)
    def _(g):
        for h in range(2):
            unpack(qw[g, :, h], f_s.at[g], 2 * h)

    bx_s[...] = jnp.zeros_like(bx_s)

    @pl.loop(0, 4)
    def _(j):
        g, yl = j // 2, lax.rem(j, 2)
        ax = ux[j] + left(ms, G, f_s[g, yl])
        p0 = f_s[g, 2 + yl] - DT * left(ms, T, bk[yl] * ax)
        p_s[j] = p0
        bx_s[yl] += gx1[j] * ax + gx0[j] * (ax + left(ms, G, (DT * bk[2 + yl]) * p0))

    @pl.loop(0, 2)
    def _(g):
        for zh, z in enumerate(lanes):
            v = [p_s[pl.ds(2 * g, 2), xl * n : (xl + 1) * n, z] for xl in range(4)]
            out[g, :, 8 * zh : 8 * zh + 8, :] = swap(jnp.concatenate(v, axis=0))

    for e in range(2):
        v = [bx_s[:, (2 * e + xm) * n : (2 * e + xm + 1) * n, z] for z in lanes for xm in range(2)]
        out[e, :, 16:24, :] = swap(jnp.concatenate(v, axis=0))


def adjoint_call(qw, ux, bk, gx0, gx1, mats):
    _, ns, _, _, nz = qw.shape
    nx = 4 * ns
    return on_chip(
        adjoint_kernel, (qw, ux, bk, gx0, gx1, *mats), [(2, ns, 24, nz // 2)],
        [(2, 4, nx, nz), (4, nx, nz), (2, nx, nz)], LIMIT["adjoint"], cost(1200, 9), "lines_adjoint",
    )[0]


def last_kernel(ids, xs, d0, t1, t2, gy0, gz0, dk, gm, tm, out, p_s, bx_s, ms):
    split_mats(gm, tm, ms)
    nx, ny, nz = d0.shape
    half = nz // 2
    t = swap(xs[:, 16:24, :]).reshape(4, ny, half)
    for zh in range(2):
        z = slice(zh * half, (zh + 1) * half)
        p_s[:, :, z] = swap(xs[:, 8 * zh : 8 * zh + 8, :]).reshape(nx, ny, half)
        bx_s[:, :, z] = t[2 * zh : 2 * zh + 2]

    @pl.loop(0, nx)
    def _(i):
        p = p_s[i]
        q = dk[i] * p
        out[0, i] = t1[i] + d0[i] * p
        out[1, i] = t2[i] + gy0[i] * left(ms, G, q) + gz0[i] * right(q, ms, T)

    for xm in range(2):
        out[1, 2 * ids[0] + xm] += bx_s[xm]


def last_call(ids, xs, fields, mats):
    nat = fields[0].shape
    vmem = pl.BlockSpec(memory_space=pltpu.VMEM)
    args = (xs, *fields, *mats)
    return pl.pallas_call(
        last_kernel,
        in_specs=[pl.BlockSpec(memory_space=pltpu.SMEM)] + [vmem] * len(args),
        out_specs=vmem,
        out_shape=jax.ShapeDtypeStruct((2,) + nat, F32),
        scratch_shapes=[pltpu.VMEM(nat, F32), pltpu.VMEM((2,) + nat[1:], F32), mats_scratch(mats)],
        compiler_params=pltpu.CompilerParams(vmem_limit_bytes=LIMIT["last"] * MIB),
        cost_estimate=cost(800, 9),
        name="slab_last",
    )(ids, *args)


def change_layout(v):
    return lax.all_to_all(v, ALL, split_axis=0, concat_axis=0, tiled=True)


def swap_groups(v):
    return lax.ppermute(v, "emit", [(0, 1), (1, 0)])


def local(
    sound_speed, density, absorption, pressure_start, velocity_start, adjoint_pressure,
    adjoint_velocity, emitter_voxel, emitter_delay, drive_waveform_samples, recorded_pressures,
    sensor_flat_position,
):
    n_emit, n_slab = lax.axis_size("emit"), lax.axis_size("slab")
    ndev = n_emit * n_slab
    planes, ny, nz = sound_speed.shape
    nx = planes * n_slab
    emit = lax.axis_index("emit")
    ids = jnp.stack([emit, lax.axis_index("slab")]).astype(jnp.int32)
    mats = pair_const(deriv_matrix(ny))
    order = (4 * np.arange(n_slab)[None, :] + np.arange(4)[:, None]).reshape(-1)
    line_mats = pair_const(deriv_matrix(nx)[np.ix_(order, order)])

    buf = start_call(
        ids, sound_speed, density, absorption, pressure_start, velocity_start, adjoint_velocity,
        emitter_voxel, emitter_delay, drive_waveform_samples, mats, ndev,
    )
    fields = prepare_call(
        ids, sound_speed, density, absorption, pressure_start, velocity_start, adjoint_pressure,
        adjoint_velocity, sensor_flat_position.reshape(1, -1), recorded_pressures, emitter_voxel,
        emitter_delay, drive_waveform_samples, mats,
    )
    gy0, gz0, dk = fields[10], fields[11], fields[0]
    lines = change_layout(buf).reshape(n_emit, n_slab, 5, 8, nz)
    xs, gx0, gx1, ux, bk = forward_call(dk, lines, line_mats)
    xs = change_layout(xs.reshape(ndev, 2, 8, nz))
    qw, d0, t1, t2 = middle_call(xs, fields[:10], adjoint_velocity, mats)
    qw = change_layout(qw).reshape(n_emit, n_slab, 2, 8, nz)
    xs = adjoint_call(qw, ux, bk, gx0, gx1, line_mats)
    xs = change_layout(xs.reshape(ndev, 24, nz // 2))
    t = last_call(ids, xs, [d0, t1, t2, gy0, gz0, dk], mats)
    other = swap_groups(t)
    s1, s2 = t[0] + other[0], t[1] + other[1]
    b = 1.0 / density
    speed_total = (2.0 * DT) * s1 * density * sound_speed
    density_total = DT * (s1 * sound_speed * sound_speed + s2 * b * b)
    return speed_total, density_total


def solution(mesh):
    in_specs = (
        P("slab", None, None), P("slab", None, None), P("slab", None, None),
        P("emit", "slab", None, None), P("emit", None, "slab", None, None),
        P("emit", "slab", None, None), P("emit", None, "slab", None, None),
        P("emit", None), P("emit", None), P(), P("emit", None, None), P(),
    )
    out_specs = (P("slab", None, None), P("slab", None, None))
    return jax.shard_map(local, mesh=mesh, in_specs=in_specs, out_specs=out_specs, check_vma=False)
```

```python
import numpy as np
import jax
import jax.numpy as jnp
from jax import lax
from jax.experimental import pallas as pl
from jax.experimental.pallas import tpu as pltpu
from jax.sharding import PartitionSpec as P

STEPS = 2
DT = 0.2
F32 = jnp.float32
BF16 = jnp.bfloat16
ALL = ("emit", "slab")
MIB = 2**20
LIMIT = {"start": 60, "prepare": 60, "forward": 24, "middle": 40, "adjoint": 20, "last": 20}


def deriv_matrix(n):
    k = np.arange(1, n // 2, dtype=np.int64)
    pts = np.arange(n, dtype=np.int64)
    shifted = (k[None, :] * (2 * pts[:, None] + 1)) % (2 * n) * (np.pi / n)
    plain = (k[None, :] * (2 * pts[:, None])) % (2 * n) * (np.pi / n)
    w = k * (2.0 * np.pi / n)
    m = (np.cos(shifted) * w) @ np.sin(plain).T - (np.sin(shifted) * w) @ np.cos(plain).T
    return m * (2.0 / n)


def pair_const(m):
    m = m.astype(np.float32)
    return [jnp.asarray(m), jnp.asarray(np.ascontiguousarray(m.T))]


def split2(v):
    hi = v.astype(BF16)
    return hi, (v - hi.astype(F32)).astype(BF16)


def split3(v):
    hi = v.astype(BF16)
    rest = v - hi.astype(F32)
    mid = rest.astype(BF16)
    return hi, mid, (rest - mid.astype(F32)).astype(BF16)


def dot(a, b):
    return jnp.dot(a, b, preferred_element_type=F32)


def split_mats(gm, tm, ms):
    for k, m in enumerate((gm, tm)):
        ms[2 * k], ms[2 * k + 1] = split2(m[...])


G, T = 0, 2


def left(ms, k, v):
    h, l = split2(v)
    return dot(ms[k], h) + (dot(ms[k], l) + dot(ms[k + 1], h))


def right(v, ms, k):
    h, l = split2(v)
    return dot(h, ms[k]) + (dot(l, ms[k]) + dot(h, ms[k + 1]))


def mats_scratch(mats):
    return pltpu.VMEM((4,) + mats[0].shape, BF16)


def params(mib, n_grid=1):
    return pltpu.CompilerParams(
        dimension_semantics=("arbitrary",) * n_grid, vmem_limit_bytes=mib * MIB
    )


def cost(mflop, mib):
    return pl.CostEstimate(flops=mflop * 10**6, bytes_accessed=mib * MIB, transcendentals=0)


def swap(v):
    return jnp.swapaxes(v, 0, 1)


def whole(shape):
    return pl.BlockSpec(shape, lambda i, ids: (0,) * len(shape))


def group_plane(shape, pick, a=0):
    block = (None,) * (len(shape) - 3) + (1,) + shape[-2:]
    return pl.BlockSpec(block, lambda i, ids: (0, a)[: len(shape) - 3] + (pick(i, ids), 0, 0))


def plane_onehot(pos, plane, ny, nz):
    local = pos - plane * (ny * nz)
    y = lax.broadcasted_iota(jnp.int32, (ny, pos.shape[1]), 0) * nz
    return jnp.where((local >= y) & (local < y + nz), 1.0, 0.0).astype(BF16)


def column_onehot(pos, nz):
    z = lax.broadcasted_iota(jnp.int32, (nz, pos.shape[1]), 0)
    return lax.rem(pos, nz) == z


def drive_at(delay, drive, step):
    amp = jnp.zeros(delay.shape, F32)
    for k in range(drive.shape[0]):
        amp = jnp.where(delay + step == k, drive[k], amp)
    return amp


def three(onehot, value):
    parts = [jnp.where(onehot, v.astype(F32), 0.0) for v in split3(value)]
    return jnp.concatenate(parts, axis=1).T.astype(BF16)


def spread(rows, cols):
    return dot(jnp.concatenate([rows] * 3, axis=1), cols)


def first_step(planes, cols, epos, numbers, ms):
    ny, nz = planes[0][0].shape
    c, rho, alpha, p, uy, uz = zip(*planes)
    at = range(len(planes))
    gy = [left(ms, G, v) for v in p]
    gz = [right(v, ms, T) for v in p]
    b = [1.0 / v for v in rho]
    bulk = [rho[k] * c[k] * c[k] for k in at]
    wy = [uy[k] - DT * b[k] * gy[k] for k in at]
    wz = [uz[k] - DT * b[k] * gz[k] for k in at]
    yz = [left(ms, T, v) for v in wy]
    zz = [right(v, ms, G) for v in wz]
    shot = [spread(plane_onehot(epos[...], n, ny, nz), cols[...]) for n in numbers]
    yz = [yz[k] + zz[k] for k in at]
    v0 = [(1.0 - DT * alpha[k]) * p[k] + (DT * bulk[k]) * yz[k] + shot[k] for k in at]
    return list(zip(gy, gz, wy, wz, yz, v0, b, bulk))


def plane_copies(srcs, dst, sems, i):
    return [
        pltpu.make_async_copy(src.at[pl.ds(i, 1)], dst.at[i, pl.ds(k, 1)], sems.at[i, k])
        for k, src in enumerate(srcs)
    ]


def start_kernel(
    drive, c, rho, alpha, p0, u, v, epos, delay, gm, tm, buf, ins, sems, outs, out_sems, mat, cols,
    pack, ms
):
    emit, slab = lax.axis_index("emit"), lax.axis_index("slab")
    nx, ny, nz = c.shape
    half = ny // 2

    def send(i):
        return pltpu.make_async_copy(outs.at[i], buf.at[:, i], out_sems.at[i])

    srcs = (p0.at[0], c, rho, alpha, u.at[0, 1], u.at[0, 2], u.at[0, 0], v.at[0, 0])
    for i in range(nx):
        for copy in plane_copies(srcs, ins, sems, i):
            copy.start()
    split_mats(gm, tm, ms)
    cols[...] = three(column_onehot(epos[...], nz), drive_at(delay[...], drive, 0))

    @pl.loop(0, nx // 2)
    def _(k):
        pair = (2 * k, 2 * k + 1)
        for i in pair:
            for copy in plane_copies(srcs, ins, sems, i):
                copy.wait()
        steps = first_step(
            [tuple(ins[i, f] for f in (1, 2, 3, 0, 4, 5)) for i in pair],
            cols, epos, [slab * nx + i for i in pair], ms,
        )
        for xm, i in enumerate(pair):
            v0, b, bulk = steps[xm][5:]
            for f, field in enumerate((ins[i, 0], ins[i, 6], v0, ins[i, 7])):
                pack[xm, 2 * f : 2 * f + 2] = field.reshape(2, half, nz)
            outs[i] = swap(pack[xm])
            send(i).start()

            @pl.when(k == emit)
            def _():
                mat[4 * xm : 4 * xm + 2] = b.reshape(2, half, nz)
                mat[4 * xm + 2 : 4 * xm + 4] = bulk.reshape(2, half, nz)

    outs[nx] = swap(mat[...])
    send(nx).start()
    for i in range(nx + 1):
        send(i).wait()


def start_call(c, rho, alpha, p0, u, v, epos, delay, drive, mats, ndev):
    nx, ny, nz = c.shape
    n_e = epos.shape[1]
    hbm, vmem, smem = (pl.BlockSpec(memory_space=m) for m in (pltpu.HBM, pltpu.VMEM, pltpu.SMEM))
    return pl.pallas_call(
        start_kernel,
        in_specs=[smem] + [hbm] * 6 + [vmem] * 4,
        out_specs=hbm,
        out_shape=jax.ShapeDtypeStruct((ndev, nx + 1, 8, nz), F32),
        scratch_shapes=[pltpu.VMEM((nx, 8, ny, nz), F32), pltpu.SemaphoreType.DMA((nx, 8)),
                        pltpu.VMEM((nx + 1, ndev, 8, nz), F32), pltpu.SemaphoreType.DMA((nx + 1,)),
                        pltpu.VMEM((8, ndev, nz), F32), pltpu.VMEM((3 * n_e, nz), BF16),
                        pltpu.VMEM((2, 8, ndev, nz), F32), mats_scratch(mats)],
        compiler_params=pltpu.CompilerParams(vmem_limit_bytes=LIMIT["start"] * MIB),
        cost_estimate=cost(2000, 13),
        name="start",
    )(drive, c, rho, alpha, p0, u, v, epos, delay, *mats)


def prepare_kernel(
    ids, drive, c, rho, alpha, p0, uy, uz, pa, ay, az, spos, rec, epos, delay, gm, tm,
    dk, stay, b, pm, cdk, wb, yz1, late, gy0, gz0, ones, scols, ecols, ms,
):
    i = pl.program_id(0)
    ny, nz = c.shape[1], c.shape[2]

    @pl.when(i == 0)
    def _():
        split_mats(gm, tm, ms)
        oh = column_onehot(spos[...], nz)
        ones[...] = jnp.where(oh, 1.0, 0.0).T.astype(BF16)
        for step in range(STEPS):
            scols[step] = three(oh, rec[step : step + 1])
        for step in range(STEPS):
            ecols[step] = three(column_onehot(epos[...], nz), drive_at(delay[...], drive, step))

    plane = ids[1] * 4 + i
    gy, gz, u1y, u1z, yz0, v0, buoy, bulk = first_step(
        [(c[0], rho[0], alpha[0], p0[0], uy[0], uz[0])], ecols.at[0], epos, [plane], ms
    )[0]
    keep = 1.0 - DT * alpha[0]
    s = plane_onehot(spos[...], plane, ny, nz)
    count = dot(s, ones[...])
    m0 = spread(s, scols[0])
    m1 = spread(s, scols[1])
    shot = spread(plane_onehot(epos[...], plane, ny, nz), ecols[1])
    gyv = left(ms, G, v0)
    gzv = right(v0, ms, T)
    db = DT * buoy
    yz = left(ms, T, u1y - db * gyv) + right(u1z - db * gzv, ms, G)
    back = left(ms, T, buoy * ay[0]) + right(buoy * az[0], ms, G)
    dk[0] = DT * bulk
    stay[0] = keep
    b[0] = buoy
    cdk[0] = count * (DT * bulk)
    pm[0] = pa[0] + (count * (keep * v0 + (DT * bulk) * yz + shot) - m1)
    wb[0] = (count * v0 - m0) - DT * back
    yz1[0] = yz
    for k, field in enumerate((yz0, gy + gyv, gz + gzv, ay[0], az[0])):
        late[0, k] = field
    gy0[0] = gy
    gz0[0] = gz


def prepare_call(
    ids, c, rho, alpha, p0, u, pa, v, spos, rec, epos, delay, drive, mats
):
    nx, ny, nz = c.shape
    n_e, n_s = epos.shape[1], spos.shape[1]
    pick = lambda i, ids: i
    plane = group_plane(c.shape, pick)
    return pl.pallas_call(
        prepare_kernel,
        grid_spec=pltpu.PrefetchScalarGridSpec(
            num_scalar_prefetch=1,
            grid=(nx,),
            in_specs=[pl.BlockSpec(memory_space=pltpu.SMEM)] + [plane] * 3
            + [group_plane(p0.shape, pick)] + [group_plane(u.shape, pick, a) for a in (1, 2)]
            + [group_plane(pa.shape, pick)] + [group_plane(v.shape, pick, a) for a in (1, 2)]
            + [whole((1, n_s)), pl.BlockSpec((None, STEPS, n_s), lambda i, ids: (0, 0, 0)),
               whole((1, n_e)), whole((1, n_e))]
            + [whole((ny, ny))] * 2,
            out_specs=[plane] * 7 + [pl.BlockSpec((1, 5, ny, nz), lambda i, ids: (i, 0, 0, 0))]
            + [plane] * 2,
            scratch_shapes=[pltpu.VMEM((n_s, nz), BF16), pltpu.VMEM((STEPS, 3 * n_s, nz), BF16),
                            pltpu.VMEM((STEPS, 3 * n_e, nz), BF16), mats_scratch(mats)],
        ),
        out_shape=[jax.ShapeDtypeStruct(c.shape, F32)] * 7
        + [jax.ShapeDtypeStruct((nx, 5, ny, nz), F32)] + [jax.ShapeDtypeStruct(c.shape, F32)] * 2,
        compiler_params=params(LIMIT["prepare"]),
        cost_estimate=cost(8000, 22),
        name="prepare",
    )(ids, drive, c, rho, alpha, p0, u, u, pa, v, v, spos, rec, epos, delay, *mats)


def on_chip(kernel, away, args, shapes, scratch, limit, estimate, name):
    vmem = pl.BlockSpec(memory_space=pltpu.VMEM)
    return pl.pallas_call(
        kernel,
        in_specs=[pl.BlockSpec(memory_space=pltpu.HBM)] * len(away) + [vmem] * len(args),
        out_specs=[vmem] * len(shapes),
        out_shape=[jax.ShapeDtypeStruct(v, F32) for v in shapes],
        scratch_shapes=[pltpu.VMEM(v, F32) if isinstance(v, tuple) else v for v in scratch]
        + [mats_scratch(args[-2:])],
        compiler_params=pltpu.CompilerParams(vmem_limit_bytes=limit * MIB),
        cost_estimate=estimate,
        name=name,
    )(*away, *args)


def unpack(block, dst, first):
    t = swap(block)
    n = t.shape[1]
    for xm in range(2):
        dst[:, (first + xm) * n : (first + xm + 1) * n, :] = t[4 * xm : 4 * xm + 4]


def forward_kernel(lines, gm, tm, out, gx0, gx1, ax, bk, in_s, mat_s, sems, f_s, o_s, ms):
    n = lines.shape[1]
    copies = [pltpu.make_async_copy(lines.at[:, :, 4], mat_s, sems.at[0])] + [
        pltpu.make_async_copy(lines.at[g, :, pl.ds(0, 4)], in_s.at[g], sems.at[1 + g]) for g in range(2)
    ]
    for copy in copies:
        copy.start()
    split_mats(gm, tm, ms)
    copies[0].wait()
    for e in range(2):
        unpack(mat_s[e], bk, 2 * e)

    @pl.loop(0, 2)
    def _(g):
        pltpu.make_async_copy(lines.at[g, :, pl.ds(0, 4)], in_s.at[g], sems.at[1 + g]).wait()
        for xl in range(4):
            rows = slice(xl * n, (xl + 1) * n)
            t = swap(in_s[g, :, xl])
            f_s[:, rows, :] = t[:6]
            ax[pl.ds(2 * g, 2), rows, :] = t[6:]
        rows = range(2)
        g0 = [left(ms, G, f_s[yl]) for yl in rows]
        u1 = [f_s[2 + yl] - (DT * bk[yl]) * g0[yl] for yl in rows]
        x0 = [left(ms, T, u1[yl]) for yl in rows]
        p1 = [f_s[4 + yl] + (DT * bk[2 + yl]) * x0[yl] for yl in rows]
        g1 = [left(ms, G, p1[yl]) for yl in rows]
        x1 = [left(ms, T, u1[yl] - (DT * bk[yl]) * g1[yl]) for yl in rows]
        for yl in rows:
            gx0[2 * g + yl] = g0[yl]
            gx1[2 * g + yl] = g1[yl]
            o_s[yl] = x0[yl]
            o_s[2 + yl] = x1[yl]
        for h in range(2):
            both = [o_s[:, (2 * h + xm) * n : (2 * h + xm + 1) * n, :] for xm in range(2)]
            out[g, :, h] = swap(jnp.concatenate(both, axis=0))


def forward_call(lines, mats):
    _, ns, _, _, nz = lines.shape
    nx = 4 * ns
    full = (4, nx, nz)
    return on_chip(
        forward_kernel, (lines,), mats, [(2, ns, 2, 8, nz), full, full, full, full],
        [(2, ns, 4, 8, nz), (2, ns, 8, nz), pltpu.SemaphoreType.DMA((3,)), (6, nx, nz), (4, nx, nz)],
        LIMIT["forward"], cost(1600, 11), "lines_forward",
    )


def middle_kernel(
    late, xs, dk, stay, b, pm, cdk, wb, yz1, gm, tm,
    buf, d0, t1, t2, x_s, o_s, ins, sems, ms,
):
    nx, ny, nz = dk.shape
    fetch = lambda i: pltpu.make_async_copy(late.at[i], ins.at[i], sems.at[i])
    for i in range(nx):
        fetch(i).start()
    split_mats(gm, tm, ms)
    for h in range(2):
        x_s[4 * h : 4 * h + 4] = swap(xs[:, h]).reshape(4, ny, nz)

    def some(planes):
        add = [dk[i] * x_s[2 * i] for i in planes]
        ey = [left(ms, G, a) for a in add]
        ez = [right(a, ms, T) for a in add]
        gy = [left(ms, T, (DT * b[i]) * e) for i, e in zip(planes, ey)]
        gz = [right((DT * b[i]) * e, ms, G) for i, e in zip(planes, ez)]
        rest = [x_s[2 * i + 1] - (e + f) for i, e, f in zip(planes, gy, gz)]
        adj = [pm[i] + cdk[i] * (stay[i] * x_s[2 * i] + r) for i, r in zip(planes, rest)]
        q = [dk[i] * a for i, a in zip(planes, adj)]
        fy = [left(ms, G, a) for a in q]
        fz = [right(a, ms, T) for a in q]
        for k, i in enumerate(planes):
            o_s[2 * i] = q[k]
            t1[i] = (yz1[i] + rest[k]) * adj[k]
        gy = [left(ms, T, b[i] * e) for i, e in zip(planes, fy)]
        gz = [right(b[i] * e, ms, G) for i, e in zip(planes, fz)]
        for k, i in enumerate(planes):
            o_s[2 * i + 1] = stay[i] * adj[k] + (cdk[i] * x_s[2 * i] + wb[i]) - DT * (gy[k] + gz[k])
            fetch(i).wait()
            d0[i] = x_s[2 * i] + ins[i, 0]
            t2[i] = (ins[i, 1] + ey[k]) * (ins[i, 3] + fy[k]) + (ins[i, 2] + ez[k]) * (ins[i, 4] + fz[k])

    some(range(nx))

    for h in range(2):
        buf[:, h] = swap(o_s[4 * h : 4 * h + 4].reshape(8, ny // 2, nz))


def middle_call(xs, fields, mats):
    nat = fields[0].shape
    saved = (8,) + nat[1:]
    return on_chip(
        middle_kernel, (fields[7],), (xs, *fields[:7], *mats), [xs.shape, nat, nat, nat],
        [saved, saved, (nat[0], 5) + nat[1:], pltpu.SemaphoreType.DMA((nat[0],))],
        LIMIT["middle"], cost(3200, 18), "slab_middle",
    )


def adjoint_kernel(qw, ux, bk, gx0, gx1, gm, tm, out, f_s, p_s, bx_s, ms):
    split_mats(gm, tm, ms)
    n, nz = qw.shape[1], qw.shape[4]
    lanes = [slice(0, nz // 2), slice(nz // 2, nz)]

    @pl.loop(0, 2)
    def _(g):
        for h in range(2):
            unpack(qw[g, :, h], f_s.at[g], 2 * h)

    at = [(g, yl) for g in range(2) for yl in range(2)]
    ax = [left(ms, G, f_s[g, yl]) for g, yl in at]
    ax = [ux[j] + v for j, v in enumerate(ax)]
    back = [left(ms, T, bk[yl] * v) for (g, yl), v in zip(at, ax)]
    p0 = [f_s[g, 2 + yl] - DT * v for (g, yl), v in zip(at, back)]
    gq = [left(ms, G, (DT * bk[2 + yl]) * v) for (g, yl), v in zip(at, p0)]
    bx = [gx1[j] * ax[j] + gx0[j] * (ax[j] + gq[j]) for j in range(4)]
    for j in range(4):
        p_s[j] = p0[j]
    for yl in range(2):
        bx_s[yl] = bx[yl] + bx[2 + yl]

    @pl.loop(0, 2)
    def _(g):
        for zh, z in enumerate(lanes):
            v = [p_s[pl.ds(2 * g, 2), xl * n : (xl + 1) * n, z] for xl in range(4)]
            out[g, :, 8 * zh : 8 * zh + 8, :] = swap(jnp.concatenate(v, axis=0))

    for e in range(2):
        v = [bx_s[:, (2 * e + xm) * n : (2 * e + xm + 1) * n, z] for z in lanes for xm in range(2)]
        out[e, :, 16:24, :] = swap(jnp.concatenate(v, axis=0))


def adjoint_call(qw, ux, bk, gx0, gx1, mats):
    _, ns, _, _, nz = qw.shape
    nx = 4 * ns
    return on_chip(
        adjoint_kernel, (), (qw, ux, bk, gx0, gx1, *mats), [(2, ns, 24, nz // 2)],
        [(2, 4, nx, nz), (4, nx, nz), (2, nx, nz)], LIMIT["adjoint"], cost(1200, 9), "lines_adjoint",
    )[0]


def last_kernel(ids, xs, d0, t1, t2, gy0, gz0, dk, gm, tm, out, p_s, bx_s, ms):
    split_mats(gm, tm, ms)
    nx, ny, nz = d0.shape
    half = nz // 2
    t = swap(xs[:, 16:24, :]).reshape(4, ny, half)
    for zh in range(2):
        z = slice(zh * half, (zh + 1) * half)
        p_s[:, :, z] = swap(xs[:, 8 * zh : 8 * zh + 8, :]).reshape(nx, ny, half)
        bx_s[:, :, z] = t[2 * zh : 2 * zh + 2]

    q = [dk[i] * p_s[i] for i in range(nx)]
    gy = [left(ms, G, v) for v in q]
    gz = [right(v, ms, T) for v in q]
    for i in range(nx):
        out[0, i] = t1[i] + d0[i] * p_s[i]
        out[1, i] = t2[i] + gy0[i] * gy[i] + gz0[i] * gz[i]

    for xm in range(2):
        out[1, 2 * ids[0] + xm] += bx_s[xm]


def last_call(ids, xs, fields, mats):
    nat = fields[0].shape
    vmem = pl.BlockSpec(memory_space=pltpu.VMEM)
    args = (xs, *fields, *mats)
    return pl.pallas_call(
        last_kernel,
        in_specs=[pl.BlockSpec(memory_space=pltpu.SMEM)] + [vmem] * len(args),
        out_specs=vmem,
        out_shape=jax.ShapeDtypeStruct((2,) + nat, F32),
        scratch_shapes=[pltpu.VMEM(nat, F32), pltpu.VMEM((2,) + nat[1:], F32), mats_scratch(mats)],
        compiler_params=pltpu.CompilerParams(vmem_limit_bytes=LIMIT["last"] * MIB),
        cost_estimate=cost(800, 9),
        name="slab_last",
    )(ids, *args)


def change_layout(v):
    return lax.all_to_all(v, ALL, split_axis=0, concat_axis=0, tiled=True)


def swap_groups(v):
    return lax.ppermute(v, "emit", [(0, 1), (1, 0)])


def local(
    sound_speed, density, absorption, pressure_start, velocity_start, adjoint_pressure,
    adjoint_velocity, emitter_voxel, emitter_delay, drive_waveform_samples, recorded_pressures,
    sensor_flat_position,
):
    n_emit, n_slab = lax.axis_size("emit"), lax.axis_size("slab")
    ndev = n_emit * n_slab
    planes, ny, nz = sound_speed.shape
    nx = planes * n_slab
    emit = lax.axis_index("emit")
    ids = jnp.stack([emit, lax.axis_index("slab")]).astype(jnp.int32)
    mats = pair_const(deriv_matrix(ny))
    order = (4 * np.arange(n_slab)[None, :] + np.arange(4)[:, None]).reshape(-1)
    line_mats = pair_const(deriv_matrix(nx)[np.ix_(order, order)])

    buf = start_call(
        sound_speed, density, absorption, pressure_start, velocity_start, adjoint_velocity,
        emitter_voxel, emitter_delay, drive_waveform_samples, mats, ndev,
    )
    fields = prepare_call(
        ids, sound_speed, density, absorption, pressure_start, velocity_start, adjoint_pressure,
        adjoint_velocity, sensor_flat_position.reshape(1, -1), recorded_pressures, emitter_voxel,
        emitter_delay, drive_waveform_samples, mats,
    )
    lines, fields = lax.optimization_barrier((change_layout(buf), fields))
    lines = lines.reshape(n_emit, n_slab, 5, 8, nz)
    xs, gx0, gx1, ux, bk = forward_call(lines, line_mats)
    xs = change_layout(xs.reshape(ndev, 2, 8, nz))
    qw, d0, t1, t2 = middle_call(xs, fields, mats)
    qw = change_layout(qw).reshape(n_emit, n_slab, 2, 8, nz)
    xs = adjoint_call(qw, ux, bk, gx0, gx1, line_mats)
    xs = change_layout(xs.reshape(ndev, 24, nz // 2))
    t = last_call(ids, xs, [d0, t1, t2, fields[8], fields[9], fields[0]], mats)
    other = swap_groups(t)
    s1, s2 = t[0] + other[0], t[1] + other[1]
    b = 1.0 / density
    speed_total = (2.0 * DT) * s1 * density * sound_speed
    density_total = DT * (s1 * sound_speed * sound_speed + s2 * b * b)
    return speed_total, density_total


def solution(mesh):
    in_specs = (
        P("slab", None, None), P("slab", None, None), P("slab", None, None),
        P("emit", "slab", None, None), P("emit", None, "slab", None, None),
        P("emit", "slab", None, None), P("emit", None, "slab", None, None),
        P("emit", None), P("emit", None), P(), P("emit", None, None), P(),
    )
    out_specs = (P("slab", None, None), P("slab", None, None))
    return jax.shard_map(local, mesh=mesh, in_specs=in_specs, out_specs=out_specs, check_vma=False)
```

```python
import numpy as np
import jax
import jax.numpy as jnp
from jax import lax
from jax.experimental import pallas as pl
from jax.experimental.pallas import tpu as pltpu
from jax.sharding import PartitionSpec as P

STEPS = 2
DT = 0.2
F32 = jnp.float32
BF16 = jnp.bfloat16
ALL = ("slab", "emit")
MIB = 2**20
LIMIT = {"start": 60, "prepare": 60, "forward": 24, "middle": 40, "adjoint": 20, "last": 20}


def deriv_matrix(n):
    k = np.arange(1, n // 2, dtype=np.int64)
    pts = np.arange(n, dtype=np.int64)
    shifted = (k[None, :] * (2 * pts[:, None] + 1)) % (2 * n) * (np.pi / n)
    plain = (k[None, :] * (2 * pts[:, None])) % (2 * n) * (np.pi / n)
    w = k * (2.0 * np.pi / n)
    m = (np.cos(shifted) * w) @ np.sin(plain).T - (np.sin(shifted) * w) @ np.cos(plain).T
    return m * (2.0 / n)


def pair_const(m):
    m = m.astype(np.float32)
    return [jnp.asarray(m), jnp.asarray(np.ascontiguousarray(m.T))]


def split2(v):
    hi = v.astype(BF16)
    return hi, (v - hi.astype(F32)).astype(BF16)


def split3(v):
    hi = v.astype(BF16)
    rest = v - hi.astype(F32)
    mid = rest.astype(BF16)
    return hi, mid, (rest - mid.astype(F32)).astype(BF16)


def dot(a, b):
    return jnp.dot(a, b, preferred_element_type=F32)


def split_mats(gm, tm, ms):
    for k, m in enumerate((gm, tm)):
        ms[2 * k], ms[2 * k + 1] = split2(m[...])


G, T = 0, 2


def left(ms, k, v):
    h, l = split2(v)
    return dot(ms[k], h) + (dot(ms[k], l) + dot(ms[k + 1], h))


def right(v, ms, k):
    h, l = split2(v)
    return dot(h, ms[k]) + (dot(l, ms[k]) + dot(h, ms[k + 1]))


def mats_scratch(mats):
    return pltpu.VMEM((4,) + mats[0].shape, BF16)


def params(mib, n_grid=1):
    return pltpu.CompilerParams(
        dimension_semantics=("arbitrary",) * n_grid, vmem_limit_bytes=mib * MIB
    )


def cost(mflop, mib):
    return pl.CostEstimate(flops=mflop * 10**6, bytes_accessed=mib * MIB, transcendentals=0)


def swap(v):
    return jnp.swapaxes(v, 0, 1)


def whole(shape):
    return pl.BlockSpec(shape, lambda i, ids: (0,) * len(shape))


def group_plane(shape, pick, a=0):
    block = (None,) * (len(shape) - 3) + (1,) + shape[-2:]
    return pl.BlockSpec(block, lambda i, ids: (0, a)[: len(shape) - 3] + (pick(i, ids), 0, 0))


def plane_onehot(pos, plane, ny, nz):
    local = pos - plane * (ny * nz)
    y = lax.broadcasted_iota(jnp.int32, (ny, pos.shape[1]), 0) * nz
    return jnp.where((local >= y) & (local < y + nz), 1.0, 0.0).astype(BF16)


def column_onehot(pos, nz):
    z = lax.broadcasted_iota(jnp.int32, (nz, pos.shape[1]), 0)
    return lax.rem(pos, nz) == z


def drive_at(delay, drive, step):
    amp = jnp.zeros(delay.shape, F32)
    for k in range(drive.shape[0]):
        amp = jnp.where(delay + step == k, drive[k], amp)
    return amp


def three(onehot, value):
    parts = [jnp.where(onehot, v.astype(F32), 0.0) for v in split3(value)]
    return jnp.concatenate(parts, axis=1).T.astype(BF16)


def spread(rows, cols):
    return dot(jnp.concatenate([rows] * 3, axis=1), cols)


def first_step(planes, cols, epos, numbers, ms):
    ny, nz = planes[0][0].shape
    c, rho, alpha, p, uy, uz = zip(*planes)
    at = range(len(planes))
    gy = [left(ms, G, v) for v in p]
    gz = [right(v, ms, T) for v in p]
    b = [1.0 / v for v in rho]
    bulk = [rho[k] * c[k] * c[k] for k in at]
    wy = [uy[k] - DT * b[k] * gy[k] for k in at]
    wz = [uz[k] - DT * b[k] * gz[k] for k in at]
    yz = [left(ms, T, v) for v in wy]
    zz = [right(v, ms, G) for v in wz]
    shot = [spread(plane_onehot(epos[...], n, ny, nz), cols[...]) for n in numbers]
    yz = [yz[k] + zz[k] for k in at]
    v0 = [(1.0 - DT * alpha[k]) * p[k] + (DT * bulk[k]) * yz[k] + shot[k] for k in at]
    return list(zip(gy, gz, wy, wz, yz, v0, b, bulk))


def plane_copies(srcs, dst, sems, i):
    return [
        pltpu.make_async_copy(src.at[pl.ds(i, 1)], dst.at[i, pl.ds(k, 1)], sems.at[i, k])
        for k, src in enumerate(srcs)
    ]


def start_kernel(
    drive, c, rho, alpha, p0, u, v, epos, delay, gm, tm, buf, ins, sems, outs, out_sems, mat, cols,
    pack, ms
):
    emit, slab = lax.axis_index("emit"), lax.axis_index("slab")
    nx, ny, nz = c.shape
    half = ny // 2

    def send(i):
        return pltpu.make_async_copy(outs.at[i], buf.at[:, i], out_sems.at[i])

    srcs = (p0.at[0], c, rho, alpha, u.at[0, 1], u.at[0, 2], u.at[0, 0], v.at[0, 0])
    for fields in (slice(0, 6), slice(6, 8)):
        for i in range(nx):
            for copy in plane_copies(srcs, ins, sems, i)[fields]:
                copy.start()
    split_mats(gm, tm, ms)
    cols[...] = three(column_onehot(epos[...], nz), drive_at(delay[...], drive, 0))

    @pl.loop(0, nx // 2)
    def _(k):
        pair = (2 * k, 2 * k + 1)
        for i in pair:
            for copy in plane_copies(srcs, ins, sems, i)[:6]:
                copy.wait()
        steps = first_step(
            [tuple(ins[i, f] for f in (1, 2, 3, 0, 4, 5)) for i in pair],
            cols, epos, [slab * nx + i for i in pair], ms,
        )
        for xm, i in enumerate(pair):
            v0, b, bulk = steps[xm][5:]
            for copy in plane_copies(srcs, ins, sems, i)[6:]:
                copy.wait()
            for f, field in enumerate((ins[i, 0], ins[i, 6], v0, ins[i, 7])):
                pack[xm, 2 * f : 2 * f + 2] = field.reshape(2, half, nz)
            outs[i] = swap(pack[xm])
            send(i).start()

            @pl.when(k == emit)
            def _():
                mat[4 * xm : 4 * xm + 2] = b.reshape(2, half, nz)
                mat[4 * xm + 2 : 4 * xm + 4] = bulk.reshape(2, half, nz)

    outs[nx] = swap(mat[...])
    send(nx).start()
    for i in range(nx + 1):
        send(i).wait()


def start_call(c, rho, alpha, p0, u, v, epos, delay, drive, mats, ndev):
    nx, ny, nz = c.shape
    n_e = epos.shape[1]
    hbm, vmem, smem = (pl.BlockSpec(memory_space=m) for m in (pltpu.HBM, pltpu.VMEM, pltpu.SMEM))
    return pl.pallas_call(
        start_kernel,
        in_specs=[smem] + [hbm] * 6 + [vmem] * 4,
        out_specs=hbm,
        out_shape=jax.ShapeDtypeStruct((ndev, nx + 1, 8, nz), F32),
        scratch_shapes=[pltpu.VMEM((nx, 8, ny, nz), F32), pltpu.SemaphoreType.DMA((nx, 8)),
                        pltpu.VMEM((nx + 1, ndev, 8, nz), F32), pltpu.SemaphoreType.DMA((nx + 1,)),
                        pltpu.VMEM((8, ndev, nz), F32), pltpu.VMEM((3 * n_e, nz), BF16),
                        pltpu.VMEM((2, 8, ndev, nz), F32), mats_scratch(mats)],
        compiler_params=pltpu.CompilerParams(vmem_limit_bytes=LIMIT["start"] * MIB),
        cost_estimate=cost(2000, 13),
        name="start",
    )(drive, c, rho, alpha, p0, u, v, epos, delay, *mats)


def prepare_kernel(
    ids, drive, c, rho, alpha, p0, uy, uz, pa, ay, az, spos, rec, epos, delay, gm, tm,
    dk, stay, b, pm, cdk, wb, yz1, late, gy0, gz0, ones, scols, ecols, ms,
):
    i = pl.program_id(0)
    ny, nz = c.shape[1], c.shape[2]

    @pl.when(i == 0)
    def _():
        split_mats(gm, tm, ms)
        oh = column_onehot(spos[...], nz)
        ones[...] = jnp.where(oh, 1.0, 0.0).T.astype(BF16)
        for step in range(STEPS):
            scols[step] = three(oh, rec[step : step + 1])
        for step in range(STEPS):
            ecols[step] = three(column_onehot(epos[...], nz), drive_at(delay[...], drive, step))

    plane = ids[1] * 4 + i
    gy, gz, u1y, u1z, yz0, v0, buoy, bulk = first_step(
        [(c[0], rho[0], alpha[0], p0[0], uy[0], uz[0])], ecols.at[0], epos, [plane], ms
    )[0]
    keep = 1.0 - DT * alpha[0]
    s = plane_onehot(spos[...], plane, ny, nz)
    count = dot(s, ones[...])
    m0 = spread(s, scols[0])
    m1 = spread(s, scols[1])
    shot = spread(plane_onehot(epos[...], plane, ny, nz), ecols[1])
    gyv = left(ms, G, v0)
    gzv = right(v0, ms, T)
    db = DT * buoy
    yz = left(ms, T, u1y - db * gyv) + right(u1z - db * gzv, ms, G)
    back = left(ms, T, buoy * ay[0]) + right(buoy * az[0], ms, G)
    dk[0] = DT * bulk
    stay[0] = keep
    b[0] = buoy
    cdk[0] = count * (DT * bulk)
    pm[0] = pa[0] + (count * (keep * v0 + (DT * bulk) * yz + shot) - m1)
    wb[0] = (count * v0 - m0) - DT * back
    yz1[0] = yz
    for k, field in enumerate((yz0, gy + gyv, gz + gzv, ay[0], az[0])):
        late[0, k] = field
    gy0[0] = gy
    gz0[0] = gz


def prepare_call(
    ids, c, rho, alpha, p0, u, pa, v, spos, rec, epos, delay, drive, mats
):
    nx, ny, nz = c.shape
    n_e, n_s = epos.shape[1], spos.shape[1]
    pick = lambda i, ids: i
    plane = group_plane(c.shape, pick)
    return pl.pallas_call(
        prepare_kernel,
        grid_spec=pltpu.PrefetchScalarGridSpec(
            num_scalar_prefetch=1,
            grid=(nx,),
            in_specs=[pl.BlockSpec(memory_space=pltpu.SMEM)] + [plane] * 3
            + [group_plane(p0.shape, pick)] + [group_plane(u.shape, pick, a) for a in (1, 2)]
            + [group_plane(pa.shape, pick)] + [group_plane(v.shape, pick, a) for a in (1, 2)]
            + [whole((1, n_s)), pl.BlockSpec((None, STEPS, n_s), lambda i, ids: (0, 0, 0)),
               whole((1, n_e)), whole((1, n_e))]
            + [whole((ny, ny))] * 2,
            out_specs=[plane] * 7 + [pl.BlockSpec((1, 5, ny, nz), lambda i, ids: (i, 0, 0, 0))]
            + [plane] * 2,
            scratch_shapes=[pltpu.VMEM((n_s, nz), BF16), pltpu.VMEM((STEPS, 3 * n_s, nz), BF16),
                            pltpu.VMEM((STEPS, 3 * n_e, nz), BF16), mats_scratch(mats)],
        ),
        out_shape=[jax.ShapeDtypeStruct(c.shape, F32)] * 7
        + [jax.ShapeDtypeStruct((nx, 5, ny, nz), F32)] + [jax.ShapeDtypeStruct(c.shape, F32)] * 2,
        compiler_params=params(LIMIT["prepare"]),
        cost_estimate=cost(8000, 22),
        name="prepare",
    )(ids, drive, c, rho, alpha, p0, u, u, pa, v, v, spos, rec, epos, delay, *mats)


def on_chip(kernel, away, args, shapes, scratch, limit, estimate, name):
    vmem = pl.BlockSpec(memory_space=pltpu.VMEM)
    return pl.pallas_call(
        kernel,
        in_specs=[pl.BlockSpec(memory_space=pltpu.HBM)] * len(away) + [vmem] * len(args),
        out_specs=[vmem] * len(shapes),
        out_shape=[jax.ShapeDtypeStruct(v, F32) for v in shapes],
        scratch_shapes=[pltpu.VMEM(v, F32) if isinstance(v, tuple) else v for v in scratch]
        + [mats_scratch(args[-2:])],
        compiler_params=pltpu.CompilerParams(vmem_limit_bytes=limit * MIB),
        cost_estimate=estimate,
        name=name,
    )(*away, *args)


def unpack(block, dst, first):
    t = swap(block)
    n = t.shape[1]
    for xm in range(2):
        dst[:, (first + xm) * n : (first + xm + 1) * n, :] = t[4 * xm : 4 * xm + 4]


def forward_kernel(lines, gm, tm, out, gx0, gx1, ax, bk, in_s, mat_s, sems, f_s, o_s, ms):
    n = lines.shape[0]
    fetch = lambda g: pltpu.make_async_copy(lines.at[:, g, pl.ds(0, 4)], in_s.at[g], sems.at[1 + g])
    copies = [pltpu.make_async_copy(lines.at[:, :, 4], mat_s, sems.at[0]), fetch(0), fetch(1)]
    for copy in copies:
        copy.start()
    split_mats(gm, tm, ms)
    copies[0].wait()
    for e in range(2):
        unpack(mat_s[:, e], bk, 2 * e)

    @pl.loop(0, 2)
    def _(g):
        fetch(g).wait()
        for xl in range(4):
            rows = slice(xl * n, (xl + 1) * n)
            t = swap(in_s[g, :, xl])
            f_s[:, rows, :] = t[:6]
            ax[pl.ds(2 * g, 2), rows, :] = t[6:]
        rows = range(2)
        g0 = [left(ms, G, f_s[yl]) for yl in rows]
        u1 = [f_s[2 + yl] - (DT * bk[yl]) * g0[yl] for yl in rows]
        x0 = [left(ms, T, u1[yl]) for yl in rows]
        p1 = [f_s[4 + yl] + (DT * bk[2 + yl]) * x0[yl] for yl in rows]
        g1 = [left(ms, G, p1[yl]) for yl in rows]
        x1 = [left(ms, T, u1[yl] - (DT * bk[yl]) * g1[yl]) for yl in rows]
        for yl in rows:
            gx0[2 * g + yl] = g0[yl]
            gx1[2 * g + yl] = g1[yl]
            o_s[yl] = x0[yl]
            o_s[2 + yl] = x1[yl]
        for h in range(2):
            both = [o_s[:, (2 * h + xm) * n : (2 * h + xm + 1) * n, :] for xm in range(2)]
            out[:, pl.ds(g, 1), h] = swap(jnp.concatenate(both, axis=0))[:, None]


def forward_call(lines, mats):
    ns, _, _, _, nz = lines.shape
    nx = 4 * ns
    full = (4, nx, nz)
    return on_chip(
        forward_kernel, (lines,), mats, [(ns, 2, 2, 8, nz), full, full, full, full],
        [(2, ns, 4, 8, nz), (ns, 2, 8, nz), pltpu.SemaphoreType.DMA((3,)), (6, nx, nz), (4, nx, nz)],
        LIMIT["forward"], cost(1600, 11), "lines_forward",
    )


def middle_kernel(
    late, xs, dk, stay, b, pm, cdk, wb, yz1, gm, tm,
    buf, d0, t1, t2, x_s, o_s, ins, sems, ms,
):
    nx, ny, nz = dk.shape
    fetch = lambda i: pltpu.make_async_copy(late.at[i], ins.at[i], sems.at[i])
    for i in range(nx):
        fetch(i).start()
    split_mats(gm, tm, ms)
    for h in range(2):
        x_s[4 * h : 4 * h + 4] = swap(xs[:, h]).reshape(4, ny, nz)

    def some(planes):
        add = [dk[i] * x_s[2 * i] for i in planes]
        ey = [left(ms, G, a) for a in add]
        ez = [right(a, ms, T) for a in add]
        gy = [left(ms, T, (DT * b[i]) * e) for i, e in zip(planes, ey)]
        gz = [right((DT * b[i]) * e, ms, G) for i, e in zip(planes, ez)]
        rest = [x_s[2 * i + 1] - (e + f) for i, e, f in zip(planes, gy, gz)]
        adj = [pm[i] + cdk[i] * (stay[i] * x_s[2 * i] + r) for i, r in zip(planes, rest)]
        q = [dk[i] * a for i, a in zip(planes, adj)]
        fy = [left(ms, G, a) for a in q]
        fz = [right(a, ms, T) for a in q]
        for k, i in enumerate(planes):
            o_s[2 * i] = q[k]
            t1[i] = (yz1[i] + rest[k]) * adj[k]
        gy = [left(ms, T, b[i] * e) for i, e in zip(planes, fy)]
        gz = [right(b[i] * e, ms, G) for i, e in zip(planes, fz)]
        for k, i in enumerate(planes):
            o_s[2 * i + 1] = stay[i] * adj[k] + (cdk[i] * x_s[2 * i] + wb[i]) - DT * (gy[k] + gz[k])
            fetch(i).wait()
            d0[i] = x_s[2 * i] + ins[i, 0]
            t2[i] = (ins[i, 1] + ey[k]) * (ins[i, 3] + fy[k]) + (ins[i, 2] + ez[k]) * (ins[i, 4] + fz[k])

    some(range(nx))

    for h in range(2):
        buf[:, h] = swap(o_s[4 * h : 4 * h + 4].reshape(8, ny // 2, nz))


def middle_call(xs, fields, mats):
    nat = fields[0].shape
    saved = (8,) + nat[1:]
    return on_chip(
        middle_kernel, (fields[7],), (xs, *fields[:7], *mats), [xs.shape, nat, nat, nat],
        [saved, saved, (nat[0], 5) + nat[1:], pltpu.SemaphoreType.DMA((nat[0],))],
        LIMIT["middle"], cost(3200, 18), "slab_middle",
    )


def adjoint_kernel(qw, ux, bk, gx0, gx1, gm, tm, out, f_s, p_s, bx_s, ms):
    split_mats(gm, tm, ms)
    n, nz = qw.shape[0], qw.shape[4]
    lanes = [slice(0, nz // 2), slice(nz // 2, nz)]

    for g in range(2):
        for h in range(2):
            unpack(qw[:, g, h], f_s.at[g], 2 * h)

    at = [(g, yl) for g in range(2) for yl in range(2)]
    ax = [left(ms, G, f_s[g, yl]) for g, yl in at]
    ax = [ux[j] + v for j, v in enumerate(ax)]
    back = [left(ms, T, bk[yl] * v) for (g, yl), v in zip(at, ax)]
    p0 = [f_s[g, 2 + yl] - DT * v for (g, yl), v in zip(at, back)]
    gq = [left(ms, G, (DT * bk[2 + yl]) * v) for (g, yl), v in zip(at, p0)]
    bx = [gx1[j] * ax[j] + gx0[j] * (ax[j] + gq[j]) for j in range(4)]
    for j in range(4):
        p_s[j] = p0[j]
    for yl in range(2):
        bx_s[yl] = bx[yl] + bx[2 + yl]

    for g in range(2):
        for zh, z in enumerate(lanes):
            v = [p_s[2 * g : 2 * g + 2, xl * n : (xl + 1) * n, z] for xl in range(4)]
            out[:, g, 8 * zh : 8 * zh + 8, :] = swap(jnp.concatenate(v, axis=0))

    for e in range(2):
        v = [bx_s[:, (2 * e + xm) * n : (2 * e + xm + 1) * n, z] for z in lanes for xm in range(2)]
        out[:, e, 16:24, :] = swap(jnp.concatenate(v, axis=0))


def adjoint_call(qw, ux, bk, gx0, gx1, mats):
    ns, _, _, _, nz = qw.shape
    nx = 4 * ns
    return on_chip(
        adjoint_kernel, (), (qw, ux, bk, gx0, gx1, *mats), [(ns, 2, 24, nz // 2)],
        [(2, 4, nx, nz), (4, nx, nz), (2, nx, nz)], LIMIT["adjoint"], cost(1200, 9), "lines_adjoint",
    )[0]


def last_kernel(ids, xs, d0, t1, t2, gy0, gz0, dk, gm, tm, out, p_s, bx_s, ms):
    split_mats(gm, tm, ms)
    nx, ny, nz = d0.shape
    half = nz // 2
    t = swap(xs[:, 16:24, :]).reshape(4, ny, half)
    for zh in range(2):
        z = slice(zh * half, (zh + 1) * half)
        p_s[:, :, z] = swap(xs[:, 8 * zh : 8 * zh + 8, :]).reshape(nx, ny, half)
        bx_s[:, :, z] = t[2 * zh : 2 * zh + 2]

    q = [dk[i] * p_s[i] for i in range(nx)]
    gy = [left(ms, G, v) for v in q]
    gz = [right(v, ms, T) for v in q]
    for i in range(nx):
        out[0, i] = t1[i] + d0[i] * p_s[i]
        out[1, i] = t2[i] + gy0[i] * gy[i] + gz0[i] * gz[i]

    for xm in range(2):
        out[1, 2 * ids[0] + xm] += bx_s[xm]


def last_call(ids, xs, fields, mats):
    nat = fields[0].shape
    vmem = pl.BlockSpec(memory_space=pltpu.VMEM)
    args = (xs, *fields, *mats)
    return pl.pallas_call(
        last_kernel,
        in_specs=[pl.BlockSpec(memory_space=pltpu.SMEM)] + [vmem] * len(args),
        out_specs=vmem,
        out_shape=jax.ShapeDtypeStruct((2,) + nat, F32),
        scratch_shapes=[pltpu.VMEM(nat, F32), pltpu.VMEM((2,) + nat[1:], F32), mats_scratch(mats)],
        compiler_params=pltpu.CompilerParams(vmem_limit_bytes=LIMIT["last"] * MIB),
        cost_estimate=cost(800, 9),
        name="slab_last",
    )(ids, *args)


def change_layout(v):
    return lax.all_to_all(v, ALL, split_axis=0, concat_axis=0, tiled=True)


def swap_groups(v):
    return lax.ppermute(v, "emit", [(0, 1), (1, 0)])


def local(
    sound_speed, density, absorption, pressure_start, velocity_start, adjoint_pressure,
    adjoint_velocity, emitter_voxel, emitter_delay, drive_waveform_samples, recorded_pressures,
    sensor_flat_position,
):
    n_emit, n_slab = lax.axis_size("emit"), lax.axis_size("slab")
    ndev = n_emit * n_slab
    planes, ny, nz = sound_speed.shape
    nx = planes * n_slab
    emit = lax.axis_index("emit")
    ids = jnp.stack([emit, lax.axis_index("slab")]).astype(jnp.int32)
    mats = pair_const(deriv_matrix(ny))
    order = (4 * np.arange(n_slab)[None, :] + np.arange(4)[:, None]).reshape(-1)
    line_mats = pair_const(deriv_matrix(nx)[np.ix_(order, order)])

    buf = start_call(
        sound_speed, density, absorption, pressure_start, velocity_start, adjoint_velocity,
        emitter_voxel, emitter_delay, drive_waveform_samples, mats, ndev,
    )
    fields = prepare_call(
        ids, sound_speed, density, absorption, pressure_start, velocity_start, adjoint_pressure,
        adjoint_velocity, sensor_flat_position.reshape(1, -1), recorded_pressures, emitter_voxel,
        emitter_delay, drive_waveform_samples, mats,
    )
    lines, fields = lax.optimization_barrier((change_layout(buf), fields))
    lines = lines.reshape(n_slab, n_emit, 5, 8, nz)
    xs, gx0, gx1, ux, bk = forward_call(lines, line_mats)
    xs = change_layout(xs.reshape(ndev, 2, 8, nz))
    qw, d0, t1, t2 = middle_call(xs, fields, mats)
    qw = change_layout(qw).reshape(n_slab, n_emit, 2, 8, nz)
    xs = adjoint_call(qw, ux, bk, gx0, gx1, line_mats)
    xs = change_layout(xs.reshape(ndev, 24, nz // 2))
    t = last_call(ids, xs, [d0, t1, t2, fields[8], fields[9], fields[0]], mats)
    other = swap_groups(t)
    s1, s2 = t[0] + other[0], t[1] + other[1]
    b = 1.0 / density
    speed_total = (2.0 * DT) * s1 * density * sound_speed
    density_total = DT * (s1 * sound_speed * sound_speed + s2 * b * b)
    return speed_total, density_total


def solution(mesh):
    in_specs = (
        P("slab", None, None), P("slab", None, None), P("slab", None, None),
        P("emit", "slab", None, None), P("emit", None, "slab", None, None),
        P("emit", "slab", None, None), P("emit", None, "slab", None, None),
        P("emit", None), P("emit", None), P(), P("emit", None, None), P(),
    )
    out_specs = (P("slab", None, None), P("slab", None, None))
    return jax.shard_map(local, mesh=mesh, in_specs=in_specs, out_specs=out_specs, check_vma=False)
```

```python
import numpy as np
import jax
import jax.numpy as jnp
from jax import lax
from jax.experimental import pallas as pl
from jax.experimental.pallas import tpu as pltpu
from jax.sharding import PartitionSpec as P

STEPS = 2
DT = 0.2
F32 = jnp.float32
BF16 = jnp.bfloat16
ALL = ("slab", "emit")
MIB = 2**20
LIMIT = {"start": 60, "prepare": 60, "forward": 24, "middle": 40, "adjoint": 20, "last": 20}


def deriv_matrix(n):
    k = np.arange(1, n // 2, dtype=np.int64)
    pts = np.arange(n, dtype=np.int64)
    shifted = (k[None, :] * (2 * pts[:, None] + 1)) % (2 * n) * (np.pi / n)
    plain = (k[None, :] * (2 * pts[:, None])) % (2 * n) * (np.pi / n)
    w = k * (2.0 * np.pi / n)
    m = (np.cos(shifted) * w) @ np.sin(plain).T - (np.sin(shifted) * w) @ np.cos(plain).T
    return m * (2.0 / n)


def pair_const(m):
    m = m.astype(np.float32)
    return [jnp.asarray(m), jnp.asarray(np.ascontiguousarray(m.T))]


def split2(v):
    hi = v.astype(BF16)
    return hi, (v - hi.astype(F32)).astype(BF16)


def split3(v):
    hi = v.astype(BF16)
    rest = v - hi.astype(F32)
    mid = rest.astype(BF16)
    return hi, mid, (rest - mid.astype(F32)).astype(BF16)


def dot(a, b):
    return jnp.dot(a, b, preferred_element_type=F32)


def split_mats(gm, tm, ms):
    for k, m in enumerate((gm, tm)):
        ms[2 * k], ms[2 * k + 1] = split2(m[...])


G, T = 0, 2


def left(ms, k, v):
    h, l = split2(v)
    return dot(ms[k], h) + (dot(ms[k], l) + dot(ms[k + 1], h))


def right(v, ms, k):
    h, l = split2(v)
    return dot(h, ms[k]) + (dot(l, ms[k]) + dot(h, ms[k + 1]))


def mats_scratch(mats):
    return pltpu.VMEM((4,) + mats[0].shape, BF16)


def params(mib, n_grid=1):
    return pltpu.CompilerParams(
        dimension_semantics=("arbitrary",) * n_grid, vmem_limit_bytes=mib * MIB
    )


def cost(mflop, mib):
    return pl.CostEstimate(flops=mflop * 10**6, bytes_accessed=mib * MIB, transcendentals=0)


def swap(v):
    return jnp.swapaxes(v, 0, 1)


def whole(shape):
    return pl.BlockSpec(shape, lambda i, ids: (0,) * len(shape))


def group_plane(shape, pick, a=0):
    block = (None,) * (len(shape) - 3) + (1,) + shape[-2:]
    return pl.BlockSpec(block, lambda i, ids: (0, a)[: len(shape) - 3] + (pick(i, ids), 0, 0))


def plane_onehot(pos, plane, ny, nz):
    local = pos - plane * (ny * nz)
    y = lax.broadcasted_iota(jnp.int32, (ny, pos.shape[1]), 0) * nz
    return jnp.where((local >= y) & (local < y + nz), 1.0, 0.0).astype(BF16)


def column_onehot(pos, nz):
    z = lax.broadcasted_iota(jnp.int32, (nz, pos.shape[1]), 0)
    return lax.rem(pos, nz) == z


def drive_at(delay, drive, step):
    amp = jnp.zeros(delay.shape, F32)
    for k in range(drive.shape[0]):
        amp = jnp.where(delay + step == k, drive[k], amp)
    return amp


def three(onehot, value):
    parts = [jnp.where(onehot, v.astype(F32), 0.0) for v in split3(value)]
    return jnp.concatenate(parts, axis=1).T.astype(BF16)


def spread(rows, cols):
    return dot(jnp.concatenate([rows] * 3, axis=1), cols)


def first_step(planes, cols, epos, numbers, ms):
    ny, nz = planes[0][0].shape
    c, rho, alpha, p, uy, uz = zip(*planes)
    at = range(len(planes))
    gy = [left(ms, G, v) for v in p]
    gz = [right(v, ms, T) for v in p]
    b = [1.0 / v for v in rho]
    bulk = [rho[k] * c[k] * c[k] for k in at]
    wy = [uy[k] - DT * b[k] * gy[k] for k in at]
    wz = [uz[k] - DT * b[k] * gz[k] for k in at]
    yz = [left(ms, T, v) for v in wy]
    zz = [right(v, ms, G) for v in wz]
    shot = [spread(plane_onehot(epos[...], n, ny, nz), cols[...]) for n in numbers]
    yz = [yz[k] + zz[k] for k in at]
    v0 = [(1.0 - DT * alpha[k]) * p[k] + (DT * bulk[k]) * yz[k] + shot[k] for k in at]
    return list(zip(gy, gz, wy, wz, yz, v0, b, bulk))


def plane_copies(srcs, dst, sems, i):
    return [
        pltpu.make_async_copy(src.at[pl.ds(i, 1)], dst.at[i, pl.ds(k, 1)], sems.at[i, k])
        for k, src in enumerate(srcs)
    ]


def start_kernel(
    drive, c, rho, alpha, p0, u, epos, delay, gm, tm, buf, ins, sems, outs, out_sems, cols, pack, ms
):
    emit, slab = lax.axis_index("emit"), lax.axis_index("slab")
    nx, ny, nz = c.shape
    half = ny // 2

    def send(i):
        return pltpu.make_async_copy(outs.at[i], buf.at[:, i], out_sems.at[i])

    srcs = (p0.at[0], c, rho, alpha, u.at[0, 1], u.at[0, 2], u.at[0, 0])
    for fields in (slice(0, 6), slice(6, 7)):
        for i in range(nx):
            for copy in plane_copies(srcs, ins, sems, i)[fields]:
                copy.start()
    split_mats(gm, tm, ms)
    cols[...] = three(column_onehot(epos[...], nz), drive_at(delay[...], drive, 0))

    @pl.loop(0, nx // 2)
    def _(k):
        pair = (2 * k, 2 * k + 1)
        for i in pair:
            for copy in plane_copies(srcs, ins, sems, i)[:6]:
                copy.wait()
        steps = first_step(
            [tuple(ins[i, f] for f in (1, 2, 3, 0, 4, 5)) for i in pair],
            cols, epos, [slab * nx + i for i in pair], ms,
        )
        for xm, i in enumerate(pair):
            v0, b, bulk = steps[xm][5:]
            for copy in plane_copies(srcs, ins, sems, i)[6:]:
                copy.wait()
            for f, field in enumerate((ins[i, 0], ins[i, 6], v0, jnp.where(emit == 0, b, bulk))):
                pack[xm, 2 * f : 2 * f + 2] = field.reshape(2, half, nz)
            outs[i] = swap(pack[xm])
            send(i).start()

    for i in range(nx):
        send(i).wait()


def start_call(c, rho, alpha, p0, u, epos, delay, drive, mats, ndev):
    nx, ny, nz = c.shape
    n_e = epos.shape[1]
    hbm, vmem, smem = (pl.BlockSpec(memory_space=m) for m in (pltpu.HBM, pltpu.VMEM, pltpu.SMEM))
    return pl.pallas_call(
        start_kernel,
        in_specs=[smem] + [hbm] * 5 + [vmem] * 4,
        out_specs=hbm,
        out_shape=jax.ShapeDtypeStruct((ndev, nx, 8, nz), F32),
        scratch_shapes=[pltpu.VMEM((nx, 7, ny, nz), F32), pltpu.SemaphoreType.DMA((nx, 7)),
                        pltpu.VMEM((nx, ndev, 8, nz), F32), pltpu.SemaphoreType.DMA((nx,)),
                        pltpu.VMEM((3 * n_e, nz), BF16),
                        pltpu.VMEM((2, 8, ndev, nz), F32), mats_scratch(mats)],
        compiler_params=pltpu.CompilerParams(vmem_limit_bytes=LIMIT["start"] * MIB),
        cost_estimate=cost(2000, 13),
        name="start",
    )(drive, c, rho, alpha, p0, u, epos, delay, *mats)


def prepare_kernel(
    ids, drive, c, rho, alpha, p0, uy, uz, pa, ax, ay, az, spos, rec, epos, delay, gm, tm,
    dk, stay, b, pm, cdk, wb, yz1, late, gy0, gz0, axs, ones, scols, ecols, pack, ms,
):
    i = pl.program_id(0)
    ny, nz = c.shape[1], c.shape[2]

    @pl.when(i == 0)
    def _():
        split_mats(gm, tm, ms)
        oh = column_onehot(spos[...], nz)
        ones[...] = jnp.where(oh, 1.0, 0.0).T.astype(BF16)
        for step in range(STEPS):
            scols[step] = three(oh, rec[step : step + 1])
        for step in range(STEPS):
            ecols[step] = three(column_onehot(epos[...], nz), drive_at(delay[...], drive, step))

    plane = ids[1] * 4 + i
    gy, gz, u1y, u1z, yz0, v0, buoy, bulk = first_step(
        [(c[0], rho[0], alpha[0], p0[0], uy[0], uz[0])], ecols.at[0], epos, [plane], ms
    )[0]
    keep = 1.0 - DT * alpha[0]
    s = plane_onehot(spos[...], plane, ny, nz)
    count = dot(s, ones[...])
    m0 = spread(s, scols[0])
    m1 = spread(s, scols[1])
    shot = spread(plane_onehot(epos[...], plane, ny, nz), ecols[1])
    gyv = left(ms, G, v0)
    gzv = right(v0, ms, T)
    db = DT * buoy
    yz = left(ms, T, u1y - db * gyv) + right(u1z - db * gzv, ms, G)
    back = left(ms, T, buoy * ay[0]) + right(buoy * az[0], ms, G)
    dk[0] = DT * bulk
    stay[0] = keep
    b[0] = buoy
    cdk[0] = count * (DT * bulk)
    pm[0] = pa[0] + (count * (keep * v0 + (DT * bulk) * yz + shot) - m1)
    wb[0] = (count * v0 - m0) - DT * back
    yz1[0] = yz
    for k, field in enumerate((yz0, gy + gyv, gz + gzv, ay[0], az[0])):
        late[0, k] = field
    gy0[0] = gy
    gz0[0] = gz
    pack[pl.ds(2 * i, 2)] = ax[0].reshape(2, ny // 2, nz)

    @pl.when(i == pl.num_programs(0) - 1)
    def _():
        axs[...] = swap(pack[...])


def prepare_call(
    ids, c, rho, alpha, p0, u, pa, v, spos, rec, epos, delay, drive, mats
):
    nx, ny, nz = c.shape
    n_e, n_s = epos.shape[1], spos.shape[1]
    pick = lambda i, ids: i
    plane = group_plane(c.shape, pick)
    return pl.pallas_call(
        prepare_kernel,
        grid_spec=pltpu.PrefetchScalarGridSpec(
            num_scalar_prefetch=1,
            grid=(nx,),
            in_specs=[pl.BlockSpec(memory_space=pltpu.SMEM)] + [plane] * 3
            + [group_plane(p0.shape, pick)] + [group_plane(u.shape, pick, a) for a in (1, 2)]
            + [group_plane(pa.shape, pick)] + [group_plane(v.shape, pick, a) for a in range(3)]
            + [whole((1, n_s)), pl.BlockSpec((None, STEPS, n_s), lambda i, ids: (0, 0, 0)),
               whole((1, n_e)), whole((1, n_e))]
            + [whole((ny, ny))] * 2,
            out_specs=[plane] * 7 + [pl.BlockSpec((1, 5, ny, nz), lambda i, ids: (i, 0, 0, 0))]
            + [plane] * 2 + [whole((ny // 2, 2 * nx, nz))],
            scratch_shapes=[pltpu.VMEM((n_s, nz), BF16), pltpu.VMEM((STEPS, 3 * n_s, nz), BF16),
                            pltpu.VMEM((STEPS, 3 * n_e, nz), BF16),
                            pltpu.VMEM((2 * nx, ny // 2, nz), F32), mats_scratch(mats)],
        ),
        out_shape=[jax.ShapeDtypeStruct(c.shape, F32)] * 7
        + [jax.ShapeDtypeStruct((nx, 5, ny, nz), F32)] + [jax.ShapeDtypeStruct(c.shape, F32)] * 2
        + [jax.ShapeDtypeStruct((ny // 2, 2 * nx, nz), F32)],
        compiler_params=params(LIMIT["prepare"]),
        cost_estimate=cost(8000, 22),
        name="prepare",
    )(ids, drive, c, rho, alpha, p0, u, u, pa, v, v, v, spos, rec, epos, delay, *mats)


def on_chip(kernel, away, args, shapes, scratch, limit, estimate, name):
    vmem = pl.BlockSpec(memory_space=pltpu.VMEM)
    return pl.pallas_call(
        kernel,
        in_specs=[pl.BlockSpec(memory_space=pltpu.HBM)] * len(away) + [vmem] * len(args),
        out_specs=[vmem] * len(shapes),
        out_shape=[jax.ShapeDtypeStruct(v, F32) for v in shapes],
        scratch_shapes=[pltpu.VMEM(v, F32) if isinstance(v, tuple) else v for v in scratch]
        + [mats_scratch(args[-2:])],
        compiler_params=pltpu.CompilerParams(vmem_limit_bytes=limit * MIB),
        cost_estimate=estimate,
        name=name,
    )(*away, *args)


def unpack(block, dst, first):
    t = swap(block)
    n = t.shape[1]
    for xm in range(2):
        dst[:, (first + xm) * n : (first + xm + 1) * n, :] = t[4 * xm : 4 * xm + 4]


def forward_kernel(lines, gm, tm, out, gx0, gx1, bk, in_s, sems, f_s, o_s, ms):
    n = lines.shape[0]
    fetch = lambda g: pltpu.make_async_copy(lines.at[:, g], in_s.at[g], sems.at[g])
    groups, at = range(2), range(4)
    for g in groups:
        fetch(g).start()
    split_mats(gm, tm, ms)
    g0, u1, x0 = [], [], []
    for g in groups:
        fetch(g).wait()
        for xl in range(4):
            rows = slice(xl * n, (xl + 1) * n)
            t = swap(in_s[g, :, xl])
            f_s[g, :, rows, :] = t[:6]
            bk[2 * g : 2 * g + 2, rows, :] = t[6:]
        g0 += [left(ms, G, f_s[g, yl]) for yl in range(2)]
        u1 += [f_s[g, 2 + yl] - (DT * bk[yl]) * g0[2 * g + yl] for yl in range(2)]
        x0 += [left(ms, T, u1[2 * g + yl]) for yl in range(2)]
    p1 = [f_s[j // 2, 4 + j % 2] + (DT * bk[2 + j % 2]) * x0[j] for j in at]
    g1 = [left(ms, G, p1[j]) for j in at]
    x1 = [left(ms, T, u1[j] - (DT * bk[j % 2]) * g1[j]) for j in at]
    for j in at:
        gx0[j] = g0[j]
        gx1[j] = g1[j]
        o_s[j // 2, j % 2] = x0[j]
        o_s[j // 2, 2 + j % 2] = x1[j]
    for g in groups:
        for h in range(2):
            both = [o_s[g, :, (2 * h + xm) * n : (2 * h + xm + 1) * n, :] for xm in range(2)]
            out[:, g, h] = swap(jnp.concatenate(both, axis=0))


def forward_call(lines, mats):
    ns, _, _, _, nz = lines.shape
    nx = 4 * ns
    full = (4, nx, nz)
    return on_chip(
        forward_kernel, (lines,), mats, [(ns, 2, 2, 8, nz), full, full, full],
        [(2, ns, 4, 8, nz), pltpu.SemaphoreType.DMA((2,)), (2, 6, nx, nz), (2, 4, nx, nz)],
        LIMIT["forward"], cost(1600, 9), "lines_forward",
    )


def middle_kernel(
    late, axs, xs, dk, stay, b, pm, cdk, wb, yz1, gm, tm,
    buf, d0, t1, t2, x_s, o_s, ins, sems, ms,
):
    nx, ny, nz = dk.shape
    fetch = lambda i: pltpu.make_async_copy(late.at[i], ins.at[i], sems.at[i])
    for i in range(nx):
        fetch(i).start()
    fetch_ax = pltpu.make_async_copy(axs, buf.at[:, 2], sems.at[nx])
    fetch_ax.start()
    split_mats(gm, tm, ms)
    for h in range(2):
        x_s[4 * h : 4 * h + 4] = swap(xs[:, h]).reshape(4, ny, nz)

    def some(planes):
        add = [dk[i] * x_s[2 * i] for i in planes]
        ey = [left(ms, G, a) for a in add]
        ez = [right(a, ms, T) for a in add]
        gy = [left(ms, T, (DT * b[i]) * e) for i, e in zip(planes, ey)]
        gz = [right((DT * b[i]) * e, ms, G) for i, e in zip(planes, ez)]
        rest = [x_s[2 * i + 1] - (e + f) for i, e, f in zip(planes, gy, gz)]
        adj = [pm[i] + cdk[i] * (stay[i] * x_s[2 * i] + r) for i, r in zip(planes, rest)]
        q = [dk[i] * a for i, a in zip(planes, adj)]
        fy = [left(ms, G, a) for a in q]
        fz = [right(a, ms, T) for a in q]
        for k, i in enumerate(planes):
            o_s[2 * i] = q[k]
            t1[i] = (yz1[i] + rest[k]) * adj[k]
        gy = [left(ms, T, b[i] * e) for i, e in zip(planes, fy)]
        gz = [right(b[i] * e, ms, G) for i, e in zip(planes, fz)]
        for k, i in enumerate(planes):
            o_s[2 * i + 1] = stay[i] * adj[k] + (cdk[i] * x_s[2 * i] + wb[i]) - DT * (gy[k] + gz[k])
            fetch(i).wait()
            d0[i] = x_s[2 * i] + ins[i, 0]
            t2[i] = (ins[i, 1] + ey[k]) * (ins[i, 3] + fy[k]) + (ins[i, 2] + ez[k]) * (ins[i, 4] + fz[k])

    some(range(nx))

    for h in range(2):
        buf[:, h] = swap(o_s[4 * h : 4 * h + 4].reshape(8, ny // 2, nz))
    fetch_ax.wait()


def middle_call(xs, fields, mats):
    nat = fields[0].shape
    saved = (8,) + nat[1:]
    return on_chip(
        middle_kernel, (fields[7], fields[10]), (xs, *fields[:7], *mats),
        [(xs.shape[0], 3) + xs.shape[2:], nat, nat, nat],
        [saved, saved, (nat[0], 5) + nat[1:], pltpu.SemaphoreType.DMA((nat[0] + 1,))],
        LIMIT["middle"], cost(3200, 18), "slab_middle",
    )


def adjoint_kernel(qw, bk, gx0, gx1, gm, tm, out, f_s, ux, p_s, bx_s, ms):
    split_mats(gm, tm, ms)
    n, nz = qw.shape[0], qw.shape[4]
    lanes = [slice(0, nz // 2), slice(nz // 2, nz)]

    for g in range(2):
        for h in range(2):
            unpack(qw[:, g, h], f_s.at[g], 2 * h)
        t = swap(qw[:, g, 2])
        for xl in range(4):
            ux[2 * g : 2 * g + 2, xl * n : (xl + 1) * n, :] = t[2 * xl : 2 * xl + 2]

    at = [(g, yl) for g in range(2) for yl in range(2)]
    ax = [left(ms, G, f_s[g, yl]) for g, yl in at]
    ax = [ux[j] + v for j, v in enumerate(ax)]
    back = [left(ms, T, bk[yl] * v) for (g, yl), v in zip(at, ax)]
    p0 = [f_s[g, 2 + yl] - DT * v for (g, yl), v in zip(at, back)]
    gq = [left(ms, G, (DT * bk[2 + yl]) * v) for (g, yl), v in zip(at, p0)]
    bx = [gx1[j] * ax[j] + gx0[j] * (ax[j] + gq[j]) for j in range(4)]
    for j in range(4):
        p_s[j] = p0[j]
    for yl in range(2):
        bx_s[yl] = bx[yl] + bx[2 + yl]

    for g in range(2):
        for zh, z in enumerate(lanes):
            v = [p_s[2 * g : 2 * g + 2, xl * n : (xl + 1) * n, z] for xl in range(4)]
            out[:, g, 8 * zh : 8 * zh + 8, :] = swap(jnp.concatenate(v, axis=0))

    for e in range(2):
        v = [bx_s[:, (2 * e + xm) * n : (2 * e + xm + 1) * n, z] for z in lanes for xm in range(2)]
        out[:, e, 16:24, :] = swap(jnp.concatenate(v, axis=0))


def adjoint_call(qw, bk, gx0, gx1, mats):
    ns, _, _, _, nz = qw.shape
    nx = 4 * ns
    return on_chip(
        adjoint_kernel, (), (qw, bk, gx0, gx1, *mats), [(ns, 2, 24, nz // 2)],
        [(2, 4, nx, nz), (4, nx, nz), (4, nx, nz), (2, nx, nz)], LIMIT["adjoint"], cost(1200, 9), "lines_adjoint",
    )[0]


def last_kernel(ids, xs, d0, t1, t2, gy0, gz0, dk, gm, tm, out, p_s, bx_s, ms):
    split_mats(gm, tm, ms)
    nx, ny, nz = d0.shape
    half = nz // 2
    t = swap(xs[:, 16:24, :]).reshape(4, ny, half)
    for zh in range(2):
        z = slice(zh * half, (zh + 1) * half)
        p_s[:, :, z] = swap(xs[:, 8 * zh : 8 * zh + 8, :]).reshape(nx, ny, half)
        bx_s[:, :, z] = t[2 * zh : 2 * zh + 2]

    q = [dk[i] * p_s[i] for i in range(nx)]
    gy = [left(ms, G, v) for v in q]
    gz = [right(v, ms, T) for v in q]
    for i in range(nx):
        out[0, i] = t1[i] + d0[i] * p_s[i]
        out[1, i] = t2[i] + gy0[i] * gy[i] + gz0[i] * gz[i]

    for xm in range(2):
        out[1, 2 * ids[0] + xm] += bx_s[xm]


def last_call(ids, xs, fields, mats):
    nat = fields[0].shape
    vmem = pl.BlockSpec(memory_space=pltpu.VMEM)
    args = (xs, *fields, *mats)
    return pl.pallas_call(
        last_kernel,
        in_specs=[pl.BlockSpec(memory_space=pltpu.SMEM)] + [vmem] * len(args),
        out_specs=vmem,
        out_shape=jax.ShapeDtypeStruct((2,) + nat, F32),
        scratch_shapes=[pltpu.VMEM(nat, F32), pltpu.VMEM((2,) + nat[1:], F32), mats_scratch(mats)],
        compiler_params=pltpu.CompilerParams(vmem_limit_bytes=LIMIT["last"] * MIB),
        cost_estimate=cost(800, 9),
        name="slab_last",
    )(ids, *args)


def change_layout(v):
    return lax.all_to_all(v, ALL, split_axis=0, concat_axis=0, tiled=True)


def swap_groups(v):
    return lax.ppermute(v, "emit", [(0, 1), (1, 0)])


def local(
    sound_speed, density, absorption, pressure_start, velocity_start, adjoint_pressure,
    adjoint_velocity, emitter_voxel, emitter_delay, drive_waveform_samples, recorded_pressures,
    sensor_flat_position,
):
    n_emit, n_slab = lax.axis_size("emit"), lax.axis_size("slab")
    ndev = n_emit * n_slab
    planes, ny, nz = sound_speed.shape
    nx = planes * n_slab
    emit = lax.axis_index("emit")
    ids = jnp.stack([emit, lax.axis_index("slab")]).astype(jnp.int32)
    mats = pair_const(deriv_matrix(ny))
    order = (4 * np.arange(n_slab)[None, :] + np.arange(4)[:, None]).reshape(-1)
    line_mats = pair_const(deriv_matrix(nx)[np.ix_(order, order)])

    buf = start_call(
        sound_speed, density, absorption, pressure_start, velocity_start, emitter_voxel,
        emitter_delay, drive_waveform_samples, mats, ndev,
    )
    fields = prepare_call(
        ids, sound_speed, density, absorption, pressure_start, velocity_start, adjoint_pressure,
        adjoint_velocity, sensor_flat_position.reshape(1, -1), recorded_pressures, emitter_voxel,
        emitter_delay, drive_waveform_samples, mats,
    )
    lines, fields = lax.optimization_barrier((change_layout(buf), fields))
    lines = lines.reshape(n_slab, n_emit, 4, 8, nz)
    xs, gx0, gx1, bk = forward_call(lines, line_mats)
    xs = change_layout(xs.reshape(ndev, 2, 8, nz))
    qw, d0, t1, t2 = middle_call(xs, fields, mats)
    qw = change_layout(qw).reshape(n_slab, n_emit, 3, 8, nz)
    xs = adjoint_call(qw, bk, gx0, gx1, line_mats)
    xs = change_layout(xs.reshape(ndev, 24, nz // 2))
    t = last_call(ids, xs, [d0, t1, t2, fields[8], fields[9], fields[0]], mats)
    other = swap_groups(t)
    s1, s2 = t[0] + other[0], t[1] + other[1]
    b = 1.0 / density
    speed_total = (2.0 * DT) * s1 * density * sound_speed
    density_total = DT * (s1 * sound_speed * sound_speed + s2 * b * b)
    return speed_total, density_total


def solution(mesh):
    in_specs = (
        P("slab", None, None), P("slab", None, None), P("slab", None, None),
        P("emit", "slab", None, None), P("emit", None, "slab", None, None),
        P("emit", "slab", None, None), P("emit", None, "slab", None, None),
        P("emit", None), P("emit", None), P(), P("emit", None, None), P(),
    )
    out_specs = (P("slab", None, None), P("slab", None, None))
    return jax.shard_map(local, mesh=mesh, in_specs=in_specs, out_specs=out_specs, check_vma=False)
```

```python
import numpy as np
import jax
import jax.numpy as jnp
from jax import lax
from jax.experimental import pallas as pl
from jax.experimental.pallas import tpu as pltpu
from jax.sharding import PartitionSpec as P

STEPS = 2
DT = 0.2
F32 = jnp.float32
BF16 = jnp.bfloat16
ALL = ("slab", "emit")
MIB = 2**20
LIMIT = {"start": 60, "prepare": 60, "forward": 24, "middle": 40, "adjoint": 20, "last": 20}


def deriv_matrix(n):
    k = np.arange(1, n // 2, dtype=np.int64)
    pts = np.arange(n, dtype=np.int64)
    shifted = (k[None, :] * (2 * pts[:, None] + 1)) % (2 * n) * (np.pi / n)
    plain = (k[None, :] * (2 * pts[:, None])) % (2 * n) * (np.pi / n)
    w = k * (2.0 * np.pi / n)
    m = (np.cos(shifted) * w) @ np.sin(plain).T - (np.sin(shifted) * w) @ np.cos(plain).T
    return m * (2.0 / n)


def pair_const(m):
    m = m.astype(np.float32)
    return [jnp.asarray(m), jnp.asarray(np.ascontiguousarray(m.T))]


def split2(v):
    hi = v.astype(BF16)
    return hi, (v - hi.astype(F32)).astype(BF16)


def split3(v):
    hi = v.astype(BF16)
    rest = v - hi.astype(F32)
    mid = rest.astype(BF16)
    return hi, mid, (rest - mid.astype(F32)).astype(BF16)


def dot(a, b):
    return jnp.dot(a, b, preferred_element_type=F32)


def split_mats(gm, tm, ms):
    for k, m in enumerate((gm, tm)):
        ms[2 * k], ms[2 * k + 1] = split2(m[...])


G, T = 0, 2


def left(ms, k, v):
    h, l = split2(v)
    return dot(ms[k], h) + (dot(ms[k], l) + dot(ms[k + 1], h))


def right(v, ms, k):
    h, l = split2(v)
    return dot(h, ms[k]) + (dot(l, ms[k]) + dot(h, ms[k + 1]))


def mats_scratch(mats):
    return pltpu.VMEM((4,) + mats[0].shape, BF16)


def params(mib, n_grid=1):
    return pltpu.CompilerParams(
        dimension_semantics=("arbitrary",) * n_grid, vmem_limit_bytes=mib * MIB
    )


def cost(mflop, mib):
    return pl.CostEstimate(flops=mflop * 10**6, bytes_accessed=mib * MIB, transcendentals=0)


def swap(v):
    return jnp.swapaxes(v, 0, 1)


def whole(shape):
    return pl.BlockSpec(shape, lambda i, ids: (0,) * len(shape))


def group_plane(shape, pick, a=0):
    block = (None,) * (len(shape) - 3) + (1,) + shape[-2:]
    return pl.BlockSpec(block, lambda i, ids: (0, a)[: len(shape) - 3] + (pick(i, ids), 0, 0))


def plane_onehot(pos, plane, ny, nz):
    local = pos - plane * (ny * nz)
    y = lax.broadcasted_iota(jnp.int32, (ny, pos.shape[1]), 0) * nz
    return jnp.where((local >= y) & (local < y + nz), 1.0, 0.0).astype(BF16)


def column_onehot(pos, nz):
    z = lax.broadcasted_iota(jnp.int32, (nz, pos.shape[1]), 0)
    return lax.rem(pos, nz) == z


def drive_at(delay, drive, step):
    amp = jnp.zeros(delay.shape, F32)
    for k in range(drive.shape[0]):
        amp = jnp.where(delay + step == k, drive[k], amp)
    return amp


def three(onehot, value):
    parts = [jnp.where(onehot, v.astype(F32), 0.0) for v in split3(value)]
    return jnp.concatenate(parts, axis=1).T.astype(BF16)


def spread(rows, cols):
    return dot(jnp.concatenate([rows] * 3, axis=1), cols)


def first_step(planes, cols, epos, numbers, ms):
    ny, nz = planes[0][0].shape
    c, rho, alpha, p, uy, uz = zip(*planes)
    at = range(len(planes))
    gy = [left(ms, G, v) for v in p]
    gz = [right(v, ms, T) for v in p]
    b = [1.0 / v for v in rho]
    bulk = [rho[k] * c[k] * c[k] for k in at]
    wy = [uy[k] - DT * b[k] * gy[k] for k in at]
    wz = [uz[k] - DT * b[k] * gz[k] for k in at]
    yz = [left(ms, T, v) for v in wy]
    zz = [right(v, ms, G) for v in wz]
    shot = [spread(plane_onehot(epos[...], n, ny, nz), cols[...]) for n in numbers]
    yz = [yz[k] + zz[k] for k in at]
    v0 = [(1.0 - DT * alpha[k]) * p[k] + (DT * bulk[k]) * yz[k] + shot[k] for k in at]
    return list(zip(gy, gz, wy, wz, yz, v0, b, bulk))


def plane_copies(srcs, dst, sems, i):
    return [
        pltpu.make_async_copy(src.at[pl.ds(i, 1)], dst.at[i, pl.ds(k, 1)], sems.at[i, k])
        for k, src in enumerate(srcs)
    ]


def start_kernel(
    drive, c, rho, alpha, p0, u, epos, delay, gm, tm, buf, ins, sems, outs, out_sems, cols, pack, ms
):
    emit, slab = lax.axis_index("emit"), lax.axis_index("slab")
    nx, ny, nz = c.shape
    half = ny // 2

    def send(i):
        return pltpu.make_async_copy(outs.at[i], buf.at[:, i], out_sems.at[i])

    srcs = (p0.at[0], c, rho, alpha, u.at[0, 1], u.at[0, 2], u.at[0, 0])
    for fields in (slice(0, 6), slice(6, 7)):
        for i in range(nx):
            for copy in plane_copies(srcs, ins, sems, i)[fields]:
                copy.start()
    split_mats(gm, tm, ms)
    cols[...] = three(column_onehot(epos[...], nz), drive_at(delay[...], drive, 0))

    @pl.loop(0, nx // 2)
    def _(k):
        pair = (2 * k, 2 * k + 1)
        for i in pair:
            for copy in plane_copies(srcs, ins, sems, i)[:6]:
                copy.wait()
        steps = first_step(
            [tuple(ins[i, f] for f in (1, 2, 3, 0, 4, 5)) for i in pair],
            cols, epos, [slab * nx + i for i in pair], ms,
        )
        for xm, i in enumerate(pair):
            v0, b, bulk = steps[xm][5:]
            for copy in plane_copies(srcs, ins, sems, i)[6:]:
                copy.wait()
            for f, field in enumerate((ins[i, 0], ins[i, 6], v0, jnp.where(emit == 0, b, bulk))):
                pack[xm, 2 * f : 2 * f + 2] = field.reshape(2, half, nz)
            outs[i] = swap(pack[xm])
            send(i).start()

    for i in range(nx):
        send(i).wait()


def start_call(c, rho, alpha, p0, u, epos, delay, drive, mats, ndev):
    nx, ny, nz = c.shape
    n_e = epos.shape[1]
    hbm, vmem, smem = (pl.BlockSpec(memory_space=m) for m in (pltpu.HBM, pltpu.VMEM, pltpu.SMEM))
    return pl.pallas_call(
        start_kernel,
        in_specs=[smem] + [hbm] * 5 + [vmem] * 4,
        out_specs=hbm,
        out_shape=jax.ShapeDtypeStruct((ndev, nx, 8, nz), F32),
        scratch_shapes=[pltpu.VMEM((nx, 7, ny, nz), F32), pltpu.SemaphoreType.DMA((nx, 7)),
                        pltpu.VMEM((nx, ndev, 8, nz), F32), pltpu.SemaphoreType.DMA((nx,)),
                        pltpu.VMEM((3 * n_e, nz), BF16),
                        pltpu.VMEM((2, 8, ndev, nz), F32), mats_scratch(mats)],
        compiler_params=pltpu.CompilerParams(vmem_limit_bytes=LIMIT["start"] * MIB),
        cost_estimate=cost(2000, 13),
        name="start",
    )(drive, c, rho, alpha, p0, u, epos, delay, *mats)


def prepare_kernel(
    ids, drive, c, rho, alpha, p0, uy, uz, pa, ax, ay, az, spos, rec, epos, delay, gm, tm,
    dk, stay, b, pm, cdk, wb, yz1, late, gy0, gz0, axs, ones, scols, ecols, pack, ms,
):
    i = pl.program_id(0)
    ny, nz = c.shape[1], c.shape[2]

    @pl.when(i == 0)
    def _():
        split_mats(gm, tm, ms)
        oh = column_onehot(spos[...], nz)
        ones[...] = jnp.where(oh, 1.0, 0.0).T.astype(BF16)
        for step in range(STEPS):
            scols[step] = three(oh, rec[step : step + 1])
        for step in range(STEPS):
            ecols[step] = three(column_onehot(epos[...], nz), drive_at(delay[...], drive, step))

    plane = ids[1] * 4 + i
    gy, gz, u1y, u1z, yz0, v0, buoy, bulk = first_step(
        [(c[0], rho[0], alpha[0], p0[0], uy[0], uz[0])], ecols.at[0], epos, [plane], ms
    )[0]
    keep = 1.0 - DT * alpha[0]
    s = plane_onehot(spos[...], plane, ny, nz)
    count = dot(s, ones[...])
    m0 = spread(s, scols[0])
    m1 = spread(s, scols[1])
    shot = spread(plane_onehot(epos[...], plane, ny, nz), ecols[1])
    gyv = left(ms, G, v0)
    gzv = right(v0, ms, T)
    db = DT * buoy
    yz = left(ms, T, u1y - db * gyv) + right(u1z - db * gzv, ms, G)
    back = left(ms, T, buoy * ay[0]) + right(buoy * az[0], ms, G)
    dk[0] = DT * bulk
    stay[0] = keep
    b[0] = buoy
    cdk[0] = count * (DT * bulk)
    pm[0] = pa[0] + (count * (keep * v0 + (DT * bulk) * yz + shot) - m1)
    wb[0] = (count * v0 - m0) - DT * back
    yz1[0] = yz
    for k, field in enumerate((yz0, gy + gyv, gz + gzv, ay[0], az[0])):
        late[0, k] = field
    gy0[0] = gy
    gz0[0] = gz
    pack[pl.ds(2 * i, 2)] = ax[0].reshape(2, ny // 2, nz)

    @pl.when(i == pl.num_programs(0) - 1)
    def _():
        axs[...] = swap(pack[...])


def prepare_call(
    ids, c, rho, alpha, p0, u, pa, v, spos, rec, epos, delay, drive, mats
):
    nx, ny, nz = c.shape
    n_e, n_s = epos.shape[1], spos.shape[1]
    pick = lambda i, ids: i
    plane = group_plane(c.shape, pick)
    return pl.pallas_call(
        prepare_kernel,
        grid_spec=pltpu.PrefetchScalarGridSpec(
            num_scalar_prefetch=1,
            grid=(nx,),
            in_specs=[pl.BlockSpec(memory_space=pltpu.SMEM)] + [plane] * 3
            + [group_plane(p0.shape, pick)] + [group_plane(u.shape, pick, a) for a in (1, 2)]
            + [group_plane(pa.shape, pick)] + [group_plane(v.shape, pick, a) for a in range(3)]
            + [whole((1, n_s)), pl.BlockSpec((None, STEPS, n_s), lambda i, ids: (0, 0, 0)),
               whole((1, n_e)), whole((1, n_e))]
            + [whole((ny, ny))] * 2,
            out_specs=[plane] * 7 + [pl.BlockSpec((1, 5, ny, nz), lambda i, ids: (i, 0, 0, 0))]
            + [plane] * 2 + [whole((ny // 2, 2 * nx, nz))],
            scratch_shapes=[pltpu.VMEM((n_s, nz), BF16), pltpu.VMEM((STEPS, 3 * n_s, nz), BF16),
                            pltpu.VMEM((STEPS, 3 * n_e, nz), BF16),
                            pltpu.VMEM((2 * nx, ny // 2, nz), F32), mats_scratch(mats)],
        ),
        out_shape=[jax.ShapeDtypeStruct(c.shape, F32)] * 7
        + [jax.ShapeDtypeStruct((nx, 5, ny, nz), F32)] + [jax.ShapeDtypeStruct(c.shape, F32)] * 2
        + [jax.ShapeDtypeStruct((ny // 2, 2 * nx, nz), F32)],
        compiler_params=params(LIMIT["prepare"]),
        cost_estimate=cost(8000, 22),
        name="prepare",
    )(ids, drive, c, rho, alpha, p0, u, u, pa, v, v, v, spos, rec, epos, delay, *mats)


def on_chip(kernel, away, args, shapes, scratch, limit, estimate, name):
    vmem = pl.BlockSpec(memory_space=pltpu.VMEM)
    return pl.pallas_call(
        kernel,
        in_specs=[pl.BlockSpec(memory_space=pltpu.HBM)] * len(away) + [vmem] * len(args),
        out_specs=[vmem] * len(shapes),
        out_shape=[jax.ShapeDtypeStruct(v, F32) for v in shapes],
        scratch_shapes=[pltpu.VMEM(v, F32) if isinstance(v, tuple) else v for v in scratch]
        + [mats_scratch(args[-2:])],
        compiler_params=pltpu.CompilerParams(vmem_limit_bytes=limit * MIB),
        cost_estimate=estimate,
        name=name,
    )(*away, *args)


def unpack(block, dst, first):
    t = swap(block)
    n = t.shape[1]
    for xm in range(2):
        dst[:, (first + xm) * n : (first + xm + 1) * n, :] = t[4 * xm : 4 * xm + 4]


def forward_kernel(lines, gm, tm, out, gx0, gx1, bk, in_s, sems, f_s, o_s, ms):
    n = lines.shape[0]
    fetch = lambda g: pltpu.make_async_copy(lines.at[:, g], in_s.at[g], sems.at[g])
    groups, at = range(2), range(4)
    for g in groups:
        fetch(g).start()
    split_mats(gm, tm, ms)
    g0, u1, x0 = [], [], []
    for g in groups:
        fetch(g).wait()
        for xl in range(4):
            rows = slice(xl * n, (xl + 1) * n)
            t = swap(in_s[g, :, xl])
            f_s[g, :, rows, :] = t[:6]
            bk[2 * g : 2 * g + 2, rows, :] = t[6:]
        g0 += [left(ms, G, f_s[g, yl]) for yl in range(2)]
        u1 += [f_s[g, 2 + yl] - (DT * bk[yl]) * g0[2 * g + yl] for yl in range(2)]
        x0 += [left(ms, T, u1[2 * g + yl]) for yl in range(2)]
    p1 = [f_s[j // 2, 4 + j % 2] + (DT * bk[2 + j % 2]) * x0[j] for j in at]
    g1 = [left(ms, G, p1[j]) for j in at]
    x1 = [left(ms, T, u1[j] - (DT * bk[j % 2]) * g1[j]) for j in at]
    for j in at:
        gx0[j] = g0[j]
        gx1[j] = g1[j]
        o_s[j // 2, j % 2] = x0[j]
        o_s[j // 2, 2 + j % 2] = x1[j]
    for g in groups:
        for h in range(2):
            both = [o_s[g, :, (2 * h + xm) * n : (2 * h + xm + 1) * n, :] for xm in range(2)]
            out[:, g, h] = swap(jnp.concatenate(both, axis=0))


def forward_call(lines, mats):
    ns, _, _, _, nz = lines.shape
    nx = 4 * ns
    full = (4, nx, nz)
    return on_chip(
        forward_kernel, (lines,), mats, [(ns, 2, 2, 8, nz), full, full, full],
        [(2, ns, 4, 8, nz), pltpu.SemaphoreType.DMA((2,)), (2, 6, nx, nz), (2, 4, nx, nz)],
        LIMIT["forward"], cost(1600, 9), "lines_forward",
    )


def middle_kernel(
    late, axs, xs, dk, stay, b, pm, cdk, wb, yz1, gm, tm,
    buf, d0, t1, t2, x_s, o_s, ins, sems, ms,
):
    nx, ny, nz = dk.shape
    fetch = lambda i: pltpu.make_async_copy(late.at[i], ins.at[i], sems.at[i])
    for i in range(nx):
        fetch(i).start()
    fetch_ax = pltpu.make_async_copy(axs, buf.at[:, 2], sems.at[nx])
    fetch_ax.start()
    split_mats(gm, tm, ms)
    for h in range(2):
        x_s[4 * h : 4 * h + 4] = swap(xs[:, h]).reshape(4, ny, nz)

    def some(planes):
        add = [dk[i] * x_s[2 * i] for i in planes]
        ey = [left(ms, G, a) for a in add]
        ez = [right(a, ms, T) for a in add]
        gy = [left(ms, T, (DT * b[i]) * e) for i, e in zip(planes, ey)]
        gz = [right((DT * b[i]) * e, ms, G) for i, e in zip(planes, ez)]
        rest = [x_s[2 * i + 1] - (e + f) for i, e, f in zip(planes, gy, gz)]
        adj = [pm[i] + cdk[i] * (stay[i] * x_s[2 * i] + r) for i, r in zip(planes, rest)]
        q = [dk[i] * a for i, a in zip(planes, adj)]
        fy = [left(ms, G, a) for a in q]
        fz = [right(a, ms, T) for a in q]
        for k, i in enumerate(planes):
            o_s[2 * i] = q[k]
            t1[i] = (yz1[i] + rest[k]) * adj[k]
        gy = [left(ms, T, b[i] * e) for i, e in zip(planes, fy)]
        gz = [right(b[i] * e, ms, G) for i, e in zip(planes, fz)]
        for k, i in enumerate(planes):
            o_s[2 * i + 1] = stay[i] * adj[k] + (cdk[i] * x_s[2 * i] + wb[i]) - DT * (gy[k] + gz[k])
            fetch(i).wait()
            d0[i] = x_s[2 * i] + ins[i, 0]
            t2[i] = (ins[i, 1] + ey[k]) * (ins[i, 3] + fy[k]) + (ins[i, 2] + ez[k]) * (ins[i, 4] + fz[k])

    some(range(nx))

    for h in range(2):
        buf[:, h] = swap(o_s[4 * h : 4 * h + 4].reshape(8, ny // 2, nz))
    fetch_ax.wait()


def middle_call(xs, fields, mats):
    nat = fields[0].shape
    saved = (8,) + nat[1:]
    return on_chip(
        middle_kernel, (fields[7], fields[10]), (xs, *fields[:7], *mats),
        [(xs.shape[0], 3) + xs.shape[2:], nat, nat, nat],
        [saved, saved, (nat[0], 5) + nat[1:], pltpu.SemaphoreType.DMA((nat[0] + 1,))],
        LIMIT["middle"], cost(3200, 18), "slab_middle",
    )


def adjoint_kernel(qw, bk, gx0, gx1, gm, tm, out, f_s, ux, p_s, bx_s, ms):
    split_mats(gm, tm, ms)
    n, nz = qw.shape[0], qw.shape[4]
    lanes = [slice(0, nz // 2), slice(nz // 2, nz)]

    for g in range(2):
        for h in range(2):
            unpack(qw[:, g, h], f_s.at[g], 2 * h)
        t = swap(qw[:, g, 2])
        for xl in range(4):
            ux[2 * g : 2 * g + 2, xl * n : (xl + 1) * n, :] = t[2 * xl : 2 * xl + 2]

    at = [(g, yl) for g in range(2) for yl in range(2)]
    ax = [left(ms, G, f_s[g, yl]) for g, yl in at]
    ax = [ux[j] + v for j, v in enumerate(ax)]
    back = [left(ms, T, bk[yl] * v) for (g, yl), v in zip(at, ax)]
    p0 = [f_s[g, 2 + yl] - DT * v for (g, yl), v in zip(at, back)]
    gq = [left(ms, G, (DT * bk[2 + yl]) * v) for (g, yl), v in zip(at, p0)]
    bx = [gx1[j] * ax[j] + gx0[j] * (ax[j] + gq[j]) for j in range(4)]
    for j in range(4):
        p_s[j] = p0[j]
    for yl in range(2):
        bx_s[yl] = bx[yl] + bx[2 + yl]

    for g in range(2):
        for zh, z in enumerate(lanes):
            v = [p_s[2 * g : 2 * g + 2, xl * n : (xl + 1) * n, z] for xl in range(4)]
            out[:, g, 8 * zh : 8 * zh + 8, :] = swap(jnp.concatenate(v, axis=0))

    for e in range(2):
        v = [bx_s[:, (2 * e + xm) * n : (2 * e + xm + 1) * n, z] for z in lanes for xm in range(2)]
        out[:, e, 16:24, :] = swap(jnp.concatenate(v, axis=0))


def adjoint_call(qw, bk, gx0, gx1, mats):
    ns, _, _, _, nz = qw.shape
    nx = 4 * ns
    return on_chip(
        adjoint_kernel, (), (qw, bk, gx0, gx1, *mats), [(ns, 2, 24, nz // 2)],
        [(2, 4, nx, nz), (4, nx, nz), (4, nx, nz), (2, nx, nz)], LIMIT["adjoint"], cost(1200, 9), "lines_adjoint",
    )[0]


def last_bulk_kernel(xs, d0, t1, out, p_s):
    nx, ny, nz = d0.shape
    half = nz // 2
    for zh in range(2):
        z = slice(zh * half, (zh + 1) * half)
        p = swap(xs[:, 8 * zh : 8 * zh + 8, :]).reshape(nx, ny, half)
        p_s[:, :, z] = p
        out[:, :, z] = t1[:, :, z] + d0[:, :, z] * p


def last_buoy_kernel(ids, xs, p_s, t2, gy0, gz0, dk, gm, tm, out, bx_s, ms):
    split_mats(gm, tm, ms)
    nx, ny, nz = t2.shape
    half = nz // 2
    t = swap(xs[:, 16:24, :]).reshape(4, ny, half)
    for zh in range(2):
        bx_s[:, :, zh * half : (zh + 1) * half] = t[2 * zh : 2 * zh + 2]
    q = [dk[i] * p_s[i] for i in range(nx)]
    gy = [left(ms, G, v) for v in q]
    gz = [right(v, ms, T) for v in q]
    for i in range(nx):
        out[i] = t2[i] + gy0[i] * gy[i] + gz0[i] * gz[i]
    for xm in range(2):
        out[2 * ids[0] + xm] += bx_s[xm]


def last_buoy_call(ids, xs, fields, mats):
    nat = fields[0].shape
    vmem = pl.BlockSpec(memory_space=pltpu.VMEM)
    args = (xs, *fields, *mats)
    return pl.pallas_call(
        last_buoy_kernel,
        in_specs=[pl.BlockSpec(memory_space=pltpu.SMEM)] + [vmem] * len(args),
        out_specs=vmem,
        out_shape=jax.ShapeDtypeStruct(nat, F32),
        scratch_shapes=[pltpu.VMEM((2,) + nat[1:], F32), mats_scratch(mats)],
        compiler_params=pltpu.CompilerParams(vmem_limit_bytes=LIMIT["last"] * MIB),
        cost_estimate=cost(800, 8),
        name="slab_last_buoy",
    )(ids, *args)


def speed_kernel(t1, other, c, rho, out, part, weight):
    @pl.loop(0, t1.shape[0])
    def _(i):
        s1 = DT * (t1[i] + other[i])
        b = 1.0 / rho[i]
        out[i] = 2.0 * s1 * rho[i] * c[i]
        part[i] = s1 * c[i] * c[i]
        weight[i] = DT * b * b


def density_kernel(t2, other, part, weight, out):
    @pl.loop(0, t2.shape[0])
    def _(i):
        out[i] = part[i] + (t2[i] + other[i]) * weight[i]


def finish(kernel, args, n_out, estimate, name):
    nat = args[-1].shape
    vmem = pl.BlockSpec(memory_space=pltpu.VMEM)
    return pl.pallas_call(
        kernel,
        in_specs=[vmem] * len(args),
        out_specs=[vmem] * n_out,
        out_shape=[jax.ShapeDtypeStruct(nat, F32)] * n_out,
        compiler_params=pltpu.CompilerParams(vmem_limit_bytes=LIMIT["last"] * MIB),
        cost_estimate=estimate,
        name=name,
    )(*args)


def change_layout(v):
    return lax.all_to_all(v, ALL, split_axis=0, concat_axis=0, tiled=True)


def swap_groups(v):
    return lax.ppermute(v, "emit", [(0, 1), (1, 0)])


def local(
    sound_speed, density, absorption, pressure_start, velocity_start, adjoint_pressure,
    adjoint_velocity, emitter_voxel, emitter_delay, drive_waveform_samples, recorded_pressures,
    sensor_flat_position,
):
    n_emit, n_slab = lax.axis_size("emit"), lax.axis_size("slab")
    ndev = n_emit * n_slab
    planes, ny, nz = sound_speed.shape
    nx = planes * n_slab
    emit = lax.axis_index("emit")
    ids = jnp.stack([emit, lax.axis_index("slab")]).astype(jnp.int32)
    mats = pair_const(deriv_matrix(ny))
    order = (4 * np.arange(n_slab)[None, :] + np.arange(4)[:, None]).reshape(-1)
    line_mats = pair_const(deriv_matrix(nx)[np.ix_(order, order)])

    buf = start_call(
        sound_speed, density, absorption, pressure_start, velocity_start, emitter_voxel,
        emitter_delay, drive_waveform_samples, mats, ndev,
    )
    fields = prepare_call(
        ids, sound_speed, density, absorption, pressure_start, velocity_start, adjoint_pressure,
        adjoint_velocity, sensor_flat_position.reshape(1, -1), recorded_pressures, emitter_voxel,
        emitter_delay, drive_waveform_samples, mats,
    )
    lines, fields = lax.optimization_barrier((change_layout(buf), fields))
    lines = lines.reshape(n_slab, n_emit, 4, 8, nz)
    xs, gx0, gx1, bk = forward_call(lines, line_mats)
    xs = change_layout(xs.reshape(ndev, 2, 8, nz))
    qw, d0, t1, t2 = middle_call(xs, fields, mats)
    qw = change_layout(qw).reshape(n_slab, n_emit, 3, 8, nz)
    xs = adjoint_call(qw, bk, gx0, gx1, line_mats)
    xs = change_layout(xs.reshape(ndev, 24, nz // 2))
    t1, p0 = finish(last_bulk_kernel, (xs, d0, t1), 2, cost(1, 5), "slab_last_bulk")
    t2 = last_buoy_call(ids, xs, [p0, t2, fields[8], fields[9], fields[0]], mats)
    speed_total, part, weight = finish(
        speed_kernel, (t1, swap_groups(t1), sound_speed, density), 3, cost(3, 100), "finish_speed"
    )
    (density_total,) = finish(
        density_kernel, (t2, swap_groups(t2), part, weight), 1, cost(3, 5), "finish_density"
    )
    return speed_total, density_total


def solution(mesh):
    in_specs = (
        P("slab", None, None), P("slab", None, None), P("slab", None, None),
        P("emit", "slab", None, None), P("emit", None, "slab", None, None),
        P("emit", "slab", None, None), P("emit", None, "slab", None, None),
        P("emit", None), P("emit", None), P(), P("emit", None, None), P(),
    )
    out_specs = (P("slab", None, None), P("slab", None, None))
    return jax.shard_map(local, mesh=mesh, in_specs=in_specs, out_specs=out_specs, check_vma=False)
```

```python
import numpy as np
import jax
import jax.numpy as jnp
from jax import lax
from jax.experimental import pallas as pl
from jax.experimental.pallas import tpu as pltpu
from jax.sharding import PartitionSpec as P

STEPS = 2
DT = 0.2
F32 = jnp.float32
BF16 = jnp.bfloat16
ALL = ("slab", "emit")
MIB = 2**20
LIMIT = {"start": 60, "prepare": 60, "forward": 24, "middle": 32, "adjoint": 20, "last": 20}


def deriv_matrix(n):
    k = np.arange(1, n // 2, dtype=np.int64)
    pts = np.arange(n, dtype=np.int64)
    shifted = (k[None, :] * (2 * pts[:, None] + 1)) % (2 * n) * (np.pi / n)
    plain = (k[None, :] * (2 * pts[:, None])) % (2 * n) * (np.pi / n)
    w = k * (2.0 * np.pi / n)
    m = (np.cos(shifted) * w) @ np.sin(plain).T - (np.sin(shifted) * w) @ np.cos(plain).T
    return m * (2.0 / n)


def pair_const(m):
    m = m.astype(np.float32)
    return [jnp.asarray(m), jnp.asarray(np.ascontiguousarray(m.T))]


def split2(v):
    hi = v.astype(BF16)
    return hi, (v - hi.astype(F32)).astype(BF16)


def split3(v):
    hi = v.astype(BF16)
    rest = v - hi.astype(F32)
    mid = rest.astype(BF16)
    return hi, mid, (rest - mid.astype(F32)).astype(BF16)


def dot(a, b):
    return jnp.dot(a, b, preferred_element_type=F32)


def split_mats(gm, tm, ms):
    for k, m in enumerate((gm, tm)):
        ms[2 * k], ms[2 * k + 1] = split2(m[...])


G, T = 0, 2


def left(ms, k, v):
    h, l = split2(v)
    return dot(ms[k], h) + (dot(ms[k], l) + dot(ms[k + 1], h))


def right(v, ms, k):
    h, l = split2(v)
    return dot(h, ms[k]) + (dot(l, ms[k]) + dot(h, ms[k + 1]))


def mats_scratch(mats):
    return pltpu.VMEM((4,) + mats[0].shape, BF16)


def params(mib, n_grid=1):
    return pltpu.CompilerParams(
        dimension_semantics=("arbitrary",) * n_grid, vmem_limit_bytes=mib * MIB
    )


def cost(mflop, mib):
    return pl.CostEstimate(flops=mflop * 10**6, bytes_accessed=mib * MIB, transcendentals=0)


def swap(v):
    return jnp.swapaxes(v, 0, 1)


def whole(shape):
    return pl.BlockSpec(shape, lambda i, ids: (0,) * len(shape))


def group_plane(shape, pick, a=0):
    block = (None,) * (len(shape) - 3) + (1,) + shape[-2:]
    return pl.BlockSpec(block, lambda i, ids: (0, a)[: len(shape) - 3] + (pick(i, ids), 0, 0))


def plane_onehot(pos, plane, ny, nz):
    local = pos - plane * (ny * nz)
    y = lax.broadcasted_iota(jnp.int32, (ny, pos.shape[1]), 0) * nz
    return jnp.where((local >= y) & (local < y + nz), 1.0, 0.0).astype(BF16)


def column_onehot(pos, nz):
    z = lax.broadcasted_iota(jnp.int32, (nz, pos.shape[1]), 0)
    return lax.rem(pos, nz) == z


def drive_at(delay, drive, step):
    amp = jnp.zeros(delay.shape, F32)
    for k in range(drive.shape[0]):
        amp = jnp.where(delay + step == k, drive[k], amp)
    return amp


def three(onehot, value):
    parts = [jnp.where(onehot, v.astype(F32), 0.0) for v in split3(value)]
    return jnp.concatenate(parts, axis=1).T.astype(BF16)


def spread(rows, cols):
    return dot(jnp.concatenate([rows] * 3, axis=1), cols)


def first_step(planes, cols, epos, numbers, ms):
    ny, nz = planes[0][0].shape
    c, rho, alpha, p, uy, uz = zip(*planes)
    at = range(len(planes))
    gy = [left(ms, G, v) for v in p]
    gz = [right(v, ms, T) for v in p]
    b = [1.0 / v for v in rho]
    bulk = [rho[k] * c[k] * c[k] for k in at]
    wy = [uy[k] - DT * b[k] * gy[k] for k in at]
    wz = [uz[k] - DT * b[k] * gz[k] for k in at]
    yz = [left(ms, T, v) for v in wy]
    zz = [right(v, ms, G) for v in wz]
    shot = [spread(plane_onehot(epos[...], n, ny, nz), cols[...]) for n in numbers]
    yz = [yz[k] + zz[k] for k in at]
    v0 = [(1.0 - DT * alpha[k]) * p[k] + (DT * bulk[k]) * yz[k] + shot[k] for k in at]
    return list(zip(gy, gz, wy, wz, yz, v0, b, bulk))


def plane_copies(srcs, dst, sems, i):
    return [
        pltpu.make_async_copy(src.at[pl.ds(i, 1)], dst.at[i, pl.ds(k, 1)], sems.at[i, k])
        for k, src in enumerate(srcs)
    ]


def start_kernel(
    drive, c, rho, alpha, p0, u, epos, delay, gm, tm, buf, ins, sems, outs, out_sems, cols, pack, ms
):
    emit, slab = lax.axis_index("emit"), lax.axis_index("slab")
    nx, ny, nz = c.shape
    half = ny // 2

    def send(i):
        return pltpu.make_async_copy(outs.at[i], buf.at[:, i], out_sems.at[i])

    srcs = (p0.at[0], c, rho, alpha, u.at[0, 1], u.at[0, 2], u.at[0, 0])
    for fields in (slice(0, 6), slice(6, 7)):
        for i in range(nx):
            for copy in plane_copies(srcs, ins, sems, i)[fields]:
                copy.start()
    split_mats(gm, tm, ms)
    cols[...] = three(column_onehot(epos[...], nz), drive_at(delay[...], drive, 0))

    @pl.loop(0, nx // 2)
    def _(k):
        pair = (2 * k, 2 * k + 1)
        for i in pair:
            for copy in plane_copies(srcs, ins, sems, i)[:6]:
                copy.wait()
        steps = first_step(
            [tuple(ins[i, f] for f in (1, 2, 3, 0, 4, 5)) for i in pair],
            cols, epos, [slab * nx + i for i in pair], ms,
        )
        for xm, i in enumerate(pair):
            v0, b, bulk = steps[xm][5:]
            for copy in plane_copies(srcs, ins, sems, i)[6:]:
                copy.wait()
            for f, field in enumerate((ins[i, 0], ins[i, 6], v0, jnp.where(emit == 0, b, bulk))):
                pack[xm, 2 * f : 2 * f + 2] = field.reshape(2, half, nz)
            outs[i] = swap(pack[xm])
            send(i).start()

    for i in range(nx):
        send(i).wait()


def start_call(c, rho, alpha, p0, u, epos, delay, drive, mats, ndev):
    nx, ny, nz = c.shape
    n_e = epos.shape[1]
    hbm, vmem, smem = (pl.BlockSpec(memory_space=m) for m in (pltpu.HBM, pltpu.VMEM, pltpu.SMEM))
    return pl.pallas_call(
        start_kernel,
        in_specs=[smem] + [hbm] * 5 + [vmem] * 4,
        out_specs=hbm,
        out_shape=jax.ShapeDtypeStruct((ndev, nx, 8, nz), F32),
        scratch_shapes=[pltpu.VMEM((nx, 7, ny, nz), F32), pltpu.SemaphoreType.DMA((nx, 7)),
                        pltpu.VMEM((nx, ndev, 8, nz), F32), pltpu.SemaphoreType.DMA((nx,)),
                        pltpu.VMEM((3 * n_e, nz), BF16),
                        pltpu.VMEM((2, 8, ndev, nz), F32), mats_scratch(mats)],
        compiler_params=pltpu.CompilerParams(vmem_limit_bytes=LIMIT["start"] * MIB),
        cost_estimate=cost(2000, 13),
        name="start",
    )(drive, c, rho, alpha, p0, u, epos, delay, *mats)


def prepare_kernel(
    ids, drive, c, rho, alpha, p0, uy, uz, pa, ax, ay, az, spos, rec, epos, delay, gm, tm,
    dk, stay, b, pm, cdk, wb, yz1, yz0_out, late, gy0, gz0, axs, ones, scols, ecols, pack, ms,
):
    i = pl.program_id(0)
    ny, nz = c.shape[1], c.shape[2]

    @pl.when(i == 0)
    def _():
        split_mats(gm, tm, ms)
        oh = column_onehot(spos[...], nz)
        ones[...] = jnp.where(oh, 1.0, 0.0).T.astype(BF16)
        for step in range(STEPS):
            scols[step] = three(oh, rec[step : step + 1])
        for step in range(STEPS):
            ecols[step] = three(column_onehot(epos[...], nz), drive_at(delay[...], drive, step))

    plane = ids[1] * 4 + i
    gy, gz, u1y, u1z, yz0, v0, buoy, bulk = first_step(
        [(c[0], rho[0], alpha[0], p0[0], uy[0], uz[0])], ecols.at[0], epos, [plane], ms
    )[0]
    keep = 1.0 - DT * alpha[0]
    s = plane_onehot(spos[...], plane, ny, nz)
    count = dot(s, ones[...])
    m0 = spread(s, scols[0])
    m1 = spread(s, scols[1])
    shot = spread(plane_onehot(epos[...], plane, ny, nz), ecols[1])
    gyv = left(ms, G, v0)
    gzv = right(v0, ms, T)
    db = DT * buoy
    yz = left(ms, T, u1y - db * gyv) + right(u1z - db * gzv, ms, G)
    back = left(ms, T, buoy * ay[0]) + right(buoy * az[0], ms, G)
    dk[0] = DT * bulk
    stay[0] = keep
    b[0] = buoy
    cdk[0] = count * (DT * bulk)
    pm[0] = pa[0] + (count * (keep * v0 + (DT * bulk) * yz + shot) - m1)
    wb[0] = (count * v0 - m0) - DT * back
    yz1[0] = yz
    yz0_out[0] = yz0
    for k, field in enumerate((gy + gyv, gz + gzv, ay[0], az[0])):
        late[0, k] = field
    gy0[0] = gy
    gz0[0] = gz
    pack[pl.ds(2 * i, 2)] = ax[0].reshape(2, ny // 2, nz)

    @pl.when(i == pl.num_programs(0) - 1)
    def _():
        axs[...] = swap(pack[...])


def prepare_call(
    ids, c, rho, alpha, p0, u, pa, v, spos, rec, epos, delay, drive, mats
):
    nx, ny, nz = c.shape
    n_e, n_s = epos.shape[1], spos.shape[1]
    pick = lambda i, ids: i
    plane = group_plane(c.shape, pick)
    return pl.pallas_call(
        prepare_kernel,
        grid_spec=pltpu.PrefetchScalarGridSpec(
            num_scalar_prefetch=1,
            grid=(nx,),
            in_specs=[pl.BlockSpec(memory_space=pltpu.SMEM)] + [plane] * 3
            + [group_plane(p0.shape, pick)] + [group_plane(u.shape, pick, a) for a in (1, 2)]
            + [group_plane(pa.shape, pick)] + [group_plane(v.shape, pick, a) for a in range(3)]
            + [whole((1, n_s)), pl.BlockSpec((None, STEPS, n_s), lambda i, ids: (0, 0, 0)),
               whole((1, n_e)), whole((1, n_e))]
            + [whole((ny, ny))] * 2,
            out_specs=[plane] * 8 + [pl.BlockSpec((1, 4, ny, nz), lambda i, ids: (i, 0, 0, 0))]
            + [plane] * 2 + [whole((ny // 2, 2 * nx, nz))],
            scratch_shapes=[pltpu.VMEM((n_s, nz), BF16), pltpu.VMEM((STEPS, 3 * n_s, nz), BF16),
                            pltpu.VMEM((STEPS, 3 * n_e, nz), BF16),
                            pltpu.VMEM((2 * nx, ny // 2, nz), F32), mats_scratch(mats)],
        ),
        out_shape=[jax.ShapeDtypeStruct(c.shape, F32)] * 8
        + [jax.ShapeDtypeStruct((nx, 4, ny, nz), F32)] + [jax.ShapeDtypeStruct(c.shape, F32)] * 2
        + [jax.ShapeDtypeStruct((ny // 2, 2 * nx, nz), F32)],
        compiler_params=params(LIMIT["prepare"]),
        cost_estimate=cost(8000, 22),
        name="prepare",
    )(ids, drive, c, rho, alpha, p0, u, u, pa, v, v, v, spos, rec, epos, delay, *mats)


def on_chip(kernel, away, args, shapes, scratch, limit, estimate, name):
    vmem = pl.BlockSpec(memory_space=pltpu.VMEM)
    return pl.pallas_call(
        kernel,
        in_specs=[pl.BlockSpec(memory_space=pltpu.HBM)] * len(away) + [vmem] * len(args),
        out_specs=[vmem] * len(shapes),
        out_shape=[jax.ShapeDtypeStruct(v, F32) for v in shapes],
        scratch_shapes=[pltpu.VMEM(v, F32) if isinstance(v, tuple) else v for v in scratch]
        + [mats_scratch(args[-2:])],
        compiler_params=pltpu.CompilerParams(vmem_limit_bytes=limit * MIB),
        cost_estimate=estimate,
        name=name,
    )(*away, *args)


def unpack(block, dst, first):
    t = swap(block)
    n = t.shape[1]
    for xm in range(2):
        dst[:, (first + xm) * n : (first + xm + 1) * n, :] = t[4 * xm : 4 * xm + 4]


def forward_kernel(lines, gm, tm, out, gx0, gx1, bk, in_s, sems, f_s, o_s, ms):
    n = lines.shape[0]
    fetch = lambda g: pltpu.make_async_copy(lines.at[:, g], in_s.at[g], sems.at[g])
    groups, at = range(2), range(4)
    for g in groups:
        fetch(g).start()
    split_mats(gm, tm, ms)
    g0, u1, x0 = [], [], []
    for g in groups:
        fetch(g).wait()
        for xl in range(4):
            rows = slice(xl * n, (xl + 1) * n)
            t = swap(in_s[g, :, xl])
            f_s[g, :, rows, :] = t[:6]
            bk[2 * g : 2 * g + 2, rows, :] = t[6:]
        g0 += [left(ms, G, f_s[g, yl]) for yl in range(2)]
        u1 += [f_s[g, 2 + yl] - (DT * bk[yl]) * g0[2 * g + yl] for yl in range(2)]
        x0 += [left(ms, T, u1[2 * g + yl]) for yl in range(2)]
    p1 = [f_s[j // 2, 4 + j % 2] + (DT * bk[2 + j % 2]) * x0[j] for j in at]
    g1 = [left(ms, G, p1[j]) for j in at]
    x1 = [left(ms, T, u1[j] - (DT * bk[j % 2]) * g1[j]) for j in at]
    for j in at:
        gx0[j] = g0[j]
        gx1[j] = g1[j]
        o_s[j // 2, j % 2] = x0[j]
        o_s[j // 2, 2 + j % 2] = x1[j]
    for g in groups:
        for h in range(2):
            both = [o_s[g, :, (2 * h + xm) * n : (2 * h + xm + 1) * n, :] for xm in range(2)]
            out[:, g, h] = swap(jnp.concatenate(both, axis=0))


def forward_call(lines, mats):
    ns, _, _, _, nz = lines.shape
    nx = 4 * ns
    full = (4, nx, nz)
    return on_chip(
        forward_kernel, (lines,), mats, [(ns, 2, 2, 8, nz), full, full, full],
        [(2, ns, 4, 8, nz), pltpu.SemaphoreType.DMA((2,)), (2, 6, nx, nz), (2, 4, nx, nz)],
        LIMIT["forward"], cost(1600, 9), "lines_forward",
    )


def middle_kernel(
    axs, xs, dk, stay, b, pm, cdk, wb, yz1, yz0, gm, tm, buf, d0, t1, x_s, o_s, sem, ms
):
    nx, ny, nz = dk.shape
    fetch_ax = pltpu.make_async_copy(axs, buf.at[:, 2], sem)
    fetch_ax.start()
    split_mats(gm, tm, ms)
    for h in range(2):
        x_s[4 * h : 4 * h + 4] = swap(xs[:, h]).reshape(4, ny, nz)

    at = range(nx)
    add = [dk[i] * x_s[2 * i] for i in at]
    ey = [left(ms, G, a) for a in add]
    ez = [right(a, ms, T) for a in add]
    gy = [left(ms, T, (DT * b[i]) * ey[i]) for i in at]
    gz = [right((DT * b[i]) * ez[i], ms, G) for i in at]
    rest = [x_s[2 * i + 1] - (gy[i] + gz[i]) for i in at]
    adj = [pm[i] + cdk[i] * (stay[i] * x_s[2 * i] + rest[i]) for i in at]
    q = [dk[i] * adj[i] for i in at]
    fy = [left(ms, G, a) for a in q]
    fz = [right(a, ms, T) for a in q]
    for i in at:
        o_s[2 * i] = q[i]
        t1[i] = (yz1[i] + rest[i]) * adj[i]
        d0[i] = x_s[2 * i] + yz0[i]
    gy = [left(ms, T, b[i] * fy[i]) for i in at]
    gz = [right(b[i] * fz[i], ms, G) for i in at]
    for i in at:
        o_s[2 * i + 1] = stay[i] * adj[i] + (cdk[i] * x_s[2 * i] + wb[i]) - DT * (gy[i] + gz[i])

    for h in range(2):
        buf[:, h] = swap(o_s[4 * h : 4 * h + 4].reshape(8, ny // 2, nz))
    fetch_ax.wait()


def middle_call(xs, fields, mats):
    nat = fields[0].shape
    saved = (2 * nat[0],) + nat[1:]
    return on_chip(
        middle_kernel, (fields[11],), (xs, *fields[:8], *mats),
        [(xs.shape[0], 3) + xs.shape[2:], nat, nat, saved, saved],
        [pltpu.SemaphoreType.DMA], LIMIT["middle"], cost(3200, 18), "slab_middle",
    )


def adjoint_kernel(qw, bk, gx0, gx1, gm, tm, out, f_s, ux, p_s, bx_s, ms):
    split_mats(gm, tm, ms)
    n, nz = qw.shape[0], qw.shape[4]
    lanes = [slice(0, nz // 2), slice(nz // 2, nz)]

    for g in range(2):
        for h in range(2):
            unpack(qw[:, g, h], f_s.at[g], 2 * h)
        t = swap(qw[:, g, 2])
        for xl in range(4):
            ux[2 * g : 2 * g + 2, xl * n : (xl + 1) * n, :] = t[2 * xl : 2 * xl + 2]

    at = [(g, yl) for g in range(2) for yl in range(2)]
    ax = [left(ms, G, f_s[g, yl]) for g, yl in at]
    ax = [ux[j] + v for j, v in enumerate(ax)]
    back = [left(ms, T, bk[yl] * v) for (g, yl), v in zip(at, ax)]
    p0 = [f_s[g, 2 + yl] - DT * v for (g, yl), v in zip(at, back)]
    gq = [left(ms, G, (DT * bk[2 + yl]) * v) for (g, yl), v in zip(at, p0)]
    bx = [gx1[j] * ax[j] + gx0[j] * (ax[j] + gq[j]) for j in range(4)]
    for j in range(4):
        p_s[j] = p0[j]
    for yl in range(2):
        bx_s[yl] = bx[yl] + bx[2 + yl]

    for g in range(2):
        for zh, z in enumerate(lanes):
            v = [p_s[2 * g : 2 * g + 2, xl * n : (xl + 1) * n, z] for xl in range(4)]
            out[:, g, 8 * zh : 8 * zh + 8, :] = swap(jnp.concatenate(v, axis=0))

    for e in range(2):
        v = [bx_s[:, (2 * e + xm) * n : (2 * e + xm + 1) * n, z] for z in lanes for xm in range(2)]
        out[:, e, 16:24, :] = swap(jnp.concatenate(v, axis=0))


def adjoint_call(qw, bk, gx0, gx1, mats):
    ns, _, _, _, nz = qw.shape
    nx = 4 * ns
    return on_chip(
        adjoint_kernel, (), (qw, bk, gx0, gx1, *mats), [(ns, 2, 24, nz // 2)],
        [(2, 4, nx, nz), (4, nx, nz), (4, nx, nz), (2, nx, nz)], LIMIT["adjoint"], cost(1200, 9), "lines_adjoint",
    )[0]


def last_bulk_kernel(xs, d0, t1, out, p_s):
    nx, ny, nz = d0.shape
    half = nz // 2
    for zh in range(2):
        z = slice(zh * half, (zh + 1) * half)
        p = swap(xs[:, 8 * zh : 8 * zh + 8, :]).reshape(nx, ny, half)
        p_s[:, :, z] = p
        out[:, :, z] = t1[:, :, z] + d0[:, :, z] * p


def last_buoy_kernel(ids, xs, p_s, dk, gy0, gz0, x_s, o_s, late, gm, tm, out, bx_s, ms):
    split_mats(gm, tm, ms)
    nx, ny, nz = dk.shape
    half = nz // 2
    t = swap(xs[:, 16:24, :]).reshape(4, ny, half)
    for zh in range(2):
        bx_s[:, :, zh * half : (zh + 1) * half] = t[2 * zh : 2 * zh + 2]

    @pl.loop(0, nx)
    def _(i):
        add = dk[i] * x_s[2 * i]
        q1 = o_s[2 * i]
        q0 = dk[i] * p_s[i]
        ey, fy, gy = (left(ms, G, v) for v in (add, q1, q0))
        ez, fz, gz = (right(v, ms, T) for v in (add, q1, q0))
        late_y = (late[i, 0] + ey) * (late[i, 2] + fy) + gy0[i] * gy
        out[i] = late_y + (late[i, 1] + ez) * (late[i, 3] + fz) + gz0[i] * gz

    for xm in range(2):
        out[2 * ids[0] + xm] += bx_s[xm]


def last_buoy_call(ids, xs, fields, mats):
    nat = fields[0].shape
    vmem = pl.BlockSpec(memory_space=pltpu.VMEM)
    args = (xs, *fields, *mats)
    return pl.pallas_call(
        last_buoy_kernel,
        in_specs=[pl.BlockSpec(memory_space=pltpu.SMEM)] + [vmem] * len(args),
        out_specs=vmem,
        out_shape=jax.ShapeDtypeStruct(nat, F32),
        scratch_shapes=[pltpu.VMEM((2,) + nat[1:], F32), mats_scratch(mats)],
        compiler_params=pltpu.CompilerParams(vmem_limit_bytes=LIMIT["last"] * MIB),
        cost_estimate=cost(2400, 16),
        name="slab_last_buoy",
    )(ids, *args)


def speed_kernel(t1, other, c, rho, out, part, weight):
    @pl.loop(0, t1.shape[0])
    def _(i):
        s1 = DT * (t1[i] + other[i])
        b = 1.0 / rho[i]
        out[i] = 2.0 * s1 * rho[i] * c[i]
        part[i] = s1 * c[i] * c[i]
        weight[i] = DT * b * b


def density_kernel(t2, other, part, weight, out):
    @pl.loop(0, t2.shape[0])
    def _(i):
        out[i] = part[i] + (t2[i] + other[i]) * weight[i]


def finish(kernel, args, n_out, estimate, name):
    nat = args[-1].shape
    vmem = pl.BlockSpec(memory_space=pltpu.VMEM)
    return pl.pallas_call(
        kernel,
        in_specs=[vmem] * len(args),
        out_specs=[vmem] * n_out,
        out_shape=[jax.ShapeDtypeStruct(nat, F32)] * n_out,
        compiler_params=pltpu.CompilerParams(vmem_limit_bytes=LIMIT["last"] * MIB),
        cost_estimate=estimate,
        name=name,
    )(*args)


def change_layout(v):
    return lax.all_to_all(v, ALL, split_axis=0, concat_axis=0, tiled=True)


def swap_groups(v):
    return lax.ppermute(v, "emit", [(0, 1), (1, 0)])


def local(
    sound_speed, density, absorption, pressure_start, velocity_start, adjoint_pressure,
    adjoint_velocity, emitter_voxel, emitter_delay, drive_waveform_samples, recorded_pressures,
    sensor_flat_position,
):
    n_emit, n_slab = lax.axis_size("emit"), lax.axis_size("slab")
    ndev = n_emit * n_slab
    planes, ny, nz = sound_speed.shape
    nx = planes * n_slab
    emit = lax.axis_index("emit")
    ids = jnp.stack([emit, lax.axis_index("slab")]).astype(jnp.int32)
    mats = pair_const(deriv_matrix(ny))
    order = (4 * np.arange(n_slab)[None, :] + np.arange(4)[:, None]).reshape(-1)
    line_mats = pair_const(deriv_matrix(nx)[np.ix_(order, order)])

    buf = start_call(
        sound_speed, density, absorption, pressure_start, velocity_start, emitter_voxel,
        emitter_delay, drive_waveform_samples, mats, ndev,
    )
    fields = prepare_call(
        ids, sound_speed, density, absorption, pressure_start, velocity_start, adjoint_pressure,
        adjoint_velocity, sensor_flat_position.reshape(1, -1), recorded_pressures, emitter_voxel,
        emitter_delay, drive_waveform_samples, mats,
    )
    lines, fields = lax.optimization_barrier((change_layout(buf), fields))
    lines = lines.reshape(n_slab, n_emit, 4, 8, nz)
    xs, gx0, gx1, bk = forward_call(lines, line_mats)
    xs = change_layout(xs.reshape(ndev, 2, 8, nz))
    qw, d0, t1, x_s, o_s = middle_call(xs, fields, mats)
    qw = change_layout(qw).reshape(n_slab, n_emit, 3, 8, nz)
    xs = adjoint_call(qw, bk, gx0, gx1, line_mats)
    xs = change_layout(xs.reshape(ndev, 24, nz // 2))
    t1, p0 = finish(last_bulk_kernel, (xs, d0, t1), 2, cost(1, 5), "slab_last_bulk")
    t2 = last_buoy_call(
        ids, xs, [p0, fields[0], fields[9], fields[10], x_s, o_s, fields[8]], mats
    )
    speed_total, part, weight = finish(
        speed_kernel, (t1, swap_groups(t1), sound_speed, density), 3, cost(3, 100), "finish_speed"
    )
    (density_total,) = finish(
        density_kernel, (t2, swap_groups(t2), part, weight), 1, cost(3, 5), "finish_density"
    )
    return speed_total, density_total


def solution(mesh):
    in_specs = (
        P("slab", None, None), P("slab", None, None), P("slab", None, None),
        P("emit", "slab", None, None), P("emit", None, "slab", None, None),
        P("emit", "slab", None, None), P("emit", None, "slab", None, None),
        P("emit", None), P("emit", None), P(), P("emit", None, None), P(),
    )
    out_specs = (P("slab", None, None), P("slab", None, None))
    return jax.shard_map(local, mesh=mesh, in_specs=in_specs, out_specs=out_specs, check_vma=False)
```

```python
import numpy as np
import jax
import jax.numpy as jnp
from jax import lax
from jax.experimental import pallas as pl
from jax.experimental.pallas import tpu as pltpu
from jax.sharding import PartitionSpec as P

STEPS = 2
DT = 0.2
F32 = jnp.float32
BF16 = jnp.bfloat16
ALL = ("slab", "emit")
MIB = 2**20
LIMIT = {"start": 60, "prepare": 60, "forward": 24, "middle": 32, "adjoint": 20, "last": 20}


def deriv_matrix(n):
    k = np.arange(1, n // 2, dtype=np.int64)
    pts = np.arange(n, dtype=np.int64)
    shifted = (k[None, :] * (2 * pts[:, None] + 1)) % (2 * n) * (np.pi / n)
    plain = (k[None, :] * (2 * pts[:, None])) % (2 * n) * (np.pi / n)
    w = k * (2.0 * np.pi / n)
    m = (np.cos(shifted) * w) @ np.sin(plain).T - (np.sin(shifted) * w) @ np.cos(plain).T
    return m * (2.0 / n)


def pair_const(m):
    m = m.astype(np.float32)
    return [jnp.asarray(m), jnp.asarray(np.ascontiguousarray(m.T))]


def split2(v):
    hi = v.astype(BF16)
    return hi, (v - hi.astype(F32)).astype(BF16)


def split3(v):
    hi = v.astype(BF16)
    rest = v - hi.astype(F32)
    mid = rest.astype(BF16)
    return hi, mid, (rest - mid.astype(F32)).astype(BF16)


def dot(a, b):
    return jnp.dot(a, b, preferred_element_type=F32)


def split_mats(gm, tm, ms):
    for k, m in enumerate((gm, tm)):
        ms[2 * k], ms[2 * k + 1] = split2(m[...])


G, T = 0, 2


def left(ms, k, v):
    h, l = split2(v)
    return dot(ms[k], h) + (dot(ms[k], l) + dot(ms[k + 1], h))


def right(v, ms, k):
    h, l = split2(v)
    return dot(h, ms[k]) + (dot(l, ms[k]) + dot(h, ms[k + 1]))


def mats_scratch(mats):
    return pltpu.VMEM((4,) + mats[0].shape, BF16)


def params(mib, n_grid=1):
    return pltpu.CompilerParams(
        dimension_semantics=("arbitrary",) * n_grid, vmem_limit_bytes=mib * MIB
    )


def cost(mflop, mib):
    return pl.CostEstimate(flops=mflop * 10**6, bytes_accessed=mib * MIB, transcendentals=0)


def swap(v):
    return jnp.swapaxes(v, 0, 1)


def whole(shape):
    return pl.BlockSpec(shape, lambda i, ids: (0,) * len(shape))


def group_plane(shape, pick, a=0):
    block = (None,) * (len(shape) - 3) + (1,) + shape[-2:]
    return pl.BlockSpec(block, lambda i, ids: (0, a)[: len(shape) - 3] + (pick(i, ids), 0, 0))


def plane_onehot(pos, plane, ny, nz):
    local = pos - plane * (ny * nz)
    y = lax.broadcasted_iota(jnp.int32, (ny, pos.shape[1]), 0) * nz
    return jnp.where((local >= y) & (local < y + nz), 1.0, 0.0).astype(BF16)


def column_onehot(pos, nz):
    z = lax.broadcasted_iota(jnp.int32, (nz, pos.shape[1]), 0)
    return lax.rem(pos, nz) == z


def drive_at(delay, drive, step):
    amp = jnp.zeros(delay.shape, F32)
    for k in range(drive.shape[0]):
        amp = jnp.where(delay + step == k, drive[k], amp)
    return amp


def three(onehot, value):
    parts = [jnp.where(onehot, v.astype(F32), 0.0) for v in split3(value)]
    return jnp.concatenate(parts, axis=1).T.astype(BF16)


def spread(rows, cols):
    return dot(jnp.concatenate([rows] * 3, axis=1), cols)


def first_step(planes, cols, epos, numbers, ms):
    ny, nz = planes[0][0].shape
    c, rho, alpha, p, uy, uz = zip(*planes)
    at = range(len(planes))
    gy = [left(ms, G, v) for v in p]
    gz = [right(v, ms, T) for v in p]
    b = [1.0 / v for v in rho]
    bulk = [rho[k] * c[k] * c[k] for k in at]
    wy = [uy[k] - DT * b[k] * gy[k] for k in at]
    wz = [uz[k] - DT * b[k] * gz[k] for k in at]
    yz = [left(ms, T, v) for v in wy]
    zz = [right(v, ms, G) for v in wz]
    shot = [spread(plane_onehot(epos[...], n, ny, nz), cols[...]) for n in numbers]
    yz = [yz[k] + zz[k] for k in at]
    v0 = [(1.0 - DT * alpha[k]) * p[k] + (DT * bulk[k]) * yz[k] + shot[k] for k in at]
    return list(zip(gy, gz, wy, wz, yz, v0, b, bulk))


def start_kernel(
    drive, c, rho, alpha, p0, u, epos, delay, gm, tm, buf, ins, sems, outs, out_sems, cols, ms
):
    emit, slab = lax.axis_index("emit"), lax.axis_index("slab")
    nx, ny, nz = c.shape
    at = range(nx)
    srcs = (p0.at[0], rho, u.at[0, 1], u.at[0, 2], c, alpha, u.at[0, 0])
    copies = [pltpu.make_async_copy(src, ins.at[k], sems.at[k]) for k, src in enumerate(srcs)]
    for copy in copies:
        copy.start()

    def send(f, field):
        outs[f] = swap(field.reshape(2 * nx, ny // 2, nz))
        copy = pltpu.make_async_copy(outs.at[f], buf.at[:, f], out_sems.at[f])
        copy.start()
        return copy

    split_mats(gm, tm, ms)
    cols[...] = three(column_onehot(epos[...], nz), drive_at(delay[...], drive, 0))
    shot = [spread(plane_onehot(epos[...], slab * nx + i, ny, nz), cols[...]) for i in at]
    copies[0].wait()
    gy = [left(ms, G, ins[0, i]) for i in at]
    gz = [right(ins[0, i], ms, T) for i in at]
    sent = [send(0, ins[0])]
    for k in (1, 2, 3):
        copies[k].wait()
    b = [1.0 / ins[1, i] for i in at]
    yz = [left(ms, T, ins[2, i] - DT * b[i] * gy[i]) for i in at]
    zz = [right(ins[3, i] - DT * b[i] * gz[i], ms, G) for i in at]
    copies[4].wait()
    bulk = [ins[1, i] * ins[4, i] * ins[4, i] for i in at]
    for i in at:
        ins[1, i] = jnp.where(emit == 0, b[i], bulk[i])
    sent.append(send(3, ins[1]))
    copies[6].wait()
    sent.append(send(1, ins[6]))
    copies[5].wait()
    for i in at:
        ins[2, i] = (1.0 - DT * ins[5, i]) * ins[0, i] + (DT * bulk[i]) * (yz[i] + zz[i]) + shot[i]
    sent.append(send(2, ins[2]))
    for copy in sent:
        copy.wait()


def start_call(c, rho, alpha, p0, u, epos, delay, drive, mats, ndev):
    nx, ny, nz = c.shape
    n_e = epos.shape[1]
    hbm, vmem, smem = (pl.BlockSpec(memory_space=m) for m in (pltpu.HBM, pltpu.VMEM, pltpu.SMEM))
    return pl.pallas_call(
        start_kernel,
        in_specs=[smem] + [hbm] * 5 + [vmem] * 4,
        out_specs=hbm,
        out_shape=jax.ShapeDtypeStruct((ndev, 4, 2 * nx, nz), F32),
        scratch_shapes=[pltpu.VMEM((7, nx, ny, nz), F32), pltpu.SemaphoreType.DMA((7,)),
                        pltpu.VMEM((4, ndev, 2 * nx, nz), F32), pltpu.SemaphoreType.DMA((4,)),
                        pltpu.VMEM((3 * n_e, nz), BF16), mats_scratch(mats)],
        compiler_params=pltpu.CompilerParams(vmem_limit_bytes=LIMIT["start"] * MIB),
        cost_estimate=cost(2000, 13),
        name="start",
    )(drive, c, rho, alpha, p0, u, epos, delay, *mats)


def prepare_kernel(
    ids, drive, c, rho, alpha, p0, uy, uz, pa, ax, ay, az, spos, rec, epos, delay, gm, tm,
    dk, stay, b, pm, cdk, wb, yz1, yz0_out, late, gy0, gz0, axs, ones, scols, ecols, pack, ms,
):
    i = pl.program_id(0)
    ny, nz = c.shape[1], c.shape[2]

    @pl.when(i == 0)
    def _():
        split_mats(gm, tm, ms)
        oh = column_onehot(spos[...], nz)
        ones[...] = jnp.where(oh, 1.0, 0.0).T.astype(BF16)
        for step in range(STEPS):
            scols[step] = three(oh, rec[step : step + 1])
        for step in range(STEPS):
            ecols[step] = three(column_onehot(epos[...], nz), drive_at(delay[...], drive, step))

    plane = ids[1] * 4 + i
    gy, gz, u1y, u1z, yz0, v0, buoy, bulk = first_step(
        [(c[0], rho[0], alpha[0], p0[0], uy[0], uz[0])], ecols.at[0], epos, [plane], ms
    )[0]
    keep = 1.0 - DT * alpha[0]
    s = plane_onehot(spos[...], plane, ny, nz)
    count = dot(s, ones[...])
    m0 = spread(s, scols[0])
    m1 = spread(s, scols[1])
    shot = spread(plane_onehot(epos[...], plane, ny, nz), ecols[1])
    gyv = left(ms, G, v0)
    gzv = right(v0, ms, T)
    db = DT * buoy
    yz = left(ms, T, u1y - db * gyv) + right(u1z - db * gzv, ms, G)
    back = left(ms, T, buoy * ay[0]) + right(buoy * az[0], ms, G)
    dk[0] = DT * bulk
    stay[0] = keep
    b[0] = buoy
    cdk[0] = count * (DT * bulk)
    pm[0] = pa[0] + (count * (keep * v0 + (DT * bulk) * yz + shot) - m1)
    wb[0] = (count * v0 - m0) - DT * back
    yz1[0] = yz
    yz0_out[0] = yz0
    for k, field in enumerate((gy + gyv, gz + gzv, ay[0], az[0])):
        late[0, k] = field
    gy0[0] = gy
    gz0[0] = gz
    pack[pl.ds(2 * i, 2)] = ax[0].reshape(2, ny // 2, nz)

    @pl.when(i == pl.num_programs(0) - 1)
    def _():
        axs[...] = swap(pack[...])


def prepare_call(
    ids, c, rho, alpha, p0, u, pa, v, spos, rec, epos, delay, drive, mats
):
    nx, ny, nz = c.shape
    n_e, n_s = epos.shape[1], spos.shape[1]
    pick = lambda i, ids: i
    plane = group_plane(c.shape, pick)
    return pl.pallas_call(
        prepare_kernel,
        grid_spec=pltpu.PrefetchScalarGridSpec(
            num_scalar_prefetch=1,
            grid=(nx,),
            in_specs=[pl.BlockSpec(memory_space=pltpu.SMEM)] + [plane] * 3
            + [group_plane(p0.shape, pick)] + [group_plane(u.shape, pick, a) for a in (1, 2)]
            + [group_plane(pa.shape, pick)] + [group_plane(v.shape, pick, a) for a in range(3)]
            + [whole((1, n_s)), pl.BlockSpec((None, STEPS, n_s), lambda i, ids: (0, 0, 0)),
               whole((1, n_e)), whole((1, n_e))]
            + [whole((ny, ny))] * 2,
            out_specs=[plane] * 8 + [pl.BlockSpec((1, 4, ny, nz), lambda i, ids: (i, 0, 0, 0))]
            + [plane] * 2 + [whole((ny // 2, 2 * nx, nz))],
            scratch_shapes=[pltpu.VMEM((n_s, nz), BF16), pltpu.VMEM((STEPS, 3 * n_s, nz), BF16),
                            pltpu.VMEM((STEPS, 3 * n_e, nz), BF16),
                            pltpu.VMEM((2 * nx, ny // 2, nz), F32), mats_scratch(mats)],
        ),
        out_shape=[jax.ShapeDtypeStruct(c.shape, F32)] * 8
        + [jax.ShapeDtypeStruct((nx, 4, ny, nz), F32)] + [jax.ShapeDtypeStruct(c.shape, F32)] * 2
        + [jax.ShapeDtypeStruct((ny // 2, 2 * nx, nz), F32)],
        compiler_params=params(LIMIT["prepare"]),
        cost_estimate=cost(8000, 22),
        name="prepare",
    )(ids, drive, c, rho, alpha, p0, u, u, pa, v, v, v, spos, rec, epos, delay, *mats)


def on_chip(kernel, away, args, shapes, scratch, limit, estimate, name):
    vmem = pl.BlockSpec(memory_space=pltpu.VMEM)
    return pl.pallas_call(
        kernel,
        in_specs=[pl.BlockSpec(memory_space=pltpu.HBM)] * len(away) + [vmem] * len(args),
        out_specs=[vmem] * len(shapes),
        out_shape=[jax.ShapeDtypeStruct(v, F32) for v in shapes],
        scratch_shapes=[pltpu.VMEM(v, F32) if isinstance(v, tuple) else v for v in scratch]
        + [mats_scratch(args[-2:])],
        compiler_params=pltpu.CompilerParams(vmem_limit_bytes=limit * MIB),
        cost_estimate=estimate,
        name=name,
    )(*away, *args)


def unpack(block, dst, first):
    t = swap(block)
    n = t.shape[1]
    for xm in range(2):
        dst[:, (first + xm) * n : (first + xm + 1) * n, :] = t[4 * xm : 4 * xm + 4]


def forward_kernel(lines, gm, tm, out, gx0, gx1, bk, in_s, sems, f_s, o_s, ms):
    n = lines.shape[0]
    groups, at = range(2), range(4)
    order = (0, 3, 1, 2)
    copies = {f: pltpu.make_async_copy(lines.at[:, :, f], in_s.at[f], sems.at[f]) for f in order}
    for f in order:
        copies[f].start()

    def take(f, dst):
        copies[f].wait()
        for g in groups:
            t = swap(in_s[f, :, g])
            for xl in range(4):
                dst[2 * g : 2 * g + 2, xl * n : (xl + 1) * n, :] = t[2 * xl : 2 * xl + 2]

    split_mats(gm, tm, ms)
    take(0, f_s.at[0])
    g0 = [left(ms, G, f_s[0, j]) for j in at]
    take(3, bk)
    take(1, f_s.at[1])
    u1 = [f_s[1, j] - (DT * bk[j % 2]) * g0[j] for j in at]
    x0 = [left(ms, T, u1[j]) for j in at]
    take(2, f_s.at[2])
    p1 = [f_s[2, j] + (DT * bk[2 + j % 2]) * x0[j] for j in at]
    g1 = [left(ms, G, p1[j]) for j in at]
    x1 = [left(ms, T, u1[j] - (DT * bk[j % 2]) * g1[j]) for j in at]
    for j in at:
        gx0[j] = g0[j]
        gx1[j] = g1[j]
        o_s[j // 2, j % 2] = x0[j]
        o_s[j // 2, 2 + j % 2] = x1[j]
    for g in groups:
        for h in range(2):
            both = [o_s[g, :, (2 * h + xm) * n : (2 * h + xm + 1) * n, :] for xm in range(2)]
            out[:, g, h] = swap(jnp.concatenate(both, axis=0))


def forward_call(lines, mats):
    ns, _, _, _, nz = lines.shape
    nx = 4 * ns
    full = (4, nx, nz)
    return on_chip(
        forward_kernel, (lines,), mats, [(ns, 2, 2, 8, nz), full, full, full],
        [(4, ns, 2, 8, nz), pltpu.SemaphoreType.DMA((4,)), (3, 4, nx, nz), (2, 4, nx, nz)],
        LIMIT["forward"], cost(1600, 9), "lines_forward",
    )


def middle_kernel(
    axs, xs, dk, stay, b, pm, cdk, wb, yz1, yz0, gm, tm, buf, d0, t1, x_s, o_s, sem, ms
):
    nx, ny, nz = dk.shape
    fetch_ax = pltpu.make_async_copy(axs, buf.at[:, 2], sem)
    fetch_ax.start()
    split_mats(gm, tm, ms)
    for h in range(2):
        x_s[4 * h : 4 * h + 4] = swap(xs[:, h]).reshape(4, ny, nz)

    at = range(nx)
    add = [dk[i] * x_s[2 * i] for i in at]
    ey = [left(ms, G, a) for a in add]
    ez = [right(a, ms, T) for a in add]
    gy = [left(ms, T, (DT * b[i]) * ey[i]) for i in at]
    gz = [right((DT * b[i]) * ez[i], ms, G) for i in at]
    rest = [x_s[2 * i + 1] - (gy[i] + gz[i]) for i in at]
    adj = [pm[i] + cdk[i] * (stay[i] * x_s[2 * i] + rest[i]) for i in at]
    q = [dk[i] * adj[i] for i in at]
    fy = [left(ms, G, a) for a in q]
    fz = [right(a, ms, T) for a in q]
    for i in at:
        o_s[2 * i] = q[i]
        t1[i] = (yz1[i] + rest[i]) * adj[i]
        d0[i] = x_s[2 * i] + yz0[i]
    gy = [left(ms, T, b[i] * fy[i]) for i in at]
    gz = [right(b[i] * fz[i], ms, G) for i in at]
    for i in at:
        o_s[2 * i + 1] = stay[i] * adj[i] + (cdk[i] * x_s[2 * i] + wb[i]) - DT * (gy[i] + gz[i])

    for h in range(2):
        buf[:, h] = swap(o_s[4 * h : 4 * h + 4].reshape(8, ny // 2, nz))
    fetch_ax.wait()


def middle_call(xs, fields, mats):
    nat = fields[0].shape
    saved = (2 * nat[0],) + nat[1:]
    return on_chip(
        middle_kernel, (fields[11],), (xs, *fields[:8], *mats),
        [(xs.shape[0], 3) + xs.shape[2:], nat, nat, saved, saved],
        [pltpu.SemaphoreType.DMA], LIMIT["middle"], cost(3200, 18), "slab_middle",
    )


def adjoint_kernel(qw, bk, gx0, gx1, gm, tm, out, f_s, ux, p_s, bx_s, ms):
    split_mats(gm, tm, ms)
    n, nz = qw.shape[0], qw.shape[4]
    lanes = [slice(0, nz // 2), slice(nz // 2, nz)]

    for g in range(2):
        for h in range(2):
            unpack(qw[:, g, h], f_s.at[g], 2 * h)
        t = swap(qw[:, g, 2])
        for xl in range(4):
            ux[2 * g : 2 * g + 2, xl * n : (xl + 1) * n, :] = t[2 * xl : 2 * xl + 2]

    at = [(g, yl) for g in range(2) for yl in range(2)]
    ax = [left(ms, G, f_s[g, yl]) for g, yl in at]
    ax = [ux[j] + v for j, v in enumerate(ax)]
    back = [left(ms, T, bk[yl] * v) for (g, yl), v in zip(at, ax)]
    p0 = [f_s[g, 2 + yl] - DT * v for (g, yl), v in zip(at, back)]
    gq = [left(ms, G, (DT * bk[2 + yl]) * v) for (g, yl), v in zip(at, p0)]
    bx = [gx1[j] * ax[j] + gx0[j] * (ax[j] + gq[j]) for j in range(4)]
    for j in range(4):
        p_s[j] = p0[j]
    for yl in range(2):
        bx_s[yl] = bx[yl] + bx[2 + yl]

    for g in range(2):
        for zh, z in enumerate(lanes):
            v = [p_s[2 * g : 2 * g + 2, xl * n : (xl + 1) * n, z] for xl in range(4)]
            out[:, g, 8 * zh : 8 * zh + 8, :] = swap(jnp.concatenate(v, axis=0))

    for e in range(2):
        v = [bx_s[:, (2 * e + xm) * n : (2 * e + xm + 1) * n, z] for z in lanes for xm in range(2)]
        out[:, e, 16:24, :] = swap(jnp.concatenate(v, axis=0))


def adjoint_call(qw, bk, gx0, gx1, mats):
    ns, _, _, _, nz = qw.shape
    nx = 4 * ns
    return on_chip(
        adjoint_kernel, (), (qw, bk, gx0, gx1, *mats), [(ns, 2, 24, nz // 2)],
        [(2, 4, nx, nz), (4, nx, nz), (4, nx, nz), (2, nx, nz)], LIMIT["adjoint"], cost(1200, 9), "lines_adjoint",
    )[0]


def last_bulk_kernel(xs, d0, t1, out, p_s):
    nx, ny, nz = d0.shape
    half = nz // 2
    for zh in range(2):
        z = slice(zh * half, (zh + 1) * half)
        p = swap(xs[:, 8 * zh : 8 * zh + 8, :]).reshape(nx, ny, half)
        p_s[:, :, z] = p
        out[:, :, z] = t1[:, :, z] + d0[:, :, z] * p


def last_buoy_kernel(ids, xs, p_s, dk, gy0, gz0, x_s, o_s, late, gm, tm, out, bx_s, ms):
    split_mats(gm, tm, ms)
    nx, ny, nz = dk.shape
    half = nz // 2
    t = swap(xs[:, 16:24, :]).reshape(4, ny, half)
    for zh in range(2):
        bx_s[:, :, zh * half : (zh + 1) * half] = t[2 * zh : 2 * zh + 2]

    @pl.loop(0, nx)
    def _(i):
        add = dk[i] * x_s[2 * i]
        q1 = o_s[2 * i]
        q0 = dk[i] * p_s[i]
        ey, fy, gy = (left(ms, G, v) for v in (add, q1, q0))
        ez, fz, gz = (right(v, ms, T) for v in (add, q1, q0))
        late_y = (late[i, 0] + ey) * (late[i, 2] + fy) + gy0[i] * gy
        out[i] = late_y + (late[i, 1] + ez) * (late[i, 3] + fz) + gz0[i] * gz

    for xm in range(2):
        out[2 * ids[0] + xm] += bx_s[xm]


def last_buoy_call(ids, xs, fields, mats):
    nat = fields[0].shape
    vmem = pl.BlockSpec(memory_space=pltpu.VMEM)
    args = (xs, *fields, *mats)
    return pl.pallas_call(
        last_buoy_kernel,
        in_specs=[pl.BlockSpec(memory_space=pltpu.SMEM)] + [vmem] * len(args),
        out_specs=vmem,
        out_shape=jax.ShapeDtypeStruct(nat, F32),
        scratch_shapes=[pltpu.VMEM((2,) + nat[1:], F32), mats_scratch(mats)],
        compiler_params=pltpu.CompilerParams(vmem_limit_bytes=LIMIT["last"] * MIB),
        cost_estimate=cost(2400, 16),
        name="slab_last_buoy",
    )(ids, *args)


def speed_kernel(t1, other, c, rho, out, part, weight):
    @pl.loop(0, t1.shape[0])
    def _(i):
        s1 = DT * (t1[i] + other[i])
        b = 1.0 / rho[i]
        out[i] = 2.0 * s1 * rho[i] * c[i]
        part[i] = s1 * c[i] * c[i]
        weight[i] = DT * b * b


def density_kernel(t2, other, part, weight, out):
    @pl.loop(0, t2.shape[0])
    def _(i):
        out[i] = part[i] + (t2[i] + other[i]) * weight[i]


def finish(kernel, args, n_out, estimate, name):
    nat = args[-1].shape
    vmem = pl.BlockSpec(memory_space=pltpu.VMEM)
    return pl.pallas_call(
        kernel,
        in_specs=[vmem] * len(args),
        out_specs=[vmem] * n_out,
        out_shape=[jax.ShapeDtypeStruct(nat, F32)] * n_out,
        compiler_params=pltpu.CompilerParams(vmem_limit_bytes=LIMIT["last"] * MIB),
        cost_estimate=estimate,
        name=name,
    )(*args)


def change_layout(v):
    return lax.all_to_all(v, ALL, split_axis=0, concat_axis=0, tiled=True)


def swap_groups(v):
    return lax.ppermute(v, "emit", [(0, 1), (1, 0)])


def local(
    sound_speed, density, absorption, pressure_start, velocity_start, adjoint_pressure,
    adjoint_velocity, emitter_voxel, emitter_delay, drive_waveform_samples, recorded_pressures,
    sensor_flat_position,
):
    n_emit, n_slab = lax.axis_size("emit"), lax.axis_size("slab")
    ndev = n_emit * n_slab
    planes, ny, nz = sound_speed.shape
    nx = planes * n_slab
    emit = lax.axis_index("emit")
    ids = jnp.stack([emit, lax.axis_index("slab")]).astype(jnp.int32)
    mats = pair_const(deriv_matrix(ny))
    order = (4 * np.arange(n_slab)[None, :] + np.arange(4)[:, None]).reshape(-1)
    line_mats = pair_const(deriv_matrix(nx)[np.ix_(order, order)])

    buf = start_call(
        sound_speed, density, absorption, pressure_start, velocity_start, emitter_voxel,
        emitter_delay, drive_waveform_samples, mats, ndev,
    )
    fields = prepare_call(
        ids, sound_speed, density, absorption, pressure_start, velocity_start, adjoint_pressure,
        adjoint_velocity, sensor_flat_position.reshape(1, -1), recorded_pressures, emitter_voxel,
        emitter_delay, drive_waveform_samples, mats,
    )
    lines, fields = lax.optimization_barrier((change_layout(buf), fields))
    lines = lines.reshape(n_slab, n_emit, 4, 8, nz)
    xs, gx0, gx1, bk = forward_call(lines, line_mats)
    xs = change_layout(xs.reshape(ndev, 2, 8, nz))
    qw, d0, t1, x_s, o_s = middle_call(xs, fields, mats)
    qw = change_layout(qw).reshape(n_slab, n_emit, 3, 8, nz)
    xs = adjoint_call(qw, bk, gx0, gx1, line_mats)
    xs = change_layout(xs.reshape(ndev, 24, nz // 2))
    t1, p0 = finish(last_bulk_kernel, (xs, d0, t1), 2, cost(1, 5), "slab_last_bulk")
    t2 = last_buoy_call(
        ids, xs, [p0, fields[0], fields[9], fields[10], x_s, o_s, fields[8]], mats
    )
    speed_total, part, weight = finish(
        speed_kernel, (t1, swap_groups(t1), sound_speed, density), 3, cost(3, 100), "finish_speed"
    )
    (density_total,) = finish(
        density_kernel, (t2, swap_groups(t2), part, weight), 1, cost(3, 5), "finish_density"
    )
    return speed_total, density_total


def solution(mesh):
    in_specs = (
        P("slab", None, None), P("slab", None, None), P("slab", None, None),
        P("emit", "slab", None, None), P("emit", None, "slab", None, None),
        P("emit", "slab", None, None), P("emit", None, "slab", None, None),
        P("emit", None), P("emit", None), P(), P("emit", None, None), P(),
    )
    out_specs = (P("slab", None, None), P("slab", None, None))
    return jax.shard_map(local, mesh=mesh, in_specs=in_specs, out_specs=out_specs, check_vma=False)
```
